32 devices in a mesh: tile: 8 (over z, y), curve: 4 (over x, core).
Axes of the slice: x: 2, y: 2, z: 4, core: 2. Of those that a mesh axis runs over, the one named last changes fastest.
Arguments:
- points: bfloat16 [8, 512, 512], P('tile', 'curve'), may hold values from -6 to 6
- valid_rows: int32 [8, 4], P('tile', 'curve'), may hold values from 32 to 128, as said below
- dest_shard: int32 [8, 4, 1], P('tile', 'curve'), may hold values from 0 to 3, as said below
- dest_slot: int32 [8, 4, 1], P('tile', 'curve'), may hold values from 0 to 0, as said below
- norm_gain: float32 [2, 512], replicated, may hold values from 0.1 to 1.9
- w_xz: bfloat16 [2, 512, 2048], replicated, may hold values from -0.25 to 0.25
- w_bc: bfloat16 [2, 512, 256], replicated, may hold values from -0.25 to 0.25
- w_dt: bfloat16 [2, 512, 16], replicated, may hold values from -0.25 to 0.25
- dt_bias: float32 [2, 16], replicated, may hold values from -1 to 1
- decay_rate: float32 [2, 16], replicated, may hold values from 7.3242187e-06 to 0.1
- skip_gain: float32 [2, 16], replicated, may hold values from 0.5 to 1.5
- gate_gain: float32 [2, 1024], replicated, may hold values from 0.1 to 1.9
- w_out: bfloat16 [2, 1024, 512], replicated, may hold values from -0.1875 to 0.1875
Outputs:
- mixed: bfloat16 [8, 512, 512], P('tile', 'curve')
The draws below stay inside these ranges and needn't reach their ends.
Inputs may be any that keep to these rules, and one draw needn't show every extreme that they name: `valid_rows`: every tile has a curve shard with all 128 points live. `dest_shard`: within each tile, the 1 block of a curve shard go to 1 different curve shards, and every curve shard receives 1 block, one for each slot. `dest_slot`: together with dest_shard, every slot of every curve shard is filled exactly once.
All inputs are finite; a program needn't handle non-finite values.
Results may differ from the reference program's by a relative error of at most 0.0061.
Values may be sent and summed in bfloat16 or wider, within the bound.
No kernel may reach another device: no remote copies, remote signals or barrier semaphores. Data moves between devices by JAX's collectives and lax.ppermute only.
A program may use at most 320 MiB of HBM per device.

```python
import math
import jax
import jax.numpy as jnp
from jax import lax

D = 512
H = 16
S = 128
LAYERS = 2
ROWS_DEV = 128
BLOCK = 128
E = 1024
BLOCKS = 1
CURVES = 4
TILES = 8
TILE_ROWS = 512
N_CURVE = 4


def draw_valid_rows(key, part):
    count_key, full_key = jax.random.split(key, 2)
    counts = jax.random.randint(count_key, (TILES, CURVES), ROWS_DEV // 4, ROWS_DEV + 1)
    fullest = jax.random.randint(full_key, (TILES,), 0, CURVES)
    shard_index = lax.iota(jnp.int32, CURVES)
    return jnp.where(shard_index[None, :] == fullest[:, None], ROWS_DEV, counts).astype(jnp.int32)


def block_routing(key):
    base_key = jax.random.fold_in(key, 17)

    def one_tile(tile_key):
        tile_keys = jax.random.split(tile_key, 4)
        shuffle = jax.random.permutation(tile_keys[0], CURVES)
        shifts = jax.random.permutation(tile_keys[1], CURVES)[:BLOCKS]
        local_order = jax.vmap(lambda sub_key: jax.random.permutation(sub_key, BLOCKS))(jax.random.split(tile_keys[2], CURVES))
        slot_order = jax.vmap(lambda sub_key: jax.random.permutation(sub_key, BLOCKS))(jax.random.split(tile_keys[3], CURVES))
        source = lax.iota(jnp.int32, CURVES)[:, None]
        target = shuffle[(source + shifts[local_order]) % CURVES]
        slot_ids = slot_order[target, local_order]
        return (target.astype(jnp.int32), slot_ids.astype(jnp.int32))
    return jax.vmap(one_tile)(jax.random.split(base_key, TILES))


def draw_dest_shard(key, part):
    return block_routing(key)[0]


def draw_dest_slot(key, part):
    return block_routing(key)[1]


def draw_decay_rate(key, part):
    lengths = jnp.array([ROWS_DEV * CURVES, ROWS_DEV * CURVES * TILES], jnp.float32)
    pick_key, slow_key, fast_key, middle_key = jax.random.split(key, 4)
    ranking = jax.vmap(lambda sub_key: jax.random.permutation(sub_key, H))(jax.random.split(pick_key, LAYERS))
    layer_index = lax.iota(jnp.int32, LAYERS)[:, None]
    slow_count = jnp.where(layer_index == 0, H // 2, 0)
    middle_count = jnp.where(layer_index == 0, H // 4, H - H // 4)
    slow_heads = ranking < slow_count
    middle_heads = ranking < slow_count + middle_count
    slow_rate = jnp.exp(jax.random.uniform(slow_key, (LAYERS, H), jnp.float32, jnp.log(0.03), jnp.log(0.5))) / lengths[:, None]
    middle_low = jnp.where(layer_index == 0, math.log(0.5), math.log(0.13))
    middle_high = jnp.where(layer_index == 0, math.log(2.0), math.log(0.26))
    middle_spread = jax.random.uniform(middle_key, (LAYERS, H), jnp.float32)
    middle_rate = jnp.exp(middle_low + middle_spread * (middle_high - middle_low)) / ROWS_DEV
    fast_rate = jnp.exp(jax.random.uniform(fast_key, (LAYERS, H), jnp.float32, jnp.log(0.02), jnp.log(0.1)))
    return jnp.where(slow_heads, slow_rate, jnp.where(middle_heads, middle_rate, fast_rate)).astype(jnp.float32)


def block_scale(stream_key, extent, cuts, low, top_value):
    def one(position, blocks):
        steps = jax.random.uniform(jax.random.fold_in(jax.random.fold_in(stream_key, 6), position), (blocks,), jnp.float32, low / len(cuts), top_value / len(cuts))
        return jnp.repeat(jnp.exp(steps), extent[position] // blocks).reshape((-1,) + (1,) * (len(extent) - position - 1))

    factor_of = one(*cuts[0])
    for cut in cuts[1:]:
        factor_of = factor_of * one(*cut)
    return factor_of


def centred(stream_key, shape, deviation, bound, cuts=(), kind=jnp.bfloat16):
    values = jax.random.normal(stream_key, shape, jnp.float32) * deviation
    if len(cuts) > 0:
        values = block_scale(stream_key, shape, cuts, -0.22, 0.18) * values
    return jnp.clip(values, min=-bound, max=bound).astype(kind)


def setup_inputs(seed: int = 0) -> dict:
    splits = jax.random.split(jax.random.key(seed), 14)
    points = centred(splits[0], (TILES, TILE_ROWS, D), 1.0, 6.0, ((0, 8), (1, 4)))
    valid_rows = draw_valid_rows(jax.random.fold_in(splits[13], 71), 0)
    dest_shard = draw_dest_shard(jax.random.fold_in(splits[13], 71), 0)
    dest_slot = draw_dest_slot(jax.random.fold_in(splits[13], 71), 0)
    norm_gain = jnp.clip(1.0 + 0.18 * jax.random.normal(splits[4], (LAYERS, D), jnp.float32), 0.1, 1.9)
    w_xz = centred(splits[5], (LAYERS, D, 2 * E), D ** -0.5, 0.25)
    w_bc = centred(splits[6], (LAYERS, D, 2 * S), D ** -0.5, 0.25)
    w_dt = centred(splits[7], (LAYERS, D, H), D ** -0.5, 0.25)
    dt_bias = jnp.clip(jax.random.uniform(splits[8], (LAYERS, H), jnp.float32, -1.0, 1.0), -1.0, 1.0)
    decay_rate = draw_decay_rate(jax.random.fold_in(splits[13], 71), 0)
    skip_gain = jnp.clip(jax.random.uniform(splits[10], (LAYERS, H), jnp.float32, 0.5, 1.5), 0.5, 1.5)
    gate_gain = jnp.clip(1.0 + 0.18 * jax.random.normal(splits[11], (LAYERS, E), jnp.float32), 0.1, 1.9)
    w_out = centred(splits[12], (LAYERS, E, D), E ** -0.5, 0.1875)
    return dict(points=points, valid_rows=valid_rows, dest_shard=dest_shard, dest_slot=dest_slot, norm_gain=norm_gain, w_xz=w_xz, w_bc=w_bc, w_dt=w_dt, dt_bias=dt_bias, decay_rate=decay_rate, skip_gain=skip_gain, gate_gain=gate_gain, w_out=w_out)


highest = lax.Precision.HIGHEST

def prepare(inputs, live_rows, norm_g, proj_xz, proj_bc, proj_dt, shift_dt, rate_dt):
    widened = inputs.astype(jnp.float32)
    scaled = widened * lax.rsqrt(lax.optimization_barrier(jnp.mean(widened * widened, axis=-1, keepdims=True)) + 1e-05) * norm_g
    normed = scaled.astype(jnp.bfloat16)
    joined = jnp.dot(normed, proj_xz, preferred_element_type=jnp.float32)
    inner_width = joined.shape[1] // 2
    values = jax.nn.silu(joined[:, :inner_width]).astype(jnp.bfloat16)
    gate_pre = joined[:, inner_width:]
    mixed_bc = jnp.dot(normed, proj_bc, preferred_element_type=jnp.float32)
    state_width = mixed_bc.shape[1] // 2
    key_rows = jax.nn.silu(mixed_bc[:, :state_width]).astype(jnp.bfloat16)
    query_rows = jax.nn.silu(mixed_bc[:, state_width:]).astype(jnp.bfloat16)
    step_sizes = jax.nn.softplus(jnp.dot(normed, proj_dt, preferred_element_type=jnp.float32) + shift_dt) * live_rows[:, None]
    running = jnp.cumsum(-step_sizes * rate_dt, axis=0)
    log_total = running[-1]
    head_count = step_sizes.shape[1]
    head_values = values.astype(jnp.float32).reshape(values.shape[0], head_count, -1)
    to_end = jnp.exp(log_total[None, :] - running) * step_sizes
    end_state = jnp.einsum('shp,sn->hpn', head_values * to_end[:, :, None], key_rows.astype(jnp.float32), precision=highest)
    return ((log_total, end_state), (widened, gate_pre, key_rows, query_rows, step_sizes, running, head_values))

def finish(carried, pieces, skip_g, gate_g, proj_out, live_rows):
    widened, gate_pre, key_rows, query_rows, step_sizes, running, head_values = pieces
    row_count = widened.shape[0]
    block_rows = min(512, row_count)
    running_heads = running.T
    steps_heads = step_sizes.T
    outputs = []
    for first_row in range(0, row_count, block_rows):
        last_row = first_row + block_rows
        scores = jnp.dot(query_rows[first_row:last_row], key_rows[:last_row].T, preferred_element_type=jnp.float32)
        causal = (first_row + lax.iota(jnp.int32, block_rows))[:, None] >= lax.iota(jnp.int32, last_row)[None, :]
        gaps = running_heads[:, first_row:last_row, None] - running_heads[:, None, :last_row]
        weights = jnp.where(causal[None], jnp.exp(jnp.where(causal[None], gaps, 0.0)), 0.0)
        weights = weights * steps_heads[:, None, :last_row] * scores[None]
        inside = jnp.einsum('hts,shp->thp', weights, head_values[:last_row], precision=highest)
        from_state = jnp.einsum('hpn,tn->thp', carried, query_rows[first_row:last_row].astype(jnp.float32), precision=highest)
        carried_part = jnp.exp(running[first_row:last_row])[:, :, None] * from_state
        outputs.append(inside + carried_part + skip_g[None, :, None] * head_values[first_row:last_row])
    head_out = jnp.concatenate(outputs, axis=0).reshape(row_count, -1)
    gated = head_out * jax.nn.silu(gate_pre)
    normed = (gated * lax.rsqrt(lax.optimization_barrier(jnp.mean(gated * gated, axis=-1, keepdims=True)) + 1e-05) * gate_g).astype(jnp.bfloat16)
    update = jnp.dot(normed, proj_out, preferred_element_type=jnp.float32)
    return (widened + live_rows[:, None] * update).astype(jnp.bfloat16)

def run_chain(shards, live, layer, params):
    norm_gain, w_xz, w_bc, w_dt, dt_bias, decay_rate, skip_gain, gate_gain, w_out = params
    head_count = w_dt.shape[-1]
    head_size = w_xz.shape[-1] // 2 // head_count
    state_width = w_bc.shape[-1] // 2
    start_state = jnp.zeros((head_count, head_size, state_width), jnp.float32)

    def advance(carried, item_pair):
        summary, pieces = prepare(item_pair[0], item_pair[1], norm_gain[layer], w_xz[layer], w_bc[layer], w_dt[layer], dt_bias[layer], decay_rate[layer])
        layer_out = finish(carried, pieces, skip_gain[layer], gate_gain[layer], w_out[layer], item_pair[1])
        return (jnp.exp(summary[0])[:, None, None] * carried + summary[1], layer_out)
    final_state, outputs = lax.scan(advance, start_state, (shards, live))
    return outputs

def reference(points, valid_rows, dest_shard, dest_slot, norm_gain, w_xz, w_bc, w_dt, dt_bias, decay_rate, skip_gain, gate_gain, w_out):
    params = (norm_gain, w_xz, w_bc, w_dt, dt_bias, decay_rate, skip_gain, gate_gain, w_out)
    tile_count = points.shape[0]
    model_width = points.shape[2]
    row_index = jnp.arange(ROWS_DEV, dtype=jnp.int32)
    live_first = (row_index[None, None, :] < valid_rows[:, :, None]).astype(jnp.float32)
    shards = points.reshape(tile_count, N_CURVE, ROWS_DEV, model_width)

    def one_tile(tile_item):
        return run_chain(tile_item[0], tile_item[1], 0, params)
    first = lax.map(one_tile, (shards, live_first))
    blocks = first.reshape(tile_count, N_CURVE * BLOCKS, BLOCK * model_width)
    block_index = jnp.arange(BLOCKS, dtype=jnp.int32) * BLOCK
    block_live = jnp.clip(valid_rows[:, :, None] - block_index[None, None, :], 0, BLOCK).reshape(tile_count, -1)
    target = (dest_shard * BLOCKS + dest_slot).reshape(tile_count, -1).astype(jnp.int32)

    def place_rows(tile_blocks, tile_target):
        return jnp.zeros_like(tile_blocks).at[tile_target].set(tile_blocks)
    moved = jax.vmap(place_rows)(blocks, target)
    moved_live = jax.vmap(place_rows)(block_live, target)
    live_second = (jnp.arange(BLOCK, dtype=jnp.int32)[None, None, :] < moved_live[:, :, None]).astype(jnp.float32)
    live_second = live_second.reshape(tile_count * N_CURVE, ROWS_DEV)
    second = run_chain(moved.reshape(tile_count * N_CURVE, ROWS_DEV, model_width), live_second, 1, params)
    return second.reshape(tile_count, N_CURVE * ROWS_DEV, model_width)
```

```python
import functools

import jax
import jax.numpy as jnp
from jax import lax
from jax.experimental import pallas as pl
from jax.experimental.pallas import tpu as pltpu
from jax.sharding import PartitionSpec as P

F32, BF16 = jnp.float32, jnp.bfloat16
EPS = 1e-5
LOG2E = 1.4426950408889634
EXTRA = 16
VMEM_BYTES = 56 * 1024 * 1024


def dot(a, b):
    return jnp.dot(a, b, preferred_element_type=F32)


def dot_nt(a, b):
    return lax.dot_general(a, b, (((1,), (1,)), ((), ())), preferred_element_type=F32)


def silu(x):
    half = 0.5 * x
    return half + half * jnp.tanh(half)


def split(x):
    hi = x.astype(BF16).astype(F32)
    return hi, x - hi


def normalise(x, gain):
    wide = x.astype(F32)
    return (wide * lax.rsqrt(jnp.mean(wide * wide, axis=-1, keepdims=True) + EPS) * gain).astype(BF16)


def spread_matrix(heads, inner, groups):
    shape = (128, groups * inner)
    row = lax.broadcasted_iota(jnp.int32, shape, 0)
    col = lax.broadcasted_iota(jnp.int32, shape, 1)
    same_group = lax.div(row, 2 * heads) == lax.div(col, inner)
    same_head = lax.rem(row, heads) == lax.div(lax.rem(col, inner), inner // heads)
    return jnp.where(same_group & same_head, 1.0, 0.0).astype(BF16)


def spread_row(row, inner):
    heads = row.shape[1]
    shape = (heads, inner)
    head = lax.broadcasted_iota(jnp.int32, shape, 0)
    col = lax.broadcasted_iota(jnp.int32, shape, 1)
    ones = jnp.where(head == lax.div(col, inner // heads), 1.0, 0.0)
    wide = jnp.broadcast_to(row, (8, heads))
    out = jnp.dot(wide, ones, preferred_element_type=F32, precision=lax.Precision.HIGHEST)
    return out[:1]


def head_steps(normed, valids, w_dt_t, columns):
    heads = w_dt_t.shape[0]
    rows = normed.shape[0] // len(valids)
    raw = dot_nt(w_dt_t, normed) + columns[:, 0:1]
    steps = jnp.maximum(raw, 0.0) + jnp.log1p(jnp.exp(-jnp.abs(raw)))
    lane = lax.broadcasted_iota(jnp.int32, (heads, rows), 1)
    steps = jnp.concatenate(
        [
            jnp.where(lane < valid, steps[:, c * rows : (c + 1) * rows], 0.0)
            for c, valid in enumerate(valids)
        ],
        axis=0,
    )
    rate = jnp.concatenate([columns[:, 1:2]] * len(valids), axis=0)
    falls = -steps * rate
    upper = lax.broadcasted_iota(jnp.int32, (rows, rows), 0) <= lax.broadcasted_iota(
        jnp.int32, (rows, rows), 1
    )
    upper = jnp.where(upper, 1.0, 0.0).astype(BF16)
    high, rest = split(falls)
    middle, low = split(rest)
    running = (
        dot(high.astype(BF16), upper) + dot(middle.astype(BF16), upper) + dot(low.astype(BF16), upper)
    )
    to_end = jnp.exp2(running[:, rows - 1 : rows] - running) * steps
    return steps, to_end, running


def by_rows(steps, to_end, running):
    parts = [*split(steps), *split(to_end), *split(jnp.exp2(running)), running]
    used = len(parts) * running.shape[0]
    stack = jnp.concatenate(parts + [jnp.zeros((128 - used, running.shape[1]), F32)], axis=0)
    return stack.T


def mix_chunk(
    turned, running, key, query, value_of, state_of, decay_scale, spread_ref, skip, put, put_state
):
    rows, heads = turned.shape[0], running.shape[0]
    inner = spread_ref.shape[1] // 3
    width = inner // heads
    row = lax.broadcasted_iota(jnp.int32, (rows, rows), 0)
    col = lax.broadcasted_iota(jnp.int32, (rows, rows), 1)
    scores = jnp.where(row >= col, dot_nt(query, key), 0.0)
    lhs = turned.astype(BF16)
    run_at = 6 * heads
    key_t = key.astype(F32).T.astype(BF16)
    lane = lax.broadcasted_iota(jnp.int32, (rows, 128), 1)
    for g in range(inner // 256):
        cols = slice(g * 256, (g + 1) * 256)
        step_x = dot(lhs, spread_ref[:, cols])
        to_end_x = dot(lhs, spread_ref[:, inner + g * 256 : inner + (g + 1) * 256])
        decay_x = dot(lhs, spread_ref[:, 2 * inner + g * 256 : 2 * inner + (g + 1) * 256])
        value = value_of(cols).astype(F32)
        weighted = (value * step_x).astype(BF16)
        state = state_of(cols)
        from_state = dot(query, state.astype(BF16)) * decay_x
        base = from_state + skip[:, cols] * value
        if put_state is not None:
            grown = dot(key_t, (value * to_end_x).astype(BF16))
            put_state(cols, decay_x[rows - 1 : rows], state * decay_x[rows - 1 : rows] + grown)
        for pair in range(2):
            weights = []
            for k in range(2):
                h = (g * 256 + pair * 128) // width + k
                gap = turned[:, run_at + h : run_at + h + 1] - running[h : h + 1, :]
                weights.append((jnp.exp2(jnp.minimum(gap, 0.0)) * scores).astype(BF16))
            half = weighted[:, pair * 128 : (pair + 1) * 128]
            zero = jnp.zeros_like(half)
            both = jnp.concatenate(
                [jnp.where(lane < width, half, zero), jnp.where(lane < width, zero, half)], axis=0
            )
            inside = dot(jnp.concatenate(weights, axis=1), both)
            put(
                slice(g * 256 + pair * 128, g * 256 + (pair + 1) * 128),
                inside + base[:, pair * 128 : (pair + 1) * 128],
                decay_x[:, pair * 128 : (pair + 1) * 128],
            )


def tile_kernel(n, *refs):
    (info, *pieces) = refs[: n + 1]
    (
        norm_g,
        w_xz,
        w_bc,
        w_dt,
        cols_ref,
        skip_g,
        gate_g,
        w_out,
        send,
        own_x,
        own_state,
        own_decay,
        own_valid,
        x_all,
        values,
        gates,
        keys,
        queries,
        steps_s,
        to_end_s,
        running_s,
        spread_s,
        scaled,
        mixed,
        x_two,
        state,
        decay,
        flat,
        valid_one,
        valid_two,
        dest,
    ) = refs[n + 1 :]
    me = lax.axis_index("curve")
    rows, width = pieces[0].shape
    heads = w_dt.shape[1]
    inner = w_out.shape[1]
    key_width = w_bc.shape[2] // 2
    part = inner // n
    for k in range(n):
        place = me ^ k
        x_all[place] = pieces[k][...]
        valid_one[place] = info[k, 0]
        dest[place] = info[k, 1] + info[k, 2]
    for c in range(n):
        valid_two[dest[c]] = valid_one[c]
    spread_s[...] = spread_matrix(heads, inner, 3)

    def project(x, layer, with_gate):
        normed = normalise(x, norm_g[layer : layer + 1, :])
        for j in range(0, inner, 256):
            tile = silu(dot(normed, w_xz[layer, :, j : j + 256])).astype(BF16)
            for c in range(n):
                values[c, :, j : j + 256] = tile[c * rows : (c + 1) * rows]
        if with_gate:
            for j in range(0, inner, 256):
                tile = silu(dot(normed, w_xz[layer, :, inner + j : inner + j + 256]))
                for c in range(n):
                    gates[c, :, j : j + 256] = tile[c * rows : (c + 1) * rows]
        bc = silu(dot(normed, w_bc[layer])).astype(BF16)
        for c in range(n):
            keys[c] = bc[c * rows : (c + 1) * rows, :key_width]
            queries[c] = bc[c * rows : (c + 1) * rows, key_width:]
        valid = valid_two if layer else valid_one
        steps, to_end, running = head_steps(
            normed, [valid[c] for c in range(n)], w_dt[layer], cols_ref[layer]
        )
        for c in range(n):
            steps_s[c] = steps[c * heads : (c + 1) * heads]
            to_end_s[c] = to_end[c * heads : (c + 1) * heads]
            running_s[c] = running[c * heads : (c + 1) * heads]

    project(x_all[...].reshape(n * rows, width), 0, True)
    skip = spread_row(skip_g[0:1, :], inner)
    state[...] = jnp.zeros_like(state)

    def first_chunk(c, _):
        running = running_s[c]
        turned = by_rows(steps_s[c], to_end_s[c], running)
        squares = []

        def put(at, head_out, decay_x):
            gated = head_out * gates[c, :, at]
            mixed[:, at] = gated
            squares.append(jnp.sum(gated * gated, axis=-1, keepdims=True))

        def put_state(at, factor, new):
            state[:, at] = new

        mix_chunk(
            turned,
            running,
            keys[c],
            queries[c],
            lambda at: values[c, :, at],
            lambda at: state[:, at],
            None,
            spread_s,
            skip,
            put,
            put_state,
        )
        scale = lax.rsqrt(sum(squares) * (1.0 / inner) + EPS)
        scaled[c] = (mixed[...] * scale * gate_g[0:1, :]).astype(BF16)
        return 0

    lax.fori_loop(0, n, first_chunk, 0)
    flat[...] = dot(scaled[...].reshape(n * rows, inner), w_out[0])
    row = lax.broadcasted_iota(jnp.int32, (rows, 1), 0)
    for c in range(n):
        live = row < valid_one[c]
        update = jnp.where(live, flat[c * rows : (c + 1) * rows, :], 0.0)
        x_two[dest[c]] = (x_all[c].astype(F32) + update).astype(BF16)

    project(x_two[...].reshape(n * rows, width), 1, False)
    state[...] = jnp.zeros_like(state)
    decay[...] = jnp.ones_like(decay)

    def second_chunk(c, _):
        @pl.when(c == me)
        def _():
            own_state[...] = state[...]
            own_decay[...] = decay[...]

        lhs = by_rows(steps_s[c], to_end_s[c], running_s[c]).astype(BF16)
        key_t = keys[c].astype(F32).T.astype(BF16)
        for j in range(0, inner, 256):
            to_end_x = dot(lhs, spread_s[:, inner + j : inner + j + 256])
            end_x = dot(lhs[rows - 16 :], spread_s[:, 2 * inner + j : 2 * inner + j + 256])[15:16]
            value = values[c, :, j : j + 256].astype(F32)
            grown = dot(key_t, (value * to_end_x).astype(BF16))
            state[:, j : j + 256] = state[:, j : j + 256] * end_x + grown
            decay[:, j : j + 256] = decay[:, j : j + 256] * end_x
        return 0

    lax.fori_loop(0, n, second_chunk, 0)
    own_x[...] = x_two[me]
    own_valid[0] = valid_two[me]
    at = pl.ds(pl.multiple_of(me * part, 128), part)
    states = state.shape[0]
    send[:states] = state[:, at].astype(BF16)
    high, low = split(decay[:, at])
    lines = lax.broadcasted_iota(jnp.int32, (EXTRA, part), 0)
    send[states:] = jnp.where(lines == 0, high[:1], jnp.where(lines == 1, low[:1], 0.0)).astype(BF16)


def own_kernel(
    x,
    valid,
    state,
    decay,
    norm_g,
    w_xz,
    w_bc,
    w_dt,
    cols_ref,
    skip_g,
    local,
    gate,
    query_out,
    decay_out,
    values,
    spread_s,
):
    heads = w_dt.shape[1]
    inner = local.shape[1]
    key_width = w_bc.shape[2] // 2
    normed = normalise(x[...], norm_g[1:2, :])
    spread_s[...] = spread_matrix(heads, inner, 3)
    for j in range(0, inner, 256):
        values[:, j : j + 256] = silu(dot(normed, w_xz[1, :, j : j + 256])).astype(BF16)
        gate[:, j : j + 256] = silu(dot(normed, w_xz[1, :, inner + j : inner + j + 256]))
    bc = silu(dot(normed, w_bc[1])).astype(BF16)
    query = bc[:, key_width:]
    query_out[...] = query
    steps, to_end, running = head_steps(normed, [valid[0]], w_dt[1], cols_ref[1])
    turned = by_rows(steps, to_end, running)

    def put(at, head_out, decay_x):
        local[:, at] = head_out
        decay_out[:, at] = decay_x * decay[:1, at]

    mix_chunk(
        turned,
        running,
        bc[:, :key_width],
        query,
        lambda at: values[:, at],
        lambda at: state[:, at],
        None,
        spread_s,
        spread_row(skip_g[1:2, :], inner),
        put,
        None,
    )


def join_kernel(radix, stride, last, *refs):
    parts, before = refs[:radix], refs[radix]
    outs = refs[radix + 1 :]
    me = lax.rem(lax.div(lax.axis_index("tile"), stride), radix)
    states = parts[0].shape[0] - EXTRA
    shape = (states, parts[0].shape[1])
    state, decay = jnp.zeros(shape, F32), jnp.ones((1, shape[1]), F32)
    ordered = outs[-1]
    for k in range(radix):
        ordered[me ^ k] = parts[k][...]

    def member(u):
        tail = ordered[u, states:].astype(F32)
        return ordered[u, :states].astype(F32), tail[0:1] + tail[1:2]

    earlier = None
    for u in range(radix):
        one, fall = member(u)
        if earlier is None:
            earlier = (jnp.where(me > u, one, state), jnp.where(me > u, fall, decay))
        elif u < radix - 1:
            earlier = (
                jnp.where(me > u, earlier[0] * fall + one, earlier[0]),
                jnp.where(me > u, earlier[1] * fall, earlier[1]),
            )
        if not last:
            if u == 0:
                whole = (one, fall)
            else:
                whole = (whole[0] * fall + one, whole[1] * fall)
    old = before[...]
    if last:
        outs[0][...] = (earlier[0] * old[states : states + 1] + old[:states]).astype(BF16)
        return
    outs[0][:states] = earlier[0] * old[states : states + 1] + old[:states]
    outs[0][states:] = jnp.broadcast_to(earlier[1] * old[states : states + 1], (8, shape[1]))
    outs[1][:states] = whole[0].astype(BF16)
    high, low = split(whole[1])
    lines = lax.broadcasted_iota(jnp.int32, (EXTRA, shape[1]), 0)
    outs[1][states:] = jnp.where(lines == 0, high, jnp.where(lines == 1, low, 0.0)).astype(BF16)


def end_kernel(n, *refs):
    states = refs[:n]
    x, valid, local, gate, query, decay, gate_g, w_out, out, mixed = refs[n:]
    me = lax.axis_index("curve")
    rows, inner = local.shape
    part = inner // n
    squares = jnp.zeros((rows, 1), F32)
    for k in range(n):
        at = pl.ds(pl.multiple_of((me ^ k) * part, 128), part)
        head_out = dot(query[...], states[k][...]) * decay[:, at] + local[:, at]
        gated = head_out * gate[:, at]
        squares += jnp.sum(gated * gated, axis=-1, keepdims=True)
        mixed[:, at] = gated
    scale = lax.rsqrt(squares * (1.0 / inner) + EPS)
    scaled = (mixed[...] * scale * gate_g[1:2, :]).astype(BF16)
    update = dot(scaled, w_out[1])
    live = lax.broadcasted_iota(jnp.int32, (rows, 1), 0) < valid[0]
    out[...] = (x[...].astype(F32) + jnp.where(live, update, 0.0)).astype(BF16)


def call(kernel, outs, scratch, smem_in, smem_out, *args):
    vmem, smem = pl.BlockSpec(memory_space=pltpu.VMEM), pl.BlockSpec(memory_space=pltpu.SMEM)
    return pl.pallas_call(
        kernel,
        out_shape=[jax.ShapeDtypeStruct(shape, kind) for shape, kind in outs],
        in_specs=[smem if i in smem_in else vmem for i in range(len(args))],
        out_specs=[smem if i in smem_out else vmem for i in range(len(outs))],
        scratch_shapes=scratch,
        compiler_params=pltpu.CompilerParams(vmem_limit_bytes=VMEM_BYTES),
    )(*args)


def swap(value, axis, mask, size):
    return lax.ppermute(value, axis, [(i, i ^ mask) for i in range(size)])


def levels(size):
    steps, stride = [], 1
    while stride < size:
        radix = 2 if (stride == 1 and size % 4) or size // stride < 4 or stride == 1 else 4
        steps.append((radix, stride))
        stride *= radix
    return steps


def local(
    tiles,
    points,
    valid_rows,
    dest_shard,
    dest_slot,
    norm_gain,
    w_xz,
    w_bc,
    w_dt,
    dt_bias,
    decay_rate,
    skip_gain,
    gate_gain,
    w_out,
):
    n = lax.axis_size("curve")
    x = points[0]
    rows, width = x.shape
    heads, inner, key_width = w_dt.shape[2], w_out.shape[1], w_bc.shape[2] // 2
    part = inner // n
    pieces = [x] + [swap(x, "curve", k, n) for k in range(1, n)]
    info = jnp.concatenate([valid_rows[0], dest_shard[0, 0], dest_slot[0, 0]])
    infos = jnp.stack([info] + [swap(info, "curve", k, n) for k in range(1, n)])
    w_dt_t = jnp.swapaxes(w_dt, 1, 2)
    columns = jnp.stack([dt_bias, decay_rate * LOG2E], axis=-1)
    send, own_x, own_state, own_decay, own_valid = call(
        functools.partial(tile_kernel, n),
        [
            ((key_width + EXTRA, part), BF16),
            ((rows, width), BF16),
            ((key_width, inner), F32),
            ((8, inner), F32),
            ((1,), jnp.int32),
        ],
        [
            pltpu.VMEM((n, rows, width), BF16),
            pltpu.VMEM((n, rows, inner), BF16),
            pltpu.VMEM((n, rows, inner), F32),
            pltpu.VMEM((n, rows, key_width), BF16),
            pltpu.VMEM((n, rows, key_width), BF16),
            pltpu.VMEM((n, heads, rows), F32),
            pltpu.VMEM((n, heads, rows), F32),
            pltpu.VMEM((n, heads, rows), F32),
            pltpu.VMEM((128, 3 * inner), BF16),
            pltpu.VMEM((n, rows, inner), BF16),
            pltpu.VMEM((rows, inner), F32),
            pltpu.VMEM((n, rows, width), BF16),
            pltpu.VMEM((key_width, inner), F32),
            pltpu.VMEM((8, inner), F32),
            pltpu.VMEM((n * rows, width), F32),
            pltpu.SMEM((n,), jnp.int32),
            pltpu.SMEM((n,), jnp.int32),
            pltpu.SMEM((n,), jnp.int32),
        ],
        (0,),
        (4,),
        infos,
        *pieces,
        norm_gain,
        w_xz,
        w_bc,
        w_dt_t,
        columns,
        skip_gain,
        gate_gain,
        w_out,
    )
    own, gate, query, decay = call(
        own_kernel,
        [
            ((rows, inner), F32),
            ((rows, inner), F32),
            ((rows, key_width), BF16),
            ((rows, inner), F32),
        ],
        [pltpu.VMEM((rows, inner), BF16), pltpu.VMEM((128, 3 * inner), BF16)],
        (1,),
        (),
        own_x,
        own_valid,
        own_state,
        own_decay,
        norm_gain,
        w_xz,
        w_bc,
        w_dt_t,
        columns,
        skip_gain,
    )
    before = jnp.concatenate([jnp.zeros((key_width, part), F32), jnp.ones((8, part), F32)])
    steps = levels(tiles)
    for i, (radix, stride) in enumerate(steps):
        last = i == len(steps) - 1
        parts = [send] + [swap(send, "tile", k * stride, tiles) for k in range(1, radix)]
        outs = [((key_width, part), BF16)]
        if not last:
            outs = [((key_width + 8, part), F32), ((key_width + EXTRA, part), BF16)]
        got = call(
            functools.partial(join_kernel, radix, stride, last),
            outs,
            [pltpu.VMEM((radix, key_width + EXTRA, part), BF16)],
            (),
            (),
            *parts,
            before,
        )
        if last:
            incoming = got[0]
        else:
            before, send = got
    states = [incoming] + [swap(incoming, "curve", k, n) for k in range(1, n)]
    (out,) = call(
        functools.partial(end_kernel, n),
        [((rows, width), BF16)],
        [pltpu.VMEM((rows, inner), F32)],
        (n + 1,),
        (),
        *states,
        own_x,
        own_valid,
        own,
        gate,
        query,
        decay,
        gate_gain,
        w_out,
    )
    return out[None]


def solution(mesh):
    in_specs = (
        P("tile", "curve", None),
        P("tile", "curve"),
        P("tile", "curve", None),
        P("tile", "curve", None),
    ) + (P(),) * 9
    return jax.shard_map(
        functools.partial(local, mesh.shape["tile"]),
        mesh=mesh,
        in_specs=in_specs,
        out_specs=P("tile", "curve", None),
        check_vma=False,
    )
```

```python
import functools

import jax
import jax.numpy as jnp
from jax import lax
from jax.experimental import pallas as pl
from jax.experimental.pallas import tpu as pltpu
from jax.sharding import PartitionSpec as P

F32, BF16 = jnp.float32, jnp.bfloat16
EPS = 1e-5
LOG2E = 1.4426950408889634
EXTRA = 16
VMEM_BYTES = 40 * 1024 * 1024


def dot(a, b):
    return jnp.dot(a, b, preferred_element_type=F32)


def dot_nt(a, b):
    return lax.dot_general(a, b, (((1,), (1,)), ((), ())), preferred_element_type=F32)


def turn(x):
    return x.astype(F32).T.astype(x.dtype)


def silu(x):
    half = 0.5 * x
    return half + half * jnp.tanh(half)


def split(x):
    hi = x.astype(BF16).astype(F32)
    return hi, x - hi


def normalise(x, gain):
    wide = x.astype(F32)
    return (wide * lax.rsqrt(jnp.mean(wide * wide, axis=-1, keepdims=True) + EPS) * gain).astype(BF16)


def iota(shape, axis):
    return lax.broadcasted_iota(jnp.int32, shape, axis)


def column(row):
    heads = row.shape[1]
    same = iota((heads, heads), 0) == iota((heads, heads), 1)
    return jnp.sum(jnp.where(same, row, 0.0), axis=1, keepdims=True)


def head_steps(normed, valids, w_dt_t, bias, rate):
    heads = w_dt_t.shape[0]
    rows = normed.shape[0] // len(valids)
    raw = dot_nt(w_dt_t, normed) + column(bias)
    steps = jnp.maximum(raw, 0.0) + jnp.log1p(jnp.exp(-jnp.abs(raw)))
    lane = iota((heads, rows), 1)
    steps = jnp.concatenate(
        [
            jnp.where(lane < valid, steps[:, c * rows : (c + 1) * rows], 0.0)
            for c, valid in enumerate(valids)
        ],
        axis=0,
    )
    falls = -steps * jnp.concatenate([column(rate) * LOG2E] * len(valids), axis=0)
    upper = jnp.where(iota((rows, rows), 0) <= iota((rows, rows), 1), 1.0, 0.0).astype(BF16)
    high, rest = split(falls)
    middle, low = split(rest)
    running = (
        dot(high.astype(BF16), upper) + dot(middle.astype(BF16), upper) + dot(low.astype(BF16), upper)
    )
    to_end = jnp.exp2(running[:, rows - 1 : rows] - running) * steps
    return steps, to_end, running


def by_rows(to_end, running):
    parts = [*split(to_end), *split(jnp.exp2(running)), running]
    used = len(parts) * running.shape[0]
    stack = jnp.concatenate(parts + [jnp.zeros((128 - used, running.shape[1]), F32)], axis=0)
    return stack.T


def seen_from(steps, running):
    return running - jnp.where(steps > 0.0, jnp.log2(jnp.maximum(steps, 1e-37)), -1e30)


def inside_pair(turned, seen, scores, value, head, heads):
    rows = turned.shape[0]
    at = 4 * heads + head
    weights = [
        (jnp.exp2(jnp.minimum(turned[:, at + k : at + k + 1] - seen[head + k : head + k + 1], 120.0)) * scores).astype(BF16)
        for k in range(2)
    ]
    left = iota((rows, 128), 1) < 64
    zero = jnp.zeros_like(value)
    both = jnp.concatenate([jnp.where(left, value, zero), jnp.where(left, zero, value)], axis=0)
    return dot(jnp.concatenate(weights, axis=1), both)


def masked_scores(query, key):
    rows = query.shape[0]
    return jnp.where(iota((rows, rows), 0) >= iota((rows, rows), 1), dot_nt(query, key), 0.0)


def pack_kernel(x, valid, shard, slot, out):
    rows, width = x.shape[1:]
    out[:rows] = x[0]
    line, lane = iota((EXTRA, width), 0), iota((EXTRA, width), 1)
    count = valid[0, 0].astype(F32)
    place = (shard[0, 0] + slot[0, 0]).astype(F32)
    out[rows:] = jnp.where(line > 0, 0.0, jnp.where(lane == 0, count, jnp.where(lane == 1, place, 0.0))).astype(BF16)


def load_kernel(count, skip_g, *refs):
    sources, (spread, skip), held, sems = refs[:count], refs[count : count + 2], refs[count + 2 : -1], refs[-1]
    copies = [pltpu.make_async_copy(a, b, sems.at[i]) for i, (a, b) in enumerate(zip(sources, held))]
    for copy in copies:
        copy.start()
    layers, heads = skip_g.shape
    inner = skip.shape[1]
    shift = (inner // heads).bit_length() - 1
    shape = (128, inner)
    head = lax.shift_right_logical(iota(shape, 1), shift)
    row = iota(shape, 0)
    for g in range(2):
        hit = (row == head + 2 * heads * g) | (row == head + 2 * heads * g + heads)
        spread[:, g * inner : (g + 1) * inner] = jnp.where(hit, 1.0, 0.0).astype(BF16)
    ones = jnp.where(head[:heads] == row[:heads], 1.0, 0.0)
    for layer in range(layers):
        wide = jnp.broadcast_to(skip_g[layer : layer + 1, :], (8, heads))
        out = jnp.dot(wide, ones, preferred_element_type=F32, precision=lax.Precision.HIGHEST)
        skip[8 * layer : 8 * layer + 8, :] = out
    for copy in copies:
        copy.wait()


def tile_kernel(n, *refs):
    pieces = refs[:n]
    (
        spread,
        skip,
        norm_g,
        w_xz,
        w_bc,
        w_dt,
        bias,
        rate,
        gate_g,
        w_out,
        send,
        own_x,
        own_live,
        normed_two,
        key_two,
        own_query,
        turned_two,
        seen_two,
        x_all,
        values,
        gates,
        keys,
        queries,
        to_end_s,
        running_s,
        seen_s,
        scaled,
        mixed,
        x_two,
        state,
        flat,
        valid_one,
        valid_two,
        dest,
    ) = refs[n:]
    me = lax.axis_index("curve")
    rows, width = x_all.shape[1:]
    heads = w_dt.shape[1]
    inner = w_out.shape[1]
    key_width = w_bc.shape[2] // 2
    part = inner // n
    line, lane = iota((EXTRA, 128), 0), iota((EXTRA, 128), 1)
    for k in range(n):
        place = me ^ k
        x_all[place] = pieces[k][:rows]
        numbers = pieces[k][rows:, :128].astype(F32)
        valid_one[place] = jnp.sum(jnp.where((line == 0) & (lane == 0), numbers, 0.0)).astype(jnp.int32)
        dest[place] = jnp.sum(jnp.where((line == 0) & (lane == 1), numbers, 0.0)).astype(jnp.int32)
    for c in range(n):
        valid_two[dest[c]] = valid_one[c]

    normed = normalise(x_all[...].reshape(n * rows, width), norm_g[0:1, :])
    bc = silu(dot(normed, w_bc[0])).astype(BF16)
    steps, to_end, running = head_steps(
        normed, [valid_one[c] for c in range(n)], w_dt[0], bias[0:1, :], rate[0:1, :]
    )
    seen = seen_from(steps, running)
    for c in range(n):
        at = slice(c * rows, (c + 1) * rows)
        keys[c] = bc[at, :key_width]
        queries[c] = bc[at, key_width:]
        at = slice(c * heads, (c + 1) * heads)
        to_end_s[c] = to_end[at]
        running_s[c] = running[at]
        seen_s[c] = seen[at]
    for j in range(0, inner, 256):
        tile = silu(dot(normed, w_xz[0, :, j : j + 256])).astype(BF16)
        for c in range(n):
            values[c, :, j : j + 256] = tile[c * rows : (c + 1) * rows]
    for j in range(0, inner, 256):
        tile = silu(dot(normed, w_xz[0, :, inner + j : inner + j + 256]))
        for c in range(n):
            gates[c, :, j : j + 256] = tile[c * rows : (c + 1) * rows]

    state[...] = jnp.zeros_like(state)

    def first_chunk(c, _):
        turned = by_rows(to_end_s[c], running_s[c])
        lhs = turned.astype(BF16)
        seen = seen_s[c]
        query = queries[c]
        scores = masked_scores(query, keys[c])
        key_t = turn(keys[c])
        squares = jnp.zeros((rows, 1), F32)
        for j in range(0, inner, 256):
            at = slice(j, j + 256)
            decay_x = dot(lhs, spread[:, inner + j : inner + j + 256])
            to_end_x = dot(lhs, spread[:, at])
            value = values[c, :, at]
            wide = value.astype(F32)
            old = state[:, at]
            base = dot(query, old.astype(BF16)) * decay_x + skip[0:1, at] * wide
            state[:, at] = old * decay_x[rows - 1 :] + dot(key_t, (wide * to_end_x).astype(BF16))
            for k in range(2):
                half = slice(128 * k, 128 * k + 128)
                head = (j + 128 * k) * heads // inner
                out = inside_pair(turned, seen, scores, value[:, half], head, heads) + base[:, half]
                gated = out * gates[c, :, j + 128 * k : j + 128 * k + 128]
                mixed[:, j + 128 * k : j + 128 * k + 128] = gated
                squares += jnp.sum(gated * gated, axis=-1, keepdims=True)
        scale = lax.rsqrt(squares * (1.0 / inner) + EPS)
        scaled[c] = (mixed[...] * scale * gate_g[0:1, :]).astype(BF16)
        return 0

    lax.fori_loop(0, n, first_chunk, 0)
    flat[...] = dot(scaled[...].reshape(n * rows, inner), w_out[0])
    row = iota((rows, 1), 0)
    for c in range(n):
        update = jnp.where(row < valid_one[c], flat[c * rows : (c + 1) * rows, :], 0.0)
        x_two[dest[c]] = (x_all[c].astype(F32) + update).astype(BF16)

    own_x[...] = x_two[me]
    own_live[...] = jnp.where(iota((rows, 128), 0) < valid_two[me], 1.0, 0.0)
    normed = normalise(x_two[...].reshape(n * rows, width), norm_g[1:2, :])
    bc = silu(dot(normed, w_bc[1])).astype(BF16)
    steps, to_end, running = head_steps(
        normed, [valid_two[c] for c in range(n)], w_dt[1], bias[1:2, :], rate[1:2, :]
    )
    seen = seen_from(steps, running)
    at = pl.ds(pl.multiple_of(me * part, 128), part)
    value = silu(dot(normed, w_xz[1, :, at]))
    total = jnp.zeros((key_width, part), F32)
    fall = jnp.ones((1, part), F32)
    for c in range(n):
        queries[c] = bc[c * rows : (c + 1) * rows, key_width:]
        key = bc[c * rows : (c + 1) * rows, :key_width]
        key_two[c] = key
        normed_two[c] = normed[c * rows : (c + 1) * rows]
        heads_at = slice(c * heads, (c + 1) * heads)
        seen_two[c] = seen[heads_at]
        turned = by_rows(to_end[heads_at], running[heads_at])
        turned_two[c] = turned
        lhs = turned.astype(BF16)
        to_end_x = dot(lhs, spread[:, at])
        end_x = dot(lhs[rows - 16 :], spread[:, pl.ds(pl.multiple_of(inner + me * part, 128), part)])[15:16]
        weighted = value[c * rows : (c + 1) * rows].astype(BF16).astype(F32) * to_end_x
        total = total * end_x + dot(turn(key), weighted.astype(BF16))
        fall = fall * end_x
    own_query[...] = queries[me]
    send[:key_width] = total.astype(BF16)
    high, low = split(fall)
    lines = iota((EXTRA, part), 0)
    send[key_width:] = jnp.where(lines == 0, high, jnp.where(lines == 1, low, 0.0)).astype(BF16)


def own_kernel(normed_two, key_two, query, turned_two, seen_two, spread, skip, w_xz, local, gate, decay):
    me = lax.axis_index("curve")
    inner = local.shape[1]
    heads = seen_two.shape[1]
    normed = normed_two[me]
    turned = turned_two[me]
    seen = seen_two[me]
    lhs = turned.astype(BF16)
    scores = masked_scores(query[...], key_two[me])
    for j in range(0, inner, 256):
        at = slice(j, j + 256)
        value = silu(dot(normed, w_xz[1, :, at])).astype(BF16)
        gate[:, at] = silu(dot(normed, w_xz[1, :, inner + j : inner + j + 256]))
        decay[:, at] = dot(lhs, spread[:, inner + j : inner + j + 256])
        base = skip[8:9, at] * value.astype(F32)
        for k in range(2):
            half = slice(128 * k, 128 * k + 128)
            head = (j + 128 * k) * heads // inner
            local[:, j + 128 * k : j + 128 * k + 128] = (
                inside_pair(turned, seen, scores, value[:, half], head, heads) + base[:, half]
            )


def earlier_kernel(normed_two, key_two, turned_two, spread, w_xz, state, fall):
    me = lax.axis_index("curve")
    inner = state.shape[1]
    rows = normed_two.shape[1]
    state[...] = jnp.zeros_like(state)
    fall[...] = jnp.ones_like(fall)

    def chunk(c, _):
        normed = normed_two[c]
        lhs = turned_two[c].astype(BF16)
        key_t = turn(key_two[c])
        for j in range(0, inner, 256):
            at = slice(j, j + 256)
            value = silu(dot(normed, w_xz[1, :, at])).astype(BF16).astype(F32)
            weighted = value * dot(lhs, spread[:, at])
            end_x = dot(lhs[rows - 16 :], spread[:, inner + j : inner + j + 256])[15:16]
            state[:, at] = state[:, at] * end_x + dot(key_t, weighted.astype(BF16))
            fall[:, at] = fall[:, at] * end_x
        return 0

    lax.fori_loop(0, me, chunk, 0)


def join_kernel(radix, stride, last, *refs):
    parts, before = refs[:radix], refs[radix] if stride > 1 else None
    outs, ordered = refs[radix + 1 + (stride > 1) : -1], refs[-1]
    me = lax.rem(lax.div(lax.axis_index("tile"), stride), radix)
    states = parts[0].shape[0] - EXTRA
    width = parts[0].shape[1]
    for k in range(radix):
        ordered[me ^ k] = parts[k][...]
    earlier = (jnp.zeros((states, width), F32), jnp.ones((1, width), F32))
    whole = None
    for u in range(radix if not last else radix - 1):
        tail = ordered[u, states:].astype(F32)
        one, fall = ordered[u, :states].astype(F32), tail[0:1] + tail[1:2]
        if u < radix - 1:
            took = jnp.where(me > u, 1.0, 0.0)
            keep = jnp.where(me > u, fall, 1.0)
            earlier = (earlier[0] * keep + one * took, earlier[1] * keep)
        if not last:
            whole = (one, fall) if u == 0 else (whole[0] * fall + one, whole[1] * fall)
    state, fall = earlier
    if before is not None:
        state = state * before[states : states + 1] + before[:states]
        fall = fall * before[states : states + 1]
    if last:
        outs[0][...] = state.astype(BF16)
        return
    outs[0][:states] = state
    outs[0][states:] = jnp.broadcast_to(fall, (8, width))
    outs[1][:states] = whole[0].astype(BF16)
    high, low = split(whole[1])
    lines = iota((EXTRA, width), 0)
    outs[1][states:] = jnp.where(lines == 0, high, jnp.where(lines == 1, low, 0.0)).astype(BF16)


def end_kernel(n, *refs):
    pieces = refs[:n]
    x, live, local, gate, query, decay, earlier, fall, gate_g, w_out, out, mixed = refs[n:]
    me = lax.axis_index("curve")
    rows, inner = local.shape
    part = inner // n
    squares = jnp.zeros((rows, 1), F32)
    for k in range(n):
        at = pl.ds(pl.multiple_of((me ^ k) * part, 128), part)
        state = pieces[k][...].astype(F32) * fall[0:1, at] + earlier[:, at]
        head_out = dot(query[...], state.astype(BF16)) * decay[:, at] + local[:, at]
        gated = head_out * gate[:, at]
        squares += jnp.sum(gated * gated, axis=-1, keepdims=True)
        mixed[:, at] = gated
    scale = lax.rsqrt(squares * (1.0 / inner) + EPS)
    scaled = (mixed[...] * scale * gate_g[1:2, :]).astype(BF16)
    update = dot(scaled, w_out[1])
    for j in range(0, x.shape[1], 128):
        at = slice(j, j + 128)
        out[0, :, at] = (x[:, at].astype(F32) + live[...] * update[:, at]).astype(BF16)


def call(kernel, outs, scratch, *args, fixed=True, out_fixed=True, spaces=None):
    vmem = pl.BlockSpec(memory_space=pltpu.VMEM)
    spaces = spaces or [pltpu.VMEM] * len(args)
    if fixed:
        spaces = [pltpu.VMEM] * len(args)
    args = [arg if s == pltpu.SMEM else pltpu.with_memory_space_constraint(arg, s) for arg, s in zip(args, spaces)]
    return pl.pallas_call(
        kernel,
        out_shape=[(pltpu.VMEM if out_fixed else jax.ShapeDtypeStruct)(shape, kind) for shape, kind in outs],
        in_specs=[pl.BlockSpec(memory_space=space) for space in spaces],
        out_specs=[vmem] * len(outs),
        scratch_shapes=scratch,
        compiler_params=pltpu.CompilerParams(vmem_limit_bytes=VMEM_BYTES),
    )(*args)


def swap(value, axis, mask, size):
    return lax.ppermute(value, axis, [(i, i ^ mask) for i in range(size)])


def levels(size):
    steps, stride = [], 1
    while stride < size:
        radix = 4 if stride > 1 and size // stride >= 4 else 2
        steps.append((radix, stride))
        stride *= radix
    return steps


def local(
    tiles,
    points,
    valid_rows,
    dest_shard,
    dest_slot,
    norm_gain,
    w_xz,
    w_bc,
    w_dt,
    dt_bias,
    decay_rate,
    skip_gain,
    gate_gain,
    w_out,
):
    n = lax.axis_size("curve")
    rows, width = points.shape[1:]
    heads, inner, key_width = w_dt.shape[2], w_out.shape[1], w_bc.shape[2] // 2
    part = inner // n
    (packed,) = call(
        pack_kernel,
        [((rows + EXTRA, width), BF16)],
        [],
        points,
        valid_rows,
        dest_shard[0],
        dest_slot[0],
        fixed=False,
        spaces=[pltpu.VMEM] + [pltpu.SMEM] * 3,
    )
    pieces = [packed] + [swap(packed, "curve", k, n) for k in range(1, n)]
    params = (norm_gain, w_xz, w_bc, jnp.swapaxes(w_dt, 1, 2), dt_bias, decay_rate, gate_gain, w_out)
    spread, skip, norm_gain, w_xz, w_bc, w_dt, dt_bias, decay_rate, gate_gain, w_out = call(
        functools.partial(load_kernel, len(params)),
        [((128, 2 * inner), BF16), ((8 * skip_gain.shape[0], inner), F32)] + [(p.shape, p.dtype) for p in params],
        [pltpu.SemaphoreType.DMA((len(params),))],
        skip_gain,
        *params,
        fixed=False,
        spaces=[pltpu.VMEM] + [pltpu.HBM] * len(params),
    )
    send, own_x, own_live, normed_two, key_two, own_query, turned_two, seen_two = call(
        functools.partial(tile_kernel, n),
        [
            ((key_width + EXTRA, part), BF16),
            ((rows, width), BF16),
            ((rows, 128), F32),
            ((n, rows, width), BF16),
            ((n, rows, key_width), BF16),
            ((rows, key_width), BF16),
            ((n, rows, 128), F32),
            ((n, heads, rows), F32),
        ],
        [
            pltpu.VMEM((n, rows, width), BF16),
            pltpu.VMEM((n, rows, inner), BF16),
            pltpu.VMEM((n, rows, inner), F32),
            pltpu.VMEM((n, rows, key_width), BF16),
            pltpu.VMEM((n, rows, key_width), BF16),
            pltpu.VMEM((n, heads, rows), F32),
            pltpu.VMEM((n, heads, rows), F32),
            pltpu.VMEM((n, heads, rows), F32),
            pltpu.VMEM((n, rows, inner), BF16),
            pltpu.VMEM((rows, inner), F32),
            pltpu.VMEM((n, rows, width), BF16),
            pltpu.VMEM((key_width, inner), F32),
            pltpu.VMEM((n * rows, width), F32),
            pltpu.SMEM((n,), jnp.int32),
            pltpu.SMEM((n,), jnp.int32),
            pltpu.SMEM((n,), jnp.int32),
        ],
        *pieces,
        spread,
        skip,
        norm_gain,
        w_xz,
        w_bc,
        w_dt,
        dt_bias,
        decay_rate,
        gate_gain,
        w_out,
    )
    own, gate, decay = call(
        own_kernel,
        [((rows, inner), F32)] * 3,
        [],
        normed_two,
        key_two,
        own_query,
        turned_two,
        seen_two,
        spread,
        skip,
        w_xz,
    )
    earlier, fall = call(
        earlier_kernel,
        [((key_width, inner), F32), ((8, inner), F32)],
        [],
        normed_two,
        key_two,
        turned_two,
        spread,
        w_xz,
    )
    before = []
    steps = levels(tiles)
    for i, (radix, stride) in enumerate(steps):
        last = i == len(steps) - 1
        parts = [send] + [swap(send, "tile", k * stride, tiles) for k in range(1, radix)]
        outs = [((key_width, part), BF16)]
        if not last:
            outs = [((key_width + 8, part), F32), ((key_width + EXTRA, part), BF16)]
        got = call(
            functools.partial(join_kernel, radix, stride, last),
            outs,
            [pltpu.VMEM((radix, key_width + EXTRA, part), BF16)],
            *parts,
            *before,
            fall if last else decay,
        )
        if last:
            incoming = got[0]
        else:
            before, send = [got[0]], got[1]
    states = [incoming] + [swap(incoming, "curve", k, n) for k in range(1, n)]
    (out,) = call(
        functools.partial(end_kernel, n),
        [((1, rows, width), BF16)],
        [pltpu.VMEM((rows, inner), F32)],
        *states,
        own_x,
        own_live,
        own,
        gate,
        own_query,
        decay,
        earlier,
        fall,
        gate_gain,
        w_out,
        out_fixed=False,
    )
    return out


def solution(mesh):
    in_specs = (
        P("tile", "curve", None),
        P("tile", "curve"),
        P("tile", "curve", None),
        P("tile", "curve", None),
    ) + (P(),) * 9
    return jax.shard_map(
        functools.partial(local, mesh.shape["tile"]),
        mesh=mesh,
        in_specs=in_specs,
        out_specs=P("tile", "curve", None),
        check_vma=False,
    )
```

```python
import functools

import jax
import jax.numpy as jnp
from jax import lax
from jax.experimental import pallas as pl
from jax.experimental.pallas import tpu as pltpu
from jax.sharding import PartitionSpec as P

F32, BF16 = jnp.float32, jnp.bfloat16
EPS = 1e-5
LOG2E = 1.4426950408889634
EXTRA = 16
VMEM_BYTES = 20 * 1024 * 1024


def dot(a, b):
    return jnp.dot(a, b, preferred_element_type=F32)


def dot_nt(a, b):
    return lax.dot_general(a, b, (((1,), (1,)), ((), ())), preferred_element_type=F32)


def turn(x):
    return x.astype(F32).T.astype(x.dtype)


def silu(x):
    half = 0.5 * x
    return half + half * jnp.tanh(half)


def split(x):
    hi = x.astype(BF16).astype(F32)
    return hi, x - hi


def normalise(x, gain):
    wide = x.astype(F32)
    return (wide * lax.rsqrt(jnp.mean(wide * wide, axis=-1, keepdims=True) + EPS) * gain).astype(BF16)


def iota(shape, axis):
    return lax.broadcasted_iota(jnp.int32, shape, axis)


def column(row):
    heads = row.shape[1]
    same = iota((heads, heads), 0) == iota((heads, heads), 1)
    return jnp.sum(jnp.where(same, row, 0.0), axis=1, keepdims=True)


def head_steps(normed, valids, w_dt_t, bias, rate):
    heads = w_dt_t.shape[0]
    rows = normed.shape[0] // len(valids)
    raw = dot_nt(w_dt_t, normed) + column(bias)
    steps = jnp.maximum(raw, 0.0) + jnp.log1p(jnp.exp(-jnp.abs(raw)))
    lane = iota((heads, rows), 1)
    steps = jnp.concatenate(
        [
            jnp.where(lane < valid, steps[:, c * rows : (c + 1) * rows], 0.0)
            for c, valid in enumerate(valids)
        ],
        axis=0,
    )
    falls = -steps * jnp.concatenate([column(rate) * LOG2E] * len(valids), axis=0)
    upper = jnp.where(iota((rows, rows), 0) <= iota((rows, rows), 1), 1.0, 0.0).astype(BF16)
    high, rest = split(falls)
    middle, low = split(rest)
    running = (
        dot(high.astype(BF16), upper) + dot(middle.astype(BF16), upper) + dot(low.astype(BF16), upper)
    )
    to_end = jnp.exp2(running[:, rows - 1 : rows] - running) * steps
    return steps, to_end, running


def by_rows(to_end, running):
    parts = [*split(to_end), *split(jnp.exp2(running)), running]
    used = len(parts) * running.shape[0]
    stack = jnp.concatenate(parts + [jnp.zeros((128 - used, running.shape[1]), F32)], axis=0)
    return stack.T


def seen_from(steps, running):
    return running - jnp.where(steps > 0.0, jnp.log2(jnp.maximum(steps, 1e-37)), -1e30)


def inside_pair(turned, seen, scores, value, head, heads):
    rows = turned.shape[0]
    at = 4 * heads + head
    weights = [
        (jnp.exp2(jnp.minimum(turned[:, at + k : at + k + 1] - seen[head + k : head + k + 1], 120.0)) * scores).astype(BF16)
        for k in range(2)
    ]
    left = iota((rows, 128), 1) < 64
    zero = jnp.zeros_like(value)
    both = jnp.concatenate([jnp.where(left, value, zero), jnp.where(left, zero, value)], axis=0)
    return dot(jnp.concatenate(weights, axis=1), both)


def masked_scores(query, key):
    rows = query.shape[0]
    return jnp.where(iota((rows, rows), 0) >= iota((rows, rows), 1), dot_nt(query, key), 0.0)


def make_spread(spread, heads):
    inner = spread.shape[1] // 2
    head = lax.shift_right_logical(iota((128, inner), 1), (inner // heads).bit_length() - 1)
    row = iota((128, inner), 0)
    for g in range(2):
        hit = (row == head + 2 * heads * g) | (row == head + 2 * heads * g + heads)
        spread[:, g * inner : (g + 1) * inner] = jnp.where(hit, 1.0, 0.0).astype(BF16)


def make_skip(skip_g, skip):
    layers, heads = skip_g.shape
    inner = skip.shape[1]
    head = lax.shift_right_logical(iota((heads, inner), 1), (inner // heads).bit_length() - 1)
    ones = jnp.where(head == iota((heads, inner), 0), 1.0, 0.0)
    for layer in range(layers):
        wide = jnp.broadcast_to(skip_g[layer : layer + 1, :], (8, heads))
        skip[8 * layer : 8 * layer + 8, :] = jnp.dot(
            wide, ones, preferred_element_type=F32, precision=lax.Precision.HIGHEST
        )


def number(numbers, lane):
    return jnp.sum(jnp.where(iota((1, 128), 1) == lane, numbers[...].astype(F32), 0.0)).astype(jnp.int32)


def pieces_work(xs, valids, slots, params, work):
    norm_g, w_xz, w_bc, w_dt, bias, rate, spread, skip = params
    gates, local, decay, grown, queries = work
    rows = xs[0].shape[0]
    heads, inner, key_width = w_dt.shape[1], w_xz.shape[1] // 2, w_bc.shape[2] // 2
    normed = normalise(jnp.concatenate(xs, axis=0), norm_g[0:1, :])
    bc = silu(dot(normed, w_bc[0])).astype(BF16)
    steps, to_end, running = head_steps(normed, valids, w_dt[0], bias[0:1, :], rate[0:1, :])
    seen = seen_from(steps, running)
    parts = []
    for i, slot in enumerate(slots):
        at, of = slice(i * rows, (i + 1) * rows), slice(i * heads, (i + 1) * heads)
        key, query = bc[at, :key_width], bc[at, key_width:]
        queries[slot] = query
        turned = by_rows(to_end[of], running[of])
        parts.append((slot, at, turned, turned.astype(BF16), seen[of], masked_scores(query, key), turn(key)))
    for j in range(0, inner, 256):
        cols, ends = slice(j, j + 256), slice(inner + j, inner + j + 256)
        values = silu(dot(normed, w_xz[:, cols])).astype(BF16)
        gate = silu(dot(normed, w_xz[:, ends]))
        for slot, at, turned, lhs, seen_here, scores, key_t in parts:
            value = values[at]
            wide = value.astype(F32)
            gates[slot, :, cols] = gate[at]
            decay[slot, :, cols] = dot(lhs, spread[:, ends])
            grown[slot, :, cols] = dot(key_t, (wide * dot(lhs, spread[:, cols])).astype(BF16))
            base = skip[0:1, cols] * wide
            for k in range(2):
                half = slice(128 * k, 128 * k + 128)
                head = (j + 128 * k) * heads // inner
                local[slot, :, j + 128 * k : j + 128 * k + 128] = (
                    inside_pair(turned, seen_here, scores, value[:, half], head, heads) + base[:, half]
                )


def begin_kernel(count, x, info, skip_g, w_xz, *refs):
    sources, w_held, held = refs[:count], refs[count], refs[count + 1 : 2 * count + 1]
    spread, skip, *work = refs[2 * count + 1 : -1]
    sems = refs[-1]
    copies = [pltpu.make_async_copy(a, b, sems.at[i]) for i, (a, b) in enumerate(zip(sources, held))]
    copies.append(pltpu.make_async_copy(w_xz.at[0], w_held, sems.at[count]))
    for copy in copies:
        copy.start()
    norm_g, w_bc, w_dt, bias, rate = held[:5]
    make_spread(spread, w_dt.shape[1])
    make_skip(skip_g, skip)
    for copy in copies:
        copy.wait()
    pieces_work([x[0]], [number(info, 0)], [0], (norm_g, w_held, w_bc, w_dt, bias, rate, spread, skip), work)


def sibling_kernel(x, info, norm_g, w_held, w_bc, w_dt, bias, rate, spread, skip, *refs):
    work = refs[-5:]
    pieces_work([x[...]], [number(info, 0)], [1], (norm_g, w_held, w_bc, w_dt, bias, rate, spread, skip), work)


def relay_kernel(x, *refs):
    refs[-1][...] = x[...]


def tile_kernel(n, *refs):
    pieces, infos, refs = refs[:n], refs[n : 2 * n], refs[2 * n :]
    norm_g, w_held, w_bc, w_dt, bias, rate, spread, skip, gate_g, w_xz, w_out = refs[:11]
    refs = refs[16:]
    work, refs = refs[:5], refs[5:]
    (
        w_two,
        w_out_two,
        send,
        own_x,
        own_live,
        normed_two,
        key_two,
        own_query,
        turned_two,
        seen_two,
        w_out_one,
        scaled,
        mixed,
        x_two,
        state,
        valid_two,
        dest,
        sems,
    ) = refs
    gates, local, decay, grown, queries = work
    me = lax.axis_index("curve")
    rows, width = x_two.shape[1:]
    heads = w_dt.shape[1]
    inner = w_out.shape[1]
    key_width = w_bc.shape[2] // 2
    part = inner // n
    copies = [
        pltpu.make_async_copy(w_out.at[0], w_out_one, sems.at[0]),
        pltpu.make_async_copy(w_xz.at[1], w_two, sems.at[1]),
        pltpu.make_async_copy(w_out.at[1], w_out_two, sems.at[2]),
    ]
    for copy in copies:
        copy.start()
    valid = [number(info, 0) for info in infos]
    for k in range(n):
        dest[k] = number(infos[k], 1) + number(infos[k], 2)
        valid_two[dest[k]] = valid[k]
    xs = [pieces[0][0]] + [piece[...] for piece in pieces[1:]]
    params = (norm_g, w_held, w_bc, w_dt, bias, rate, spread, skip)
    pieces_work(xs[2:], valid[2:], list(range(2, n)), params, work)

    for c in range(n):
        k = me ^ c
        query = queries[k]
        squares = jnp.zeros((rows, 1), F32)
        for j in range(0, inner, 256):
            at = slice(j, j + 256)
            out = local[k, :, at]
            if c:
                old = state[:, at]
                out += dot(query, old.astype(BF16)) * decay[k, :, at]
                state[:, at] = old * decay[k, rows - 1 :, at] + grown[k, :, at]
            else:
                state[:, at] = grown[k, :, at]
            gated = out * gates[k, :, at]
            mixed[:, at] = gated
            squares += jnp.sum(gated * gated, axis=-1, keepdims=True)
        scale = lax.rsqrt(squares * (1.0 / inner) + EPS)
        scaled[k] = (mixed[...] * scale * gate_g[0:1, :]).astype(BF16)
    copies[0].wait()
    flat = dot(scaled[...].reshape(n * rows, inner), w_out_one[...])
    row = iota((rows, 1), 0)
    for k in range(n):
        update = jnp.where(row < valid[k], flat[k * rows : (k + 1) * rows, :], 0.0)
        x_two[dest[k]] = (xs[k].astype(F32) + update).astype(BF16)

    own_x[...] = x_two[me]
    own_live[...] = jnp.where(iota((rows, 128), 0) < valid_two[me], 1.0, 0.0)
    normed = normalise(x_two[...].reshape(n * rows, width), norm_g[1:2, :])
    bc = silu(dot(normed, w_bc[1])).astype(BF16)
    steps, to_end, running = head_steps(
        normed, [valid_two[c] for c in range(n)], w_dt[1], bias[1:2, :], rate[1:2, :]
    )
    seen = seen_from(steps, running)
    copies[1].wait()
    at = pl.ds(pl.multiple_of(me * part, 128), part)
    value = silu(dot(normed, w_two[:, at]))
    total = jnp.zeros((key_width, part), F32)
    fall = jnp.ones((1, part), F32)
    for c in range(n):
        queries[c] = bc[c * rows : (c + 1) * rows, key_width:]
        key = bc[c * rows : (c + 1) * rows, :key_width]
        key_two[c] = key
        normed_two[c] = normed[c * rows : (c + 1) * rows]
        heads_at = slice(c * heads, (c + 1) * heads)
        seen_two[c] = seen[heads_at]
        turned = by_rows(to_end[heads_at], running[heads_at])
        turned_two[c] = turned
        lhs = turned.astype(BF16)
        to_end_x = dot(lhs, spread[:, at])
        end_x = dot(lhs[rows - 16 :], spread[:, pl.ds(pl.multiple_of(inner + me * part, 128), part)])[15:16]
        weighted = value[c * rows : (c + 1) * rows].astype(BF16).astype(F32) * to_end_x
        total = total * end_x + dot(turn(key), weighted.astype(BF16))
        fall = fall * end_x
    own_query[...] = queries[me]
    send[:key_width] = total.astype(BF16)
    high, low = split(fall)
    lines = iota((EXTRA, part), 0)
    send[key_width:] = jnp.where(lines == 0, high, jnp.where(lines == 1, low, 0.0)).astype(BF16)
    copies[2].wait()


def own_kernel(normed_two, key_two, query, turned_two, seen_two, spread, skip, w_xz, local, gate, decay):
    me = lax.axis_index("curve")
    inner = local.shape[1]
    heads = seen_two.shape[1]
    normed = normed_two[me]
    turned = turned_two[me]
    seen = seen_two[me]
    lhs = turned.astype(BF16)
    scores = masked_scores(query[...], key_two[me])
    for j in range(0, inner, 256):
        at = slice(j, j + 256)
        value = silu(dot(normed, w_xz[:, at])).astype(BF16)
        gate[:, at] = silu(dot(normed, w_xz[:, inner + j : inner + j + 256]))
        decay[:, at] = dot(lhs, spread[:, inner + j : inner + j + 256])
        base = skip[8:9, at] * value.astype(F32)
        for k in range(2):
            half = slice(128 * k, 128 * k + 128)
            head = (j + 128 * k) * heads // inner
            local[:, j + 128 * k : j + 128 * k + 128] = (
                inside_pair(turned, seen, scores, value[:, half], head, heads) + base[:, half]
            )


def earlier_kernel(normed_two, key_two, turned_two, spread, w_xz, state, fall):
    me = lax.axis_index("curve")
    inner = state.shape[1]
    rows = normed_two.shape[1]
    state[...] = jnp.zeros_like(state)
    fall[...] = jnp.ones_like(fall)

    def chunk(c, _):
        normed = normed_two[c]
        lhs = turned_two[c].astype(BF16)
        key_t = turn(key_two[c])
        for j in range(0, inner, 256):
            at = slice(j, j + 256)
            value = silu(dot(normed, w_xz[:, at])).astype(BF16).astype(F32)
            weighted = value * dot(lhs, spread[:, at])
            end_x = dot(lhs[rows - 16 :], spread[:, inner + j : inner + j + 256])[15:16]
            state[:, at] = state[:, at] * end_x + dot(key_t, weighted.astype(BF16))
            fall[:, at] = fall[:, at] * end_x
        return 0

    lax.fori_loop(0, me, chunk, 0)


def join_kernel(radix, stride, last, *refs):
    parts, before = refs[:radix], refs[radix] if stride > 1 else None
    outs, ordered = refs[radix + 1 + (stride > 1) : -1], refs[-1]
    me = lax.rem(lax.div(lax.axis_index("tile"), stride), radix)
    states = parts[0].shape[0] - EXTRA
    width = parts[0].shape[1]
    for k in range(radix):
        ordered[me ^ k] = parts[k][...]
    earlier = (jnp.zeros((states, width), F32), jnp.ones((1, width), F32))
    whole = None
    for u in range(radix if not last else radix - 1):
        tail = ordered[u, states:].astype(F32)
        one, fall = ordered[u, :states].astype(F32), tail[0:1] + tail[1:2]
        if u < radix - 1:
            took = jnp.where(me > u, 1.0, 0.0)
            keep = jnp.where(me > u, fall, 1.0)
            earlier = (earlier[0] * keep + one * took, earlier[1] * keep)
        if not last:
            whole = (one, fall) if u == 0 else (whole[0] * fall + one, whole[1] * fall)
    state, fall = earlier
    if before is not None:
        state = state * before[states : states + 1] + before[:states]
        fall = fall * before[states : states + 1]
    if last:
        outs[0][...] = state.astype(BF16)
        return
    outs[0][:states] = state
    outs[0][states:] = jnp.broadcast_to(fall, (8, width))
    outs[1][:states] = whole[0].astype(BF16)
    high, low = split(whole[1])
    lines = iota((EXTRA, width), 0)
    outs[1][states:] = jnp.where(lines == 0, high, jnp.where(lines == 1, low, 0.0)).astype(BF16)


def end_kernel(n, *refs):
    pieces = refs[:n]
    x, live, local, gate, query, decay, earlier, fall, gate_g, w_out, out, mixed = refs[n:]
    me = lax.axis_index("curve")
    rows, inner = local.shape
    part = inner // n
    squares = jnp.zeros((rows, 1), F32)
    for k in range(n):
        at = pl.ds(pl.multiple_of((me ^ k) * part, 128), part)
        state = pieces[k][...].astype(F32) * fall[0:1, at] + earlier[:, at]
        head_out = dot(query[...], state.astype(BF16)) * decay[:, at] + local[:, at]
        gated = head_out * gate[:, at]
        squares += jnp.sum(gated * gated, axis=-1, keepdims=True)
        mixed[:, at] = gated
    scale = lax.rsqrt(squares * (1.0 / inner) + EPS)
    scaled = (mixed[...] * scale * gate_g[1:2, :]).astype(BF16)
    update = dot(scaled, w_out[...])
    for j in range(0, x.shape[1], 128):
        at = slice(j, j + 128)
        out[0, :, at] = (x[:, at].astype(F32) + live[...] * update[:, at]).astype(BF16)


def call(kernel, outs, scratch, *args, in_hbm=(), aliases={}, out_fixed=True):
    vmem = pl.BlockSpec(memory_space=pltpu.VMEM)
    spaces = [pltpu.HBM if i in in_hbm else pltpu.VMEM for i in range(len(args))]
    args = [pltpu.with_memory_space_constraint(arg, space) for arg, space in zip(args, spaces)]
    return pl.pallas_call(
        kernel,
        out_shape=[(pltpu.VMEM if out_fixed else jax.ShapeDtypeStruct)(shape, kind) for shape, kind in outs],
        in_specs=[pl.BlockSpec(memory_space=space) for space in spaces],
        out_specs=[vmem] * len(outs),
        scratch_shapes=scratch,
        input_output_aliases=aliases,
        compiler_params=pltpu.CompilerParams(vmem_limit_bytes=VMEM_BYTES),
    )(*args)


def swap(value, axis, mask, size):
    return lax.ppermute(value, axis, [(i, i ^ mask) for i in range(size)])


def levels(size):
    steps, stride = [], 1
    while stride < size:
        radix = 4 if stride > 1 and size // stride >= 4 else 2
        steps.append((radix, stride))
        stride *= radix
    return steps


def local(
    tiles,
    points,
    valid_rows,
    dest_shard,
    dest_slot,
    norm_gain,
    w_xz,
    w_bc,
    w_dt,
    dt_bias,
    decay_rate,
    skip_gain,
    gate_gain,
    w_out,
):
    n = lax.axis_size("curve")
    rows, width = points.shape[1:]
    heads, inner, key_width = w_dt.shape[2], w_out.shape[1], w_bc.shape[2] // 2
    part = inner // n
    x = points[0]
    info = jnp.concatenate([valid_rows, dest_shard[0], dest_slot[0], jnp.zeros((1, 125), jnp.int32)], axis=1)
    infos = [info] + [swap(info, "curve", k, n) for k in range(1, n)]
    pieces = [points] + [None] * (n - 1)
    for k in range(2, n, 2):
        pieces[k] = swap(x, "curve", k, n)
    pieces[1] = swap(x, "curve", 1, n)
    params = (norm_gain, w_bc, jnp.swapaxes(w_dt, 1, 2), dt_bias, decay_rate, gate_gain)
    work = [
        ((n, rows, inner), F32),
        ((n, rows, inner), F32),
        ((n, rows, inner), F32),
        ((n, key_width, inner), F32),
        ((n, rows, key_width), BF16),
    ]
    w_held, norm_gain, w_bc, w_dt, dt_bias, decay_rate, gate_gain, spread, skip, *work_done = call(
        functools.partial(begin_kernel, len(params)),
        [(w_xz.shape[1:], BF16)]
        + [(p.shape, p.dtype) for p in params]
        + [((128, 2 * inner), BF16), ((8 * skip_gain.shape[0], inner), F32)]
        + work,
        [pltpu.SemaphoreType.DMA((len(params) + 1,))],
        points,
        info,
        skip_gain,
        w_xz,
        *params,
        in_hbm=range(3, 4 + len(params)),
    )
    for k in range(3, n, 2):
        (passed,) = call(relay_kernel, [((rows, width), BF16)], [], pieces[k - 1], skip, *infos[1:])
        pieces[k] = swap(passed, "curve", 1, n)
    shared = (norm_gain, w_held, w_bc, w_dt, dt_bias, decay_rate, spread, skip)
    work_done = call(
        lambda x, info, late, *refs: sibling_kernel(x, info, *refs),
        work,
        [],
        pieces[1],
        infos[1],
        pieces[2],
        *shared,
        *work_done,
        aliases={11 + i: i for i in range(5)},
    )
    first = 2 * n + 11
    *_, w_two, w_out_two, send, own_x, own_live, normed_two, key_two, own_query, turned_two, seen_two = call(
        functools.partial(tile_kernel, n),
        work
        + [
            (w_xz.shape[1:], BF16),
            (w_out.shape[1:], BF16),
            ((key_width + EXTRA, part), BF16),
            ((rows, width), BF16),
            ((rows, 128), F32),
            ((n, rows, width), BF16),
            ((n, rows, key_width), BF16),
            ((rows, key_width), BF16),
            ((n, rows, 128), F32),
            ((n, heads, rows), F32),
        ],
        [
            pltpu.VMEM(w_out.shape[1:], BF16),
            pltpu.VMEM((n, rows, inner), BF16),
            pltpu.VMEM((rows, inner), F32),
            pltpu.VMEM((n, rows, width), BF16),
            pltpu.VMEM((key_width, inner), F32),
            pltpu.SMEM((n,), jnp.int32),
            pltpu.SMEM((n,), jnp.int32),
            pltpu.SemaphoreType.DMA((3,)),
        ],
        *pieces,
        *infos,
        *shared,
        gate_gain,
        w_xz,
        w_out,
        *work_done,
        in_hbm=(first - 2, first - 1),
        aliases={first + i: i for i in range(5)},
    )
    own, gate, decay = call(
        own_kernel,
        [((rows, inner), F32)] * 3,
        [],
        normed_two,
        key_two,
        own_query,
        turned_two,
        seen_two,
        spread,
        skip,
        w_two,
    )
    earlier, fall = call(
        earlier_kernel,
        [((key_width, inner), F32), ((8, inner), F32)],
        [],
        normed_two,
        key_two,
        turned_two,
        spread,
        w_two,
    )
    before = []
    steps = levels(tiles)
    for i, (radix, stride) in enumerate(steps):
        last = i == len(steps) - 1
        parts = [send] + [swap(send, "tile", k * stride, tiles) for k in range(1, radix)]
        outs = [((key_width, part), BF16)]
        if not last:
            outs = [((key_width + 8, part), F32), ((key_width + EXTRA, part), BF16)]
        got = call(
            functools.partial(join_kernel, radix, stride, last),
            outs,
            [pltpu.VMEM((radix, key_width + EXTRA, part), BF16)],
            *parts,
            *before,
            fall if last else decay,
        )
        if last:
            incoming = got[0]
        else:
            before, send = [got[0]], got[1]
    states = [incoming] + [swap(incoming, "curve", k, n) for k in range(1, n)]
    (out,) = call(
        functools.partial(end_kernel, n),
        [((1, rows, width), BF16)],
        [pltpu.VMEM((rows, inner), F32)],
        *states,
        own_x,
        own_live,
        own,
        gate,
        own_query,
        decay,
        earlier,
        fall,
        gate_gain,
        w_out_two,
        out_fixed=False,
    )
    return out


def solution(mesh):
    in_specs = (
        P("tile", "curve", None),
        P("tile", "curve"),
        P("tile", "curve", None),
        P("tile", "curve", None),
    ) + (P(),) * 9
    return jax.shard_map(
        functools.partial(local, mesh.shape["tile"]),
        mesh=mesh,
        in_specs=in_specs,
        out_specs=P("tile", "curve", None),
        check_vma=False,
    )
```

```python
import functools

import jax
import jax.numpy as jnp
from jax import lax
from jax.experimental import pallas as pl
from jax.experimental.pallas import tpu as pltpu
from jax.sharding import PartitionSpec as P

F32, BF16 = jnp.float32, jnp.bfloat16
EPS = 1e-5
LOG2E = 1.4426950408889634
EXTRA = 16
VMEM_BYTES = 20 * 1024 * 1024


def dot(a, b):
    return jnp.dot(a, b, preferred_element_type=F32)


def dot_nt(a, b):
    return lax.dot_general(a, b, (((1,), (1,)), ((), ())), preferred_element_type=F32)


def turn(x):
    return x.astype(F32).T.astype(x.dtype)


def silu(x):
    half = 0.5 * x
    return half + half * jnp.tanh(half)


def split(x):
    hi = x.astype(BF16).astype(F32)
    return hi, x - hi


def normalise(x, gain):
    wide = x.astype(F32)
    return (wide * lax.rsqrt(jnp.mean(wide * wide, axis=-1, keepdims=True) + EPS) * gain).astype(BF16)


def iota(shape, axis):
    return lax.broadcasted_iota(jnp.int32, shape, axis)


def column(row):
    heads = row.shape[1]
    same = iota((heads, heads), 0) == iota((heads, heads), 1)
    return jnp.sum(jnp.where(same, row, 0.0), axis=1, keepdims=True)


def head_steps(normed, valids, w_dt_t, bias, rate):
    heads = w_dt_t.shape[0]
    rows = normed.shape[0] // len(valids)
    raw = dot_nt(w_dt_t, normed) + column(bias)
    steps = jnp.maximum(raw, 0.0) + jnp.log1p(jnp.exp(-jnp.abs(raw)))
    lane = iota((heads, rows), 1)
    steps = jnp.concatenate(
        [
            jnp.where(lane < valid, steps[:, c * rows : (c + 1) * rows], 0.0)
            for c, valid in enumerate(valids)
        ],
        axis=0,
    )
    falls = -steps * jnp.concatenate([column(rate) * LOG2E] * len(valids), axis=0)
    upper = jnp.where(iota((rows, rows), 0) <= iota((rows, rows), 1), 1.0, 0.0).astype(BF16)
    high, rest = split(falls)
    middle, low = split(rest)
    running = (
        dot(high.astype(BF16), upper) + dot(middle.astype(BF16), upper) + dot(low.astype(BF16), upper)
    )
    to_end = jnp.exp2(running[:, rows - 1 : rows] - running) * steps
    return steps, to_end, running


def by_rows(to_end, running):
    parts = [*split(to_end), *split(jnp.exp2(running)), running]
    used = len(parts) * running.shape[0]
    stack = jnp.concatenate(parts + [jnp.zeros((128 - used, running.shape[1]), F32)], axis=0)
    return stack.T


def seen_from(steps, running):
    return running - jnp.where(steps > 0.0, jnp.log2(jnp.maximum(steps, 1e-37)), -1e30)


def inside_pair(turned, seen, scores, value, head, heads):
    rows = turned.shape[0]
    at = 4 * heads + head
    weights = [
        (jnp.exp2(jnp.minimum(turned[:, at + k : at + k + 1] - seen[head + k : head + k + 1], 120.0)) * scores).astype(BF16)
        for k in range(2)
    ]
    left = iota((rows, 128), 1) < 64
    zero = jnp.zeros_like(value)
    both = jnp.concatenate([jnp.where(left, value, zero), jnp.where(left, zero, value)], axis=0)
    return dot(jnp.concatenate(weights, axis=1), both)


def masked_scores(query, key):
    rows = query.shape[0]
    return jnp.where(iota((rows, rows), 0) >= iota((rows, rows), 1), dot_nt(query, key), 0.0)


def make_spread(spread, heads):
    inner = spread.shape[1] // 2
    head = lax.shift_right_logical(iota((128, inner), 1), (inner // heads).bit_length() - 1)
    row = iota((128, inner), 0)
    for g in range(2):
        hit = (row == head + 2 * heads * g) | (row == head + 2 * heads * g + heads)
        spread[:, g * inner : (g + 1) * inner] = jnp.where(hit, 1.0, 0.0).astype(BF16)


def make_skip(skip_g, skip):
    layers, heads = skip_g.shape
    inner = skip.shape[1]
    head = lax.shift_right_logical(iota((heads, inner), 1), (inner // heads).bit_length() - 1)
    ones = jnp.where(head == iota((heads, inner), 0), 1.0, 0.0)
    for layer in range(layers):
        wide = jnp.broadcast_to(skip_g[layer : layer + 1, :], (8, heads))
        skip[8 * layer : 8 * layer + 8, :] = jnp.dot(
            wide, ones, preferred_element_type=F32, precision=lax.Precision.HIGHEST
        )


def pack_kernel(x, valid, shard, slot, out, sem):
    rows, width = x.shape[1:]
    copy = pltpu.make_async_copy(x.at[0], out.at[pl.ds(0, rows)], sem)
    copy.start()
    line, lane = iota((EXTRA, width), 0), iota((EXTRA, width), 1)
    count = valid[0, 0].astype(F32)
    place = (shard[0, 0, 0] + slot[0, 0, 0]).astype(F32)
    first = jnp.where(lane == 0, count, jnp.where(lane == 1, place, 0.0))
    out[rows:] = jnp.where(line == 0, first, 0.0).astype(BF16)
    copy.wait()


def number(packed, lane):
    extra = packed[packed.shape[0] - EXTRA :, :128].astype(F32)
    hit = (iota((EXTRA, 128), 0) == 0) & (iota((EXTRA, 128), 1) == lane)
    return jnp.sum(jnp.where(hit, extra, 0.0)).astype(jnp.int32)


def block_of(packed):
    return packed[: packed.shape[0] - EXTRA]


def pieces_work(xs, valids, slots, params, work, ready=lambda: None):
    norm_g, w_xz, w_bc, w_dt, bias, rate, spread, skip = params
    gates, local, decay, grown, queries = work
    rows = xs[0].shape[0]
    heads, inner, key_width = w_dt.shape[1], w_xz.shape[1] // 2, w_bc.shape[2] // 2
    normed = normalise(jnp.concatenate(xs, axis=0), norm_g[0:1, :])
    bc = silu(dot(normed, w_bc[0])).astype(BF16)
    steps, to_end, running = head_steps(normed, valids, w_dt[0], bias[0:1, :], rate[0:1, :])
    seen = seen_from(steps, running)
    parts = []
    for i, slot in enumerate(slots):
        at, of = slice(i * rows, (i + 1) * rows), slice(i * heads, (i + 1) * heads)
        key, query = bc[at, :key_width], bc[at, key_width:]
        queries[slot] = query
        turned = by_rows(to_end[of], running[of])
        parts.append((slot, at, turned, turned.astype(BF16), seen[of], masked_scores(query, key), turn(key)))
    ready()
    for j in range(0, inner, 256):
        cols, ends = slice(j, j + 256), slice(inner + j, inner + j + 256)
        values = silu(dot(normed, w_xz[:, cols])).astype(BF16)
        gate = silu(dot(normed, w_xz[:, ends]))
        for slot, at, turned, lhs, seen_here, scores, key_t in parts:
            value = values[at]
            wide = value.astype(F32)
            gates[slot, :, cols] = gate[at]
            decay[slot, :, cols] = dot(lhs, spread[:, ends])
            grown[slot, :, cols] = dot(key_t, (wide * dot(lhs, spread[:, cols])).astype(BF16))
            base = skip[0:1, cols] * wide
            for k in range(2):
                half = slice(128 * k, 128 * k + 128)
                head = (j + 128 * k) * heads // inner
                local[slot, :, j + 128 * k : j + 128 * k + 128] = (
                    inside_pair(turned, seen_here, scores, value[:, half], head, heads) + base[:, half]
                )


def begin_kernel(count, packed, w_xz, *refs):
    sources, w_held, held = refs[:count], refs[count], refs[count + 1 : 2 * count + 1]
    spread, skip, *work = refs[2 * count + 1 : -1]
    sems = refs[-1]
    copies = [pltpu.make_async_copy(a, b, sems.at[i]) for i, (a, b) in enumerate(zip(sources, held))]
    copies.append(pltpu.make_async_copy(w_xz.at[0], w_held, sems.at[count]))
    for copy in copies:
        copy.start()
    norm_g, w_bc, w_dt, bias, rate, skip_g = held[:6]
    make_spread(spread, w_dt.shape[1])
    for copy in copies[:-1]:
        copy.wait()
    make_skip(skip_g, skip)
    params = (norm_g, w_held, w_bc, w_dt, bias, rate, spread, skip)
    pieces_work([block_of(packed)], [number(packed, 0)], [0], params, work, copies[-1].wait)


def sibling_kernel(packed, late, *refs):
    pieces_work([block_of(packed)], [number(packed, 0)], [1], refs[:8], refs[-5:])


def relay_kernel(x, *refs):
    refs[-1][...] = x[...]


def tile_kernel(n, *refs):
    pieces, refs = refs[:n], refs[n:]
    norm_g, w_held, w_bc, w_dt, bias, rate, spread, skip, gate_g, w_xz, w_out = refs[:11]
    refs = refs[16:]
    work, refs = refs[:5], refs[5:]
    (
        w_two,
        w_out_two,
        keep,
        send,
        own_x,
        own_live,
        normed_two,
        key_two,
        own_query,
        turned_two,
        seen_two,
        w_out_one,
        scaled,
        mixed,
        x_two,
        state,
        halves,
        valid_two,
        dest,
        sems,
    ) = refs
    gates, local, decay, grown, queries = work
    me = lax.axis_index("curve")
    rows, width = x_two.shape[1:]
    heads = w_dt.shape[1]
    inner = w_out.shape[1]
    key_width = w_bc.shape[2] // 2
    part = inner // n
    copies = [
        pltpu.make_async_copy(w_out.at[0], w_out_one, sems.at[0]),
        pltpu.make_async_copy(w_xz.at[1], w_two, sems.at[1]),
        pltpu.make_async_copy(w_out.at[1], w_out_two, sems.at[2]),
    ]
    for copy in copies:
        copy.start()
    valid = [number(piece, 0) for piece in pieces]
    for k in range(n):
        dest[k] = number(pieces[k], 1)
        valid_two[dest[k]] = valid[k]
    xs = [block_of(piece) for piece in pieces]
    params = (norm_g, w_held, w_bc, w_dt, bias, rate, spread, skip)
    pieces_work(xs[2:], valid[2:], list(range(2, n)), params, work)

    for c in range(n):
        k = me ^ c
        query = queries[k]
        squares = jnp.zeros((rows, 1), F32)
        for j in range(0, inner, 256):
            at = slice(j, j + 256)
            out = local[k, :, at]
            if c:
                old = state[:, at]
                out += dot(query, old.astype(BF16)) * decay[k, :, at]
                state[:, at] = old * decay[k, rows - 1 :, at] + grown[k, :, at]
            else:
                state[:, at] = grown[k, :, at]
            gated = out * gates[k, :, at]
            mixed[:, at] = gated
            squares += jnp.sum(gated * gated, axis=-1, keepdims=True)
        scale = lax.rsqrt(squares * (1.0 / inner) + EPS)
        scaled[k] = (mixed[...] * scale * gate_g[0:1, :]).astype(BF16)
    copies[0].wait()
    flat = dot(scaled[...].reshape(n * rows, inner), w_out_one[...])
    row = iota((rows, 1), 0)
    for k in range(n):
        update = jnp.where(row < valid[k], flat[k * rows : (k + 1) * rows, :], 0.0)
        x_two[dest[k]] = (xs[k].astype(F32) + update).astype(BF16)

    own_x[...] = x_two[me]
    own_live[...] = jnp.where(iota((rows, 128), 0) < valid_two[me], 1.0, 0.0)
    normed = normalise(x_two[...].reshape(n * rows, width), norm_g[1:2, :])
    bc = silu(dot(normed, w_bc[1])).astype(BF16)
    steps, to_end, running = head_steps(
        normed, [valid_two[c] for c in range(n)], w_dt[1], bias[1:2, :], rate[1:2, :]
    )
    seen = seen_from(steps, running)
    copies[1].wait()
    at = pl.ds(pl.multiple_of(me * part, 128), part)
    value = silu(dot(normed, w_two[:, at]))
    total = jnp.zeros((key_width, part), F32)
    fall = jnp.ones((1, part), F32)
    for c in range(n):
        queries[c] = bc[c * rows : (c + 1) * rows, key_width:]
        key = bc[c * rows : (c + 1) * rows, :key_width]
        key_two[c] = key
        normed_two[c] = normed[c * rows : (c + 1) * rows]
        heads_at = slice(c * heads, (c + 1) * heads)
        seen_two[c] = seen[heads_at]
        turned = by_rows(to_end[heads_at], running[heads_at])
        turned_two[c] = turned
        lhs = turned.astype(BF16)
        to_end_x = dot(lhs, spread[:, at])
        end_x = dot(lhs[rows - 16 :], spread[:, pl.ds(pl.multiple_of(inner + me * part, 128), part)])[15:16]
        weighted = value[c * rows : (c + 1) * rows].astype(BF16).astype(F32) * to_end_x
        total = total * end_x + dot(turn(key), weighted.astype(BF16))
        fall = fall * end_x
    own_query[...] = queries[me]
    half = key_width // 2
    halves[0] = total[:half].astype(BF16)
    halves[1] = total[half:].astype(BF16)
    mine = lax.rem(lax.axis_index("tile"), 2)
    for out, which in ((keep, mine), (send, 1 - mine)):
        out[:half] = halves[which]
        out[half:] = decay_rows(fall)
    copies[2].wait()


def own_kernel(normed_two, key_two, query, turned_two, seen_two, spread, skip, w_xz, local, gate, decay):
    me = lax.axis_index("curve")
    inner = local.shape[1]
    heads = seen_two.shape[1]
    normed = normed_two[me]
    turned = turned_two[me]
    seen = seen_two[me]
    lhs = turned.astype(BF16)
    scores = masked_scores(query[...], key_two[me])
    for j in range(0, inner, 256):
        at = slice(j, j + 256)
        value = silu(dot(normed, w_xz[:, at])).astype(BF16)
        gate[:, at] = silu(dot(normed, w_xz[:, inner + j : inner + j + 256]))
        decay[:, at] = dot(lhs, spread[:, inner + j : inner + j + 256])
        base = skip[8:9, at] * value.astype(F32)
        for k in range(2):
            half = slice(128 * k, 128 * k + 128)
            head = (j + 128 * k) * heads // inner
            local[:, j + 128 * k : j + 128 * k + 128] = (
                inside_pair(turned, seen, scores, value[:, half], head, heads) + base[:, half]
            )


def earlier_kernel(normed_two, key_two, turned_two, spread, w_xz, state, fall):
    me = lax.axis_index("curve")
    inner = state.shape[1]
    rows = normed_two.shape[1]
    state[...] = jnp.zeros_like(state)
    fall[...] = jnp.ones_like(fall)

    def chunk(c, _):
        normed = normed_two[c]
        lhs = turned_two[c].astype(BF16)
        key_t = turn(key_two[c])
        for j in range(0, inner, 256):
            at = slice(j, j + 256)
            value = silu(dot(normed, w_xz[:, at])).astype(BF16).astype(F32)
            weighted = value * dot(lhs, spread[:, at])
            end_x = dot(lhs[rows - 16 :], spread[:, inner + j : inner + j + 256])[15:16]
            state[:, at] = state[:, at] * end_x + dot(key_t, weighted.astype(BF16))
            fall[:, at] = fall[:, at] * end_x
        return 0

    lax.fori_loop(0, me, chunk, 0)


def pair_kernel(mine, theirs, beside, first, send, ordered):
    me = lax.rem(lax.axis_index("tile"), 2)
    half, width = mine.shape[0] - EXTRA, mine.shape[1]
    ordered[me] = mine[...]
    ordered[1 - me] = theirs[...]
    (one, fall_one), (two, fall_two) = (state_and_decay(ordered, u) for u in range(2))
    first[:half] = one
    first[half:] = jnp.broadcast_to(fall_one, (8, width))
    send[:half] = (one * fall_two + two).astype(BF16)
    send[half:] = decay_rows(fall_one * fall_two)


def decay_rows(fall):
    high, low = split(fall)
    lines = iota((EXTRA, fall.shape[1]), 0)
    return jnp.where(lines == 0, high, jnp.where(lines == 1, low, 0.0)).astype(BF16)


def state_and_decay(ordered, u):
    states = ordered.shape[1] - EXTRA
    tail = ordered[u, states:].astype(F32)
    return ordered[u, :states].astype(F32), tail[0:1] + tail[1:2]


def join_kernel(radix, stride, last, *refs):
    deeper = stride > 2
    parts, before = refs[:radix], refs[radix] if deeper else None
    refs = refs[radix + deeper :]
    tile = lax.axis_index("tile")
    me = lax.rem(lax.div(tile, stride), radix)
    half, width = parts[0].shape[0] - EXTRA, parts[0].shape[1]
    ordered = refs[-1]
    for k in range(radix):
        ordered[me ^ k] = parts[k][...]
    earlier = (jnp.zeros((half, width), F32), jnp.ones((1, width), F32))
    whole = None
    for u in range(radix if not last else radix - 1):
        one, fall = state_and_decay(ordered, u)
        if u < radix - 1:
            took = jnp.where(me > u, 1.0, 0.0)
            keep = jnp.where(me > u, fall, 1.0)
            earlier = (earlier[0] * keep + one * took, earlier[1] * keep)
        if not last:
            whole = (one, fall) if u == 0 else (whole[0] * fall + one, whole[1] * fall)
    state, fall = earlier
    if deeper:
        state = state * before[half : half + 1] + before[:half]
        fall = fall * before[half : half + 1]
    if not last:
        outs = refs[1:3]
        outs[0][:half] = state
        outs[0][half:] = jnp.broadcast_to(fall, (8, width))
        outs[1][:half] = whole[0].astype(BF16)
        outs[1][half:] = decay_rows(whole[1])
        return
    first, mine, theirs = refs[0], refs[2], refs[3]
    second = state * first[half : half + 1] + first[:half]
    odd = lax.rem(tile, 2) == 1
    mine[...] = jnp.where(odd, second, state).astype(BF16)
    theirs[...] = jnp.where(odd, state, second).astype(BF16)


def end_kernel(n, *refs):
    near, far = refs[:n], refs[n : 2 * n]
    x, live, local, gate, query, decay, earlier, fall, gate_g, w_out, out, mixed = refs[2 * n :]
    me = lax.axis_index("curve")
    even = lax.rem(lax.axis_index("tile"), 2) == 0
    rows, inner = local.shape
    part = inner // n
    squares = jnp.zeros((rows, 1), F32)
    for k in range(n):
        at = pl.ds(pl.multiple_of((me ^ k) * part, 128), part)
        ours, others = near[k][...].astype(F32), far[k][...].astype(F32)
        entering = [jnp.where(even, ours, others), jnp.where(even, others, ours)]
        state = jnp.concatenate(entering, axis=0) * fall[0:1, at] + earlier[:, at]
        head_out = dot(query[...], state.astype(BF16)) * decay[:, at] + local[:, at]
        gated = head_out * gate[:, at]
        squares += jnp.sum(gated * gated, axis=-1, keepdims=True)
        mixed[:, at] = gated
    scale = lax.rsqrt(squares * (1.0 / inner) + EPS)
    scaled = (mixed[...] * scale * gate_g[1:2, :]).astype(BF16)
    update = dot(scaled, w_out[...])
    for j in range(0, x.shape[1], 128):
        at = slice(j, j + 128)
        out[0, :, at] = (x[:, at].astype(F32) + live[...] * update[:, at]).astype(BF16)


def call(kernel, outs, scratch, *args, in_hbm=(), free=(), aliases={}, out_fixed=True):
    vmem = pl.BlockSpec(memory_space=pltpu.VMEM)
    spaces = [pltpu.HBM if i in in_hbm else pltpu.VMEM for i in range(len(args))]
    spaces = [pltpu.SMEM if i in free else space for i, space in enumerate(spaces)]
    args = [
        arg if space == pltpu.SMEM else pltpu.with_memory_space_constraint(arg, space)
        for arg, space in zip(args, spaces)
    ]
    return pl.pallas_call(
        kernel,
        out_shape=[(pltpu.VMEM if out_fixed else jax.ShapeDtypeStruct)(shape, kind) for shape, kind in outs],
        in_specs=[pl.BlockSpec(memory_space=space) for space in spaces],
        out_specs=[vmem] * len(outs),
        scratch_shapes=scratch,
        input_output_aliases=aliases,
        compiler_params=pltpu.CompilerParams(vmem_limit_bytes=VMEM_BYTES),
    )(*args)


def swap(value, axis, mask, size):
    return lax.ppermute(value, axis, [(i, i ^ mask) for i in range(size)])


def levels(size):
    steps, stride = [], 2
    while stride < size:
        radix = 4 if size // stride >= 4 else 2
        steps.append((radix, stride))
        stride *= radix
    return steps


def local(
    tiles,
    points,
    valid_rows,
    dest_shard,
    dest_slot,
    norm_gain,
    w_xz,
    w_bc,
    w_dt,
    dt_bias,
    decay_rate,
    skip_gain,
    gate_gain,
    w_out,
):
    n = lax.axis_size("curve")
    rows, width = points.shape[1:]
    heads, inner, key_width = w_dt.shape[2], w_out.shape[1], w_bc.shape[2] // 2
    part = inner // n
    half = key_width // 2
    (packed,) = call(
        pack_kernel,
        [((rows + EXTRA, width), BF16)],
        [pltpu.SemaphoreType.DMA],
        points,
        valid_rows,
        dest_shard,
        dest_slot,
        in_hbm=(0,),
        free=(1, 2, 3),
    )
    pieces = [packed] + [None] * (n - 1)
    for k in range(2, n, 2):
        pieces[k] = swap(packed, "curve", k, n)
    pieces[1] = swap(packed, "curve", 1, n)
    params = (norm_gain, w_bc, jnp.swapaxes(w_dt, 1, 2), dt_bias, decay_rate, skip_gain, gate_gain)
    work = [
        ((n, rows, inner), F32),
        ((n, rows, inner), F32),
        ((n, rows, inner), F32),
        ((n, key_width, inner), F32),
        ((n, rows, key_width), BF16),
    ]
    w_held, norm_gain, w_bc, w_dt, dt_bias, decay_rate, _, gate_gain, spread, skip, *work_done = call(
        functools.partial(begin_kernel, len(params)),
        [(w_xz.shape[1:], BF16)]
        + [(p.shape, p.dtype) for p in params]
        + [((128, 2 * inner), BF16), ((8 * skip_gain.shape[0], inner), F32)]
        + work,
        [pltpu.SemaphoreType.DMA((len(params) + 1,))],
        packed,
        w_xz,
        *params,
        in_hbm=range(1, 2 + len(params)),
    )
    for k in range(3, n, 2):
        (passed,) = call(relay_kernel, [(packed.shape, BF16)], [], pieces[k - 1], skip)
        pieces[k] = swap(passed, "curve", 1, n)
    shared = (norm_gain, w_held, w_bc, w_dt, dt_bias, decay_rate, spread, skip)
    work_done = call(
        sibling_kernel,
        work,
        [],
        pieces[1],
        pieces[2],
        *shared,
        *work_done,
        aliases={10 + i: i for i in range(5)},
    )
    first = n + 11
    *_, w_two, w_out_two, keep, send, own_x, own_live, normed_two, key_two, own_query, turned_two, seen_two = call(
        functools.partial(tile_kernel, n),
        work
        + [
            (w_xz.shape[1:], BF16),
            (w_out.shape[1:], BF16),
            ((half + EXTRA, part), BF16),
            ((half + EXTRA, part), BF16),
            ((rows, width), BF16),
            ((rows, 128), F32),
            ((n, rows, width), BF16),
            ((n, rows, key_width), BF16),
            ((rows, key_width), BF16),
            ((n, rows, 128), F32),
            ((n, heads, rows), F32),
        ],
        [
            pltpu.VMEM(w_out.shape[1:], BF16),
            pltpu.VMEM((n, rows, inner), BF16),
            pltpu.VMEM((rows, inner), F32),
            pltpu.VMEM((n, rows, width), BF16),
            pltpu.VMEM((key_width, inner), F32),
            pltpu.VMEM((2, half, part), BF16),
            pltpu.SMEM((n,), jnp.int32),
            pltpu.SMEM((n,), jnp.int32),
            pltpu.SemaphoreType.DMA((3,)),
        ],
        *pieces,
        *shared,
        gate_gain,
        w_xz,
        w_out,
        *work_done,
        in_hbm=(first - 2, first - 1),
        aliases={first + i: i for i in range(5)},
    )
    own, gate, decay = call(
        own_kernel,
        [((rows, inner), F32)] * 3,
        [],
        normed_two,
        key_two,
        own_query,
        turned_two,
        seen_two,
        spread,
        skip,
        w_two,
    )
    earlier, fall = call(
        earlier_kernel,
        [((key_width, inner), F32), ((8, inner), F32)],
        [],
        normed_two,
        key_two,
        turned_two,
        spread,
        w_two,
    )
    first, send = call(
        pair_kernel,
        [((half + 8, part), F32), ((half + EXTRA, part), BF16)],
        [pltpu.VMEM((2, half + EXTRA, part), BF16)],
        keep,
        swap(send, "tile", 1, tiles),
        decay,
    )
    before = []
    steps = levels(tiles)
    for i, (radix, stride) in enumerate(steps):
        last = i == len(steps) - 1
        parts = [send] + [swap(send, "tile", k * stride, tiles) for k in range(1, radix)]
        if last:
            outs = [((half, part), BF16)] * 2
        else:
            outs = [((half + 8, part), F32), ((half + EXTRA, part), BF16)]
        got = call(
            functools.partial(join_kernel, radix, stride, last),
            outs,
            [pltpu.VMEM((radix, half + EXTRA, part), BF16)],
            *parts,
            *before,
            *([first, fall] if last else [first]),
        )
        if not last:
            before, send = [got[0]], got[1]
    mine, theirs = got
    near = [mine] + [swap(mine, "curve", k, n) for k in range(1, n)]
    pairs = [(t * n + c, t, c) for t in range(tiles) for c in range(n)]
    far = [
        lax.ppermute(theirs, ("tile", "curve"), [(i, (t ^ 1) * n + (c ^ k)) for i, t, c in pairs]) for k in range(n)
    ]
    (out,) = call(
        functools.partial(end_kernel, n),
        [((1, rows, width), BF16)],
        [pltpu.VMEM((rows, inner), F32)],
        *near,
        *far,
        own_x,
        own_live,
        own,
        gate,
        own_query,
        decay,
        earlier,
        fall,
        gate_gain,
        w_out_two,
        out_fixed=False,
    )
    return out


def solution(mesh):
    in_specs = (
        P("tile", "curve", None),
        P("tile", "curve"),
        P("tile", "curve", None),
        P("tile", "curve", None),
    ) + (P(),) * 9
    return jax.shard_map(
        functools.partial(local, mesh.shape["tile"]),
        mesh=mesh,
        in_specs=in_specs,
        out_specs=P("tile", "curve", None),
        check_vma=False,
    )
```

```python
import functools

import jax
import jax.numpy as jnp
from jax import lax
from jax.experimental import pallas as pl
from jax.experimental.pallas import tpu as pltpu
from jax.sharding import PartitionSpec as P

F32, BF16 = jnp.float32, jnp.bfloat16
EPS = 1e-5
LOG2E = 1.4426950408889634
EXTRA = 16
VMEM_BYTES = 20 * 1024 * 1024


def dot(a, b):
    return jnp.dot(a, b, preferred_element_type=F32)


def dot_nt(a, b):
    return lax.dot_general(a, b, (((1,), (1,)), ((), ())), preferred_element_type=F32)


def turn(x):
    return x.astype(F32).T.astype(x.dtype)


def silu(x):
    half = 0.5 * x
    return half + half * jnp.tanh(half)


def split(x):
    hi = x.astype(BF16).astype(F32)
    return hi, x - hi


def normalise(x, gain):
    wide = x.astype(F32)
    return (wide * lax.rsqrt(jnp.mean(wide * wide, axis=-1, keepdims=True) + EPS) * gain).astype(BF16)


def iota(shape, axis):
    return lax.broadcasted_iota(jnp.int32, shape, axis)


def column(row):
    heads = row.shape[1]
    same = iota((heads, heads), 0) == iota((heads, heads), 1)
    return jnp.sum(jnp.where(same, row, 0.0), axis=1, keepdims=True)


def head_steps(normed, valids, w_dt_t, bias, rate):
    heads = w_dt_t.shape[0]
    rows = normed.shape[0] // len(valids)
    raw = dot_nt(w_dt_t, normed) + column(bias)
    steps = jnp.maximum(raw, 0.0) + jnp.log1p(jnp.exp(-jnp.abs(raw)))
    lane = iota((heads, rows), 1).astype(F32)
    steps = jnp.concatenate(
        [
            jnp.where(lane < valid, steps[:, c * rows : (c + 1) * rows], 0.0)
            for c, valid in enumerate(valids)
        ],
        axis=0,
    )
    falls = -steps * jnp.concatenate([column(rate) * LOG2E] * len(valids), axis=0)
    upper = jnp.where(iota((rows, rows), 0) <= iota((rows, rows), 1), 1.0, 0.0).astype(BF16)
    high, rest = split(falls)
    middle, low = split(rest)
    running = (
        dot(high.astype(BF16), upper) + dot(middle.astype(BF16), upper) + dot(low.astype(BF16), upper)
    )
    to_end = jnp.exp2(running[:, rows - 1 : rows] - running) * steps
    return steps, to_end, running


def by_rows(to_end, running):
    parts = [*split(to_end), *split(jnp.exp2(running)), running]
    used = len(parts) * running.shape[0]
    stack = jnp.concatenate(parts + [jnp.zeros((128 - used, running.shape[1]), F32)], axis=0)
    return stack.T


def seen_from(steps, running):
    return running - jnp.where(steps > 0.0, jnp.log2(jnp.maximum(steps, 1e-37)), -1e30)


def inside_pair(turned, seen, scores, value, head, heads):
    rows = turned.shape[0]
    at = 4 * heads + head
    weights = [
        (jnp.exp2(jnp.minimum(turned[:, at + k : at + k + 1] - seen[head + k : head + k + 1], 120.0)) * scores).astype(BF16)
        for k in range(2)
    ]
    left = iota((rows, 128), 1) < 64
    zero = jnp.zeros_like(value)
    both = jnp.concatenate([jnp.where(left, value, zero), jnp.where(left, zero, value)], axis=0)
    return dot(jnp.concatenate(weights, axis=1), both)


def masked_scores(query, key):
    rows = query.shape[0]
    return jnp.where(iota((rows, rows), 0) >= iota((rows, rows), 1), dot_nt(query, key), 0.0)


def make_spread(spread, heads):
    inner = spread.shape[1] // 2
    head = lax.shift_right_logical(iota((128, inner), 1), (inner // heads).bit_length() - 1)
    row = iota((128, inner), 0)
    for g in range(2):
        hit = (row == head + 2 * heads * g) | (row == head + 2 * heads * g + heads)
        spread[:, g * inner : (g + 1) * inner] = jnp.where(hit, 1.0, 0.0).astype(BF16)


def make_skip(skip_g, skip):
    layers, heads = skip_g.shape
    inner = skip.shape[1]
    head = lax.shift_right_logical(iota((heads, inner), 1), (inner // heads).bit_length() - 1)
    ones = jnp.where(head == iota((heads, inner), 0), 1.0, 0.0)
    for layer in range(layers):
        wide = jnp.broadcast_to(skip_g[layer : layer + 1, :], (8, heads))
        skip[8 * layer : 8 * layer + 8, :] = jnp.dot(
            wide, ones, preferred_element_type=F32, precision=lax.Precision.HIGHEST
        )


def pack_kernel(count, x, valid, shard, slot, *refs):
    sources, out, held, sems = refs[:count], refs[count], refs[count + 1 : -1], refs[-1]
    rows, width = x.shape[1:]
    copies = [pltpu.make_async_copy(x.at[0], out.at[pl.ds(0, rows)], sems.at[count])]
    copies += [pltpu.make_async_copy(a, b, sems.at[i]) for i, (a, b) in enumerate(zip(sources, held))]
    for copy in copies:
        copy.start()
    line, lane = iota((EXTRA, width), 0), iota((EXTRA, width), 1)
    count = valid[0, 0].astype(F32)
    place = (shard[0, 0, 0] + slot[0, 0, 0]).astype(F32)
    first = jnp.where(lane == 0, count, jnp.where(lane == 1, place, 0.0))
    out[rows:] = jnp.where(line == 0, first, 0.0).astype(BF16)
    for copy in copies:
        copy.wait()


def live_count(packed):
    at = packed.shape[0] - EXTRA
    return packed[at:, :128].astype(F32)[0:1, 0:1]


def place_of(packed):
    extra = packed[packed.shape[0] - EXTRA :, :128].astype(F32)
    hit = (iota((EXTRA, 128), 0) == 0) & (iota((EXTRA, 128), 1) == 1)
    return jnp.sum(jnp.where(hit, extra, 0.0)).astype(jnp.int32)


def block_of(packed):
    return packed[: packed.shape[0] - EXTRA]


def pieces_work(xs, valids, slots, params, work, ready=lambda: None):
    norm_g, w_xz, w_bc, w_dt, bias, rate, spread, skip = params
    gates, local, decay, grown, queries = work
    rows = xs[0].shape[0]
    heads, inner, key_width = w_dt.shape[1], w_xz.shape[1] // 2, w_bc.shape[2] // 2
    normed = normalise(jnp.concatenate(xs, axis=0), norm_g[0:1, :])
    bc = silu(dot(normed, w_bc[0])).astype(BF16)
    steps, to_end, running = head_steps(normed, valids, w_dt[0], bias[0:1, :], rate[0:1, :])
    seen = seen_from(steps, running)
    parts = []
    for i, slot in enumerate(slots):
        at, of = slice(i * rows, (i + 1) * rows), slice(i * heads, (i + 1) * heads)
        key, query = bc[at, :key_width], bc[at, key_width:]
        queries[slot] = query
        turned = by_rows(to_end[of], running[of])
        parts.append((slot, at, turned, turned.astype(BF16), seen[of], masked_scores(query, key), turn(key)))
    ready()
    for j in range(0, inner, 256):
        cols, ends = slice(j, j + 256), slice(inner + j, inner + j + 256)
        values = silu(dot(normed, w_xz[:, cols])).astype(BF16)
        gate = silu(dot(normed, w_xz[:, ends]))
        for slot, at, turned, lhs, seen_here, scores, key_t in parts:
            value = values[at]
            wide = value.astype(F32)
            gates[slot, :, cols] = gate[at]
            decay[slot, :, cols] = dot(lhs, spread[:, ends])
            grown[slot, :, cols] = dot(key_t, (wide * dot(lhs, spread[:, cols])).astype(BF16))
            base = skip[0:1, cols] * wide
            for k in range(2):
                half = slice(128 * k, 128 * k + 128)
                head = (j + 128 * k) * heads // inner
                local[slot, :, j + 128 * k : j + 128 * k + 128] = (
                    inside_pair(turned, seen_here, scores, value[:, half], head, heads) + base[:, half]
                )


def begin_kernel(packed, norm_g, w_bc, w_dt, bias, rate, skip_g, w_xz, w_held, spread, skip, *refs):
    work, sem = refs[:-1], refs[-1]
    copy = pltpu.make_async_copy(w_xz.at[0], w_held, sem)
    copy.start()
    make_spread(spread, w_dt.shape[1])
    make_skip(skip_g, skip)
    params = (norm_g, w_held, w_bc, w_dt, bias, rate, spread, skip)
    pieces_work([block_of(packed)], [live_count(packed)], [0], params, work, copy.wait)


def sibling_kernel(packed, late, *refs):
    pieces_work([block_of(packed)], [live_count(packed)], [1], refs[:8], refs[-5:])


def relay_kernel(x, *refs):
    refs[-1][...] = x[...]


def tile_kernel(n, *refs):
    pieces, refs = refs[:n], refs[n:]
    norm_g, w_held, w_bc, w_dt, bias, rate, spread, skip, gate_g, w_xz, w_out = refs[:11]
    refs = refs[16:]
    work, refs = refs[:5], refs[5:]
    (
        w_two,
        w_out_two,
        send,
        own_x,
        own_live,
        normed_two,
        key_two,
        own_query,
        to_end_two,
        running_two,
        seen_two,
        w_out_one,
        scaled,
        scales,
        x_two,
        valid_two,
        state,
        sems,
    ) = refs
    gates, local, decay, grown, queries = work
    me = lax.axis_index("curve")
    rows, width = x_two.shape[1:]
    heads = w_dt.shape[1]
    inner = w_out.shape[1]
    key_width = w_bc.shape[2] // 2
    part = inner // n
    copies = [
        pltpu.make_async_copy(w_out.at[0], w_out_one, sems.at[0]),
        pltpu.make_async_copy(w_xz.at[1], w_two, sems.at[1]),
        pltpu.make_async_copy(w_out.at[1], w_out_two, sems.at[2]),
    ]
    for copy in copies:
        copy.start()
    valid = [live_count(piece) for piece in pieces]
    dest = [place_of(piece) for piece in pieces]
    for k in range(n):
        valid_two[dest[k]] = jnp.broadcast_to(valid[k], (8, 128))
    xs = [block_of(piece) for piece in pieces]
    params = (norm_g, w_held, w_bc, w_dt, bias, rate, spread, skip)
    pieces_work(xs[2:], valid[2:], list(range(2, n)), params, work)

    for c in range(n):
        k = me ^ c
        query = queries[k]
        squares = jnp.zeros((rows, 1), F32)
        for j in range(0, inner, 256):
            at = slice(j, j + 256)
            out = local[k, :, at]
            if c:
                old = state[:, at]
                out += dot(query, old.astype(BF16)) * decay[k, :, at]
                state[:, at] = old * decay[k, rows - 1 :, at] + grown[k, :, at]
            else:
                state[:, at] = grown[k, :, at]
            gated = out * gates[k, :, at]
            scaled[k, :, at] = (gated * gate_g[0:1, at]).astype(BF16)
            squares += jnp.sum(gated * gated, axis=-1, keepdims=True)
        scale = lax.rsqrt(squares * (1.0 / inner) + EPS)
        scales[k] = jnp.broadcast_to(scale, (rows, 128))
    copies[0].wait()
    flat = dot(scaled[...].reshape(n * rows, inner), w_out_one[...])
    row = iota((rows, 128), 0).astype(F32)
    for k in range(n):
        factor = jnp.where(row < valid[k], scales[k], 0.0)
        for j in range(0, width, 128):
            at = slice(j, j + 128)
            update = flat[k * rows : (k + 1) * rows, at] * factor
            x_two[dest[k], :, at] = (xs[k][:, at].astype(F32) + update).astype(BF16)

    own_x[...] = x_two[me]
    own_live[...] = jnp.where(row < valid_two[me][0:1], 1.0, 0.0)
    normed = normalise(x_two[...].reshape(n * rows, width), norm_g[1:2, :])
    steps, to_end, running = head_steps(
        normed, [valid_two[c][0:1, 0:1] for c in range(n)], w_dt[1], bias[1:2, :], rate[1:2, :]
    )
    bc = silu(dot(normed, w_bc[1])).astype(BF16)
    copies[1].wait()
    at = pl.ds(pl.multiple_of(me * part, 128), part)
    value = silu(dot(normed, w_two[:, at])).astype(BF16).astype(F32)
    after = jnp.zeros((heads, 1), F32)
    suffixes = [None] * n
    for c in reversed(range(n)):
        suffixes[c] = after
        after = after + running[c * heads : (c + 1) * heads, rows - 1 :]
    whole = jnp.broadcast_to(after, (heads, rows))
    turned = [
        by_rows(to_end[c * heads : (c + 1) * heads] * jnp.exp2(suffixes[c]), whole).astype(BF16) for c in range(n)
    ]
    to_end_x = dot(jnp.concatenate(turned, axis=0), spread[:, at])
    fall = dot(turned[0][:16], spread[:, pl.ds(pl.multiple_of(inner + me * part, 128), part)])[0:1]
    send[:key_width] = dot(turn(bc[:, :key_width]), (value * to_end_x).astype(BF16)).astype(BF16)
    send[key_width:] = decay_rows(fall)
    seen = seen_from(steps, running)
    for c in range(n):
        chunk, of = slice(c * rows, (c + 1) * rows), slice(c * heads, (c + 1) * heads)
        normed_two[c] = normed[chunk]
        key_two[c] = bc[chunk, :key_width]
        queries[c] = bc[chunk, key_width:]
        to_end_two[c] = to_end[of]
        running_two[c] = running[of]
        seen_two[c] = seen[of]
    own_query[...] = queries[me]
    copies[2].wait()


def own_kernel(
    normed_two, key_two, query, to_end_two, running_two, seen_two, spread, skip, w_xz, local, gate, decay
):
    me = lax.axis_index("curve")
    inner = local.shape[1]
    heads = seen_two.shape[1]
    normed = normed_two[me]
    turned = by_rows(to_end_two[me], running_two[me])
    seen = seen_two[me]
    lhs = turned.astype(BF16)
    scores = masked_scores(query[...], key_two[me])
    for j in range(0, inner, 256):
        at = slice(j, j + 256)
        value = silu(dot(normed, w_xz[:, at])).astype(BF16)
        gate[:, at] = silu(dot(normed, w_xz[:, inner + j : inner + j + 256]))
        decay[:, at] = dot(lhs, spread[:, inner + j : inner + j + 256])
        base = skip[8:9, at] * value.astype(F32)
        for k in range(2):
            half = slice(128 * k, 128 * k + 128)
            head = (j + 128 * k) * heads // inner
            local[:, j + 128 * k : j + 128 * k + 128] = (
                inside_pair(turned, seen, scores, value[:, half], head, heads) + base[:, half]
            )


def earlier_kernel(normed_two, key_two, to_end_two, running_two, spread, w_xz, state, fall):
    me = lax.axis_index("curve")
    inner = state.shape[1]
    rows = normed_two.shape[1]
    state[...] = jnp.zeros_like(state)
    fall[...] = jnp.ones_like(fall)

    def chunk(c, _):
        normed = normed_two[c]
        lhs = by_rows(to_end_two[c], running_two[c]).astype(BF16)
        key_t = turn(key_two[c])
        for j in range(0, inner, 256):
            at = slice(j, j + 256)
            value = silu(dot(normed, w_xz[:, at])).astype(BF16).astype(F32)
            weighted = value * dot(lhs, spread[:, at])
            end_x = dot(lhs[rows - 16 :], spread[:, inner + j : inner + j + 256])[15:16]
            state[:, at] = state[:, at] * end_x + dot(key_t, weighted.astype(BF16))
            fall[:, at] = fall[:, at] * end_x
        return 0

    lax.fori_loop(0, me, chunk, 0)


def decay_rows(fall):
    high, low = split(fall)
    lines = iota((EXTRA, fall.shape[1]), 0)
    return jnp.where(lines == 0, high, jnp.where(lines == 1, low, 0.0)).astype(BF16)


def state_and_decay(ordered, u):
    states = ordered.shape[1] - EXTRA
    tail = ordered[u, states:].astype(F32)
    return ordered[u, :states].astype(F32), tail[0:1] + tail[1:2]


def join_kernel(radix, stride, last, *refs):
    deeper = stride > 1
    parts, before = refs[:radix], refs[radix] if deeper else None
    outs, ordered = refs[radix + 1 + deeper : -1], refs[-1]
    me = lax.rem(lax.div(lax.axis_index("tile"), stride), radix)
    states, width = parts[0].shape[0] - EXTRA, parts[0].shape[1]
    for k in range(radix):
        ordered[me ^ k] = parts[k][...]
    earlier = (jnp.zeros((states, width), F32), jnp.ones((1, width), F32))
    whole = None
    for u in range(radix if not last else radix - 1):
        one, fall = state_and_decay(ordered, u)
        if u < radix - 1:
            took = jnp.where(me > u, 1.0, 0.0)
            keep = jnp.where(me > u, fall, 1.0)
            earlier = (earlier[0] * keep + one * took, earlier[1] * keep)
        if not last:
            whole = (one, fall) if u == 0 else (whole[0] * fall + one, whole[1] * fall)
    state, fall = earlier
    if deeper:
        state = state * before[states : states + 1] + before[:states]
        fall = fall * before[states : states + 1]
    if last:
        outs[0][...] = state.astype(BF16)
        return
    outs[0][:states] = state
    outs[0][states:] = jnp.broadcast_to(fall, (8, width))
    outs[1][:states] = whole[0].astype(BF16)
    outs[1][states:] = decay_rows(whole[1])


def end_kernel(n, *refs):
    pieces = refs[:n]
    x, live, local, gate, query, decay, earlier, fall, gate_g, w_out, out = refs[n:]
    me = lax.axis_index("curve")
    rows, inner = local.shape
    part = inner // n
    squares = jnp.zeros((rows, 1), F32)
    update = None
    for k in range(n):
        at = pl.ds(pl.multiple_of((me ^ k) * part, 128), part)
        state = pieces[k][...].astype(F32) * fall[0:1, at] + earlier[:, at]
        head_out = dot(query[...], state.astype(BF16)) * decay[:, at] + local[:, at]
        gated = head_out * gate[:, at]
        squares += jnp.sum(gated * gated, axis=-1, keepdims=True)
        of_part = dot((gated * gate_g[1:2, at]).astype(BF16), w_out[at, :])
        update = of_part if update is None else update + of_part
    scale = lax.rsqrt(squares * (1.0 / inner) + EPS)
    factor = live[...] * jnp.broadcast_to(scale, live.shape)
    for j in range(0, x.shape[1], 128):
        at = slice(j, j + 128)
        out[0, :, at] = (x[:, at].astype(F32) + factor * update[:, at]).astype(BF16)


def call(kernel, outs, scratch, *args, in_hbm=(), free=(), aliases={}, out_fixed=True):
    vmem = pl.BlockSpec(memory_space=pltpu.VMEM)
    spaces = [pltpu.HBM if i in in_hbm else pltpu.VMEM for i in range(len(args))]
    spaces = [pltpu.SMEM if i in free else space for i, space in enumerate(spaces)]
    args = [
        arg if space == pltpu.SMEM else pltpu.with_memory_space_constraint(arg, space)
        for arg, space in zip(args, spaces)
    ]
    return pl.pallas_call(
        kernel,
        out_shape=[(pltpu.VMEM if out_fixed else jax.ShapeDtypeStruct)(shape, kind) for shape, kind in outs],
        in_specs=[pl.BlockSpec(memory_space=space) for space in spaces],
        out_specs=[vmem] * len(outs),
        scratch_shapes=scratch,
        input_output_aliases=aliases,
        compiler_params=pltpu.CompilerParams(vmem_limit_bytes=VMEM_BYTES),
    )(*args)


def swap(value, axis, mask, size):
    return lax.ppermute(value, axis, [(i, i ^ mask) for i in range(size)])


def levels(size):
    steps, stride = [], 1
    while stride < size:
        radix = 4 if stride > 1 and size // stride >= 4 else 2
        steps.append((radix, stride))
        stride *= radix
    return steps


def local(
    tiles,
    points,
    valid_rows,
    dest_shard,
    dest_slot,
    norm_gain,
    w_xz,
    w_bc,
    w_dt,
    dt_bias,
    decay_rate,
    skip_gain,
    gate_gain,
    w_out,
):
    n = lax.axis_size("curve")
    rows, width = points.shape[1:]
    heads, inner, key_width = w_dt.shape[2], w_out.shape[1], w_bc.shape[2] // 2
    part = inner // n
    params = (norm_gain, w_bc, jnp.swapaxes(w_dt, 1, 2), dt_bias, decay_rate, skip_gain, gate_gain)
    packed, norm_gain, w_bc, w_dt, dt_bias, decay_rate, skip_gain, gate_gain = call(
        functools.partial(pack_kernel, len(params)),
        [((rows + EXTRA, width), BF16)] + [(p.shape, p.dtype) for p in params],
        [pltpu.SemaphoreType.DMA((len(params) + 1,))],
        points,
        valid_rows,
        dest_shard,
        dest_slot,
        *params,
        in_hbm=(0, *range(4, 4 + len(params))),
        free=(1, 2, 3),
    )
    pieces = [packed] + [None] * (n - 1)
    for k in range(2, n, 2):
        pieces[k] = swap(packed, "curve", k, n)
    pieces[1] = swap(packed, "curve", 1, n)
    work = [
        ((n, rows, inner), F32),
        ((n, rows, inner), F32),
        ((n, rows, inner), F32),
        ((n, key_width, inner), F32),
        ((n, rows, key_width), BF16),
    ]
    w_held, spread, skip, *work_done = call(
        begin_kernel,
        [(w_xz.shape[1:], BF16), ((128, 2 * inner), BF16), ((8 * skip_gain.shape[0], inner), F32)] + work,
        [pltpu.SemaphoreType.DMA],
        packed,
        norm_gain,
        w_bc,
        w_dt,
        dt_bias,
        decay_rate,
        skip_gain,
        w_xz,
        in_hbm=(7,),
    )
    for k in range(3, n, 2):
        (passed,) = call(relay_kernel, [(packed.shape, BF16)], [], pieces[k - 1], skip)
        pieces[k] = swap(passed, "curve", 1, n)
    shared = (norm_gain, w_held, w_bc, w_dt, dt_bias, decay_rate, spread, skip)
    work_done = call(
        sibling_kernel,
        work,
        [],
        pieces[1],
        pieces[2],
        *shared,
        *work_done,
        aliases={10 + i: i for i in range(5)},
    )
    first = n + 11
    got = call(
        functools.partial(tile_kernel, n),
        work
        + [
            (w_xz.shape[1:], BF16),
            (w_out.shape[1:], BF16),
            ((key_width + EXTRA, part), BF16),
            ((rows, width), BF16),
            ((rows, 128), F32),
            ((n, rows, width), BF16),
            ((n, rows, key_width), BF16),
            ((rows, key_width), BF16),
            ((n, heads, rows), F32),
            ((n, heads, rows), F32),
            ((n, heads, rows), F32),
        ],
        [
            pltpu.VMEM(w_out.shape[1:], BF16),
            pltpu.VMEM((n, rows, inner), BF16),
            pltpu.VMEM((n, rows, 128), F32),
            pltpu.VMEM((n, rows, width), BF16),
            pltpu.VMEM((n, 8, 128), F32),
            pltpu.VMEM((key_width, inner), F32),
            pltpu.SemaphoreType.DMA((3,)),
        ],
        *pieces,
        *shared,
        gate_gain,
        w_xz,
        w_out,
        *work_done,
        in_hbm=(first - 2, first - 1),
        aliases={first + i: i for i in range(5)},
    )
    w_two, w_out_two, send, own_x, own_live, normed_two, key_two, own_query = got[5:13]
    to_end_two, running_two, seen_two = got[13:]
    own, gate, decay = call(
        own_kernel,
        [((rows, inner), F32)] * 3,
        [],
        normed_two,
        key_two,
        own_query,
        to_end_two,
        running_two,
        seen_two,
        spread,
        skip,
        w_two,
    )
    earlier, fall = call(
        earlier_kernel,
        [((key_width, inner), F32), ((8, inner), F32)],
        [],
        normed_two,
        key_two,
        to_end_two,
        running_two,
        spread,
        w_two,
    )
    before = []
    steps = levels(tiles)
    for i, (radix, stride) in enumerate(steps):
        last = i == len(steps) - 1
        parts = [send] + [swap(send, "tile", k * stride, tiles) for k in range(1, radix)]
        outs = [((key_width, part), BF16)]
        if not last:
            outs = [((key_width + 8, part), F32), ((key_width + EXTRA, part), BF16)]
        got = call(
            functools.partial(join_kernel, radix, stride, last),
            outs,
            [pltpu.VMEM((radix, key_width + EXTRA, part), BF16)],
            *parts,
            *before,
            fall if last else decay,
        )
        if not last:
            before, send = [got[0]], got[1]
    incoming = got[0]
    states = [incoming] + [swap(incoming, "curve", k, n) for k in range(1, n)]
    (out,) = call(
        functools.partial(end_kernel, n),
        [((1, rows, width), BF16)],
        [],
        *states,
        own_x,
        own_live,
        own,
        gate,
        own_query,
        decay,
        earlier,
        fall,
        gate_gain,
        w_out_two,
        out_fixed=False,
    )
    return out


def solution(mesh):
    in_specs = (
        P("tile", "curve", None),
        P("tile", "curve"),
        P("tile", "curve", None),
        P("tile", "curve", None),
    ) + (P(),) * 9
    return jax.shard_map(
        functools.partial(local, mesh.shape["tile"]),
        mesh=mesh,
        in_specs=in_specs,
        out_specs=P("tile", "curve", None),
        check_vma=False,
    )
```

```python
import functools

import jax
import jax.numpy as jnp
from jax import lax
from jax.experimental import pallas as pl
from jax.experimental.pallas import tpu as pltpu
from jax.sharding import PartitionSpec as P

F32, BF16 = jnp.float32, jnp.bfloat16
EPS = 1e-5
LOG2E = 1.4426950408889634
EXTRA = 16
VMEM_BYTES = 20 * 1024 * 1024


def dot(a, b):
    return jnp.dot(a, b, preferred_element_type=F32)


def dot_nt(a, b):
    return lax.dot_general(a, b, (((1,), (1,)), ((), ())), preferred_element_type=F32)


def turn(x):
    return x.astype(F32).T.astype(x.dtype)


def silu(x):
    half = 0.5 * x
    return half + half * jnp.tanh(half)


def split(x):
    hi = x.astype(BF16).astype(F32)
    return hi, x - hi


def normalise(x, gain):
    wide = x.astype(F32)
    return (wide * lax.rsqrt(jnp.mean(wide * wide, axis=-1, keepdims=True) + EPS) * gain).astype(BF16)


def iota(shape, axis):
    return lax.broadcasted_iota(jnp.int32, shape, axis)


def column(row):
    heads = row.shape[1]
    same = iota((heads, heads), 0) == iota((heads, heads), 1)
    return jnp.sum(jnp.where(same, row, 0.0), axis=1, keepdims=True)


def head_steps(normed, valids, w_dt_t, bias, rate):
    heads = w_dt_t.shape[0]
    rows = normed.shape[0] // len(valids)
    raw = dot_nt(w_dt_t, normed) + column(bias)
    steps = jnp.maximum(raw, 0.0) + jnp.log1p(jnp.exp(-jnp.abs(raw)))
    lane = iota((heads, rows), 1).astype(F32)
    steps = jnp.concatenate(
        [
            jnp.where(lane < valid, steps[:, c * rows : (c + 1) * rows], 0.0)
            for c, valid in enumerate(valids)
        ],
        axis=0,
    )
    falls = -steps * jnp.concatenate([column(rate) * LOG2E] * len(valids), axis=0)
    upper = jnp.where(iota((rows, rows), 0) <= iota((rows, rows), 1), 1.0, 0.0).astype(BF16)
    high, rest = split(falls)
    middle, low = split(rest)
    running = (
        dot(high.astype(BF16), upper) + dot(middle.astype(BF16), upper) + dot(low.astype(BF16), upper)
    )
    to_end = jnp.exp2(running[:, rows - 1 : rows] - running) * steps
    return steps, to_end, running


def by_rows(to_end, running):
    high, rest = split(running)
    parts = [*split(to_end), *split(jnp.exp2(running)), high, *split(rest)]
    used = len(parts) * running.shape[0]
    stack = jnp.concatenate(parts + [jnp.zeros((128 - used, running.shape[1]), F32)], axis=0)
    return stack.T.astype(BF16)


def seen_from(steps, running):
    return running - jnp.where(steps > 0.0, jnp.log2(jnp.maximum(steps, 1e-37)), -1e30)


def inside_pair(lhs, spread, seen, scores, value, head):
    rows = lhs.shape[0]
    heads = seen.shape[0]
    at = spread.shape[1] - (heads - head) * 128
    run = dot(lhs, spread[:, at : at + 256])
    row = jnp.concatenate([seen[head : head + 1], seen[head + 1 : head + 2]], axis=1)
    weights = jnp.exp2(jnp.minimum(run - row, 120.0)) * scores
    left = iota((rows, 128), 1) < 64
    zero = jnp.zeros_like(value)
    both = jnp.concatenate([jnp.where(left, value, zero), jnp.where(left, zero, value)], axis=0)
    return dot(weights.astype(BF16), both)


def masked_scores(query, key):
    rows = query.shape[0]
    scores = jnp.where(iota((rows, rows), 0) >= iota((rows, rows), 1), dot_nt(query, key), 0.0)
    return jnp.concatenate([scores, scores], axis=1)


def make_spread(spread, heads, inner):
    head = lax.shift_right_logical(iota((128, inner), 1), (inner // heads).bit_length() - 1)
    row = iota((128, inner), 0)
    for g in range(2):
        hit = (row == head + 2 * heads * g) | (row == head + 2 * heads * g + heads)
        spread[:, g * inner : (g + 1) * inner] = jnp.where(hit, 1.0, 0.0).astype(BF16)
    row = iota((128, 128), 0) - 4 * heads
    for h in range(heads):
        hit = (row == h) | (row == h + heads) | (row == h + 2 * heads)
        spread[:, 2 * inner + 128 * h : 2 * inner + 128 * h + 128] = jnp.where(hit, 1.0, 0.0).astype(BF16)


def make_skip(skip_g, skip):
    layers, heads = skip_g.shape
    inner = skip.shape[1]
    head = lax.shift_right_logical(iota((heads, inner), 1), (inner // heads).bit_length() - 1)
    ones = jnp.where(head == iota((heads, inner), 0), 1.0, 0.0)
    for layer in range(layers):
        wide = jnp.broadcast_to(skip_g[layer : layer + 1, :], (8, heads))
        skip[8 * layer : 8 * layer + 8, :] = jnp.dot(
            wide, ones, preferred_element_type=F32, precision=lax.Precision.HIGHEST
        )


def pack_kernel(count, heads, inner, x, valid, shard, slot, *refs):
    sources, out, spread, held, sems = refs[:count], refs[count], refs[count + 1], refs[count + 2 : -1], refs[-1]
    rows, width = x.shape[1:]
    copies = [pltpu.make_async_copy(x.at[0], out.at[pl.ds(0, rows)], sems.at[count])]
    copies += [pltpu.make_async_copy(a, b, sems.at[i]) for i, (a, b) in enumerate(zip(sources, held))]
    for copy in copies:
        copy.start()
    line, lane = iota((EXTRA, width), 0), iota((EXTRA, width), 1)
    count = valid[0, 0].astype(F32)
    place = (shard[0, 0, 0] + slot[0, 0, 0]).astype(F32)
    first = jnp.where(lane == 0, count, jnp.where(lane == 1, place, 0.0))
    out[rows:] = jnp.where(line == 0, first, 0.0).astype(BF16)
    make_spread(spread, heads, inner)
    for copy in copies:
        copy.wait()


def live_count(packed):
    at = packed.shape[0] - EXTRA
    return packed[at:, :128].astype(F32)[0:1, 0:1]


def place_of(packed):
    extra = packed[packed.shape[0] - EXTRA :, :128].astype(F32)
    hit = (iota((EXTRA, 128), 0) == 0) & (iota((EXTRA, 128), 1) == 1)
    return jnp.sum(jnp.where(hit, extra, 0.0)).astype(jnp.int32)


def block_of(packed):
    return packed[: packed.shape[0] - EXTRA]


def pieces_work(xs, valids, slots, params, work, ready=lambda j: None):
    norm_g, w_xz, w_bc, w_dt, bias, rate, spread, skip = params
    gates, local, decay, grown, queries = work
    rows = xs[0].shape[0]
    heads, inner, key_width = w_dt.shape[1], w_xz.shape[1] // 2, w_bc.shape[2] // 2
    normed = normalise(jnp.concatenate(xs, axis=0), norm_g[0:1, :])
    bc = silu(dot(normed, w_bc[0])).astype(BF16)
    steps, to_end, running = head_steps(normed, valids, w_dt[0], bias[0:1, :], rate[0:1, :])
    seen = seen_from(steps, running)
    parts = []
    for i, slot in enumerate(slots):
        at, of = slice(i * rows, (i + 1) * rows), slice(i * heads, (i + 1) * heads)
        key, query = bc[at, :key_width], bc[at, key_width:]
        queries[slot] = query
        parts.append((slot, at, by_rows(to_end[of], running[of]), seen[of], masked_scores(query, key), turn(key)))
    for j in range(0, inner, 256):
        ready(j)
        cols, ends = slice(j, j + 256), slice(inner + j, inner + j + 256)
        values = silu(dot(normed, w_xz[:, cols])).astype(BF16)
        gate = silu(dot(normed, w_xz[:, ends]))
        for slot, at, lhs, seen_here, scores, key_t in parts:
            value = values[at]
            wide = value.astype(F32)
            gates[slot, :, cols] = gate[at]
            decay[slot, :, cols] = dot(lhs, spread[:, ends])
            grown[slot, :, cols] = dot(key_t, (wide * dot(lhs, spread[:, cols])).astype(BF16))
            base = skip[0:1, cols] * wide
            for k in range(2):
                half = slice(128 * k, 128 * k + 128)
                head = (j + 128 * k) * heads // inner
                local[slot, :, j + 128 * k : j + 128 * k + 128] = (
                    inside_pair(lhs, spread, seen_here, scores, value[:, half], head) + base[:, half]
                )


def begin_kernel(packed, norm_g, w_bc, w_dt, bias, rate, skip_g, spread, w_xz, w_held, skip, *refs):
    work, sems = refs[:-1], refs[-1]
    inner = skip.shape[1]
    copies = {}
    for i, j in enumerate(range(0, inner, 256)):
        copies[j] = []
        for g in range(2):
            at = pl.ds(g * inner + j, 256)
            copies[j].append(pltpu.make_async_copy(w_xz.at[0, :, at], w_held.at[:, at], sems.at[2 * i + g]))
            copies[j][-1].start()

    def ready(j):
        for copy in copies[j]:
            copy.wait()

    make_skip(skip_g, skip)
    params = (norm_g, w_held, w_bc, w_dt, bias, rate, spread, skip)
    pieces_work([block_of(packed)], [live_count(packed)], [0], params, work, ready)


def sibling_kernel(packed, late, *refs):
    pieces_work([block_of(packed)], [live_count(packed)], [1], refs[:8], refs[-5:])


def relay_kernel(x, *refs):
    refs[-1][...] = x[...]


def tile_kernel(n, *refs):
    pieces, refs = refs[:n], refs[n:]
    norm_g, w_held, w_bc, w_dt, bias, rate, spread, skip, gate_g, w_xz, w_out = refs[:11]
    refs = refs[16:]
    work, refs = refs[:5], refs[5:]
    (
        w_two,
        w_out_two,
        send,
        own_x,
        own_live,
        normed_two,
        key_two,
        own_query,
        to_end_two,
        running_two,
        seen_two,
        w_out_one,
        scaled,
        scales,
        x_two,
        valid_two,
        state,
        sems,
    ) = refs
    gates, local, decay, grown, queries = work
    me = lax.axis_index("curve")
    rows, width = x_two.shape[1:]
    heads = w_dt.shape[1]
    inner = w_out.shape[1]
    key_width = w_bc.shape[2] // 2
    part = inner // n
    copies = [
        pltpu.make_async_copy(w_out.at[0], w_out_one, sems.at[0]),
        pltpu.make_async_copy(w_xz.at[1], w_two, sems.at[1]),
        pltpu.make_async_copy(w_out.at[1], w_out_two, sems.at[2]),
    ]
    for copy in copies:
        copy.start()
    valid = [live_count(piece) for piece in pieces]
    dest = [place_of(piece) for piece in pieces]
    for k in range(n):
        valid_two[dest[k]] = jnp.broadcast_to(valid[k], (8, 128))
    xs = [block_of(piece) for piece in pieces]
    params = (norm_g, w_held, w_bc, w_dt, bias, rate, spread, skip)
    pieces_work(xs[2:], valid[2:], list(range(2, n)), params, work)

    for c in range(n):
        k = me ^ c
        query = queries[k]
        squares = jnp.zeros((rows, 1), F32)
        for j in range(0, inner, 256):
            at = slice(j, j + 256)
            out = local[k, :, at]
            if c:
                old = state[:, at]
                out += dot(query, old.astype(BF16)) * decay[k, :, at]
                state[:, at] = old * decay[k, rows - 1 :, at] + grown[k, :, at]
            else:
                state[:, at] = grown[k, :, at]
            gated = out * gates[k, :, at]
            scaled[k, :, at] = (gated * gate_g[0:1, at]).astype(BF16)
            squares += jnp.sum(gated * gated, axis=-1, keepdims=True)
        scale = lax.rsqrt(squares * (1.0 / inner) + EPS)
        scales[k] = jnp.broadcast_to(scale, (rows, 128))
    copies[0].wait()
    flat = dot(scaled[...].reshape(n * rows, inner), w_out_one[...])
    row = iota((rows, 128), 0).astype(F32)
    for k in range(n):
        factor = jnp.where(row < valid[k], scales[k], 0.0)
        for j in range(0, width, 128):
            at = slice(j, j + 128)
            update = flat[k * rows : (k + 1) * rows, at] * factor
            x_two[dest[k], :, at] = (xs[k][:, at].astype(F32) + update).astype(BF16)

    own_x[...] = x_two[me]
    own_live[...] = jnp.where(row < valid_two[me][0:1], 1.0, 0.0)
    normed = normalise(x_two[...].reshape(n * rows, width), norm_g[1:2, :])
    steps, to_end, running = head_steps(
        normed, [valid_two[c][0:1, 0:1] for c in range(n)], w_dt[1], bias[1:2, :], rate[1:2, :]
    )
    bc = silu(dot(normed, w_bc[1])).astype(BF16)
    copies[1].wait()
    at = pl.ds(pl.multiple_of(me * part, 128), part)
    value = silu(dot(normed, w_two[:, at])).astype(BF16).astype(F32)
    after = jnp.zeros((heads, 1), F32)
    suffixes = [None] * n
    for c in reversed(range(n)):
        suffixes[c] = after
        after = after + running[c * heads : (c + 1) * heads, rows - 1 :]
    whole = jnp.broadcast_to(after, (heads, rows))
    turned = [
        by_rows(to_end[c * heads : (c + 1) * heads] * jnp.exp2(suffixes[c]), whole) for c in range(n)
    ]
    to_end_x = dot(jnp.concatenate(turned, axis=0), spread[:, at])
    fall = dot(turned[0][:16], spread[:, pl.ds(pl.multiple_of(inner + me * part, 128), part)])[0:1]
    send[:key_width] = dot(turn(bc[:, :key_width]), (value * to_end_x).astype(BF16)).astype(BF16)
    send[key_width:] = decay_rows(fall)
    seen = seen_from(steps, running)
    for c in range(n):
        chunk, of = slice(c * rows, (c + 1) * rows), slice(c * heads, (c + 1) * heads)
        normed_two[c] = normed[chunk]
        key_two[c] = bc[chunk, :key_width]
        queries[c] = bc[chunk, key_width:]
        to_end_two[c] = to_end[of]
        running_two[c] = running[of]
        seen_two[c] = seen[of]
    own_query[...] = queries[me]
    copies[2].wait()


def own_kernel(
    normed_two, key_two, query, to_end_two, running_two, seen_two, spread, skip, w_xz, local, gate, decay
):
    me = lax.axis_index("curve")
    inner = local.shape[1]
    heads = seen_two.shape[1]
    normed = normed_two[me]
    lhs = by_rows(to_end_two[me], running_two[me])
    seen = seen_two[me]
    scores = masked_scores(query[...], key_two[me])
    for j in range(0, inner, 256):
        at = slice(j, j + 256)
        value = silu(dot(normed, w_xz[:, at])).astype(BF16)
        gate[:, at] = silu(dot(normed, w_xz[:, inner + j : inner + j + 256]))
        decay[:, at] = dot(lhs, spread[:, inner + j : inner + j + 256])
        base = skip[8:9, at] * value.astype(F32)
        for k in range(2):
            half = slice(128 * k, 128 * k + 128)
            head = (j + 128 * k) * heads // inner
            local[:, j + 128 * k : j + 128 * k + 128] = (
                inside_pair(lhs, spread, seen, scores, value[:, half], head) + base[:, half]
            )


def earlier_kernel(normed_two, key_two, to_end_two, running_two, spread, w_xz, state, fall):
    me = lax.axis_index("curve")
    inner = state.shape[1]
    rows = normed_two.shape[1]
    state[...] = jnp.zeros_like(state)
    fall[...] = jnp.ones_like(fall)

    def chunk(c, _):
        normed = normed_two[c]
        lhs = by_rows(to_end_two[c], running_two[c])
        key_t = turn(key_two[c])
        for j in range(0, inner, 256):
            at = slice(j, j + 256)
            value = silu(dot(normed, w_xz[:, at])).astype(BF16).astype(F32)
            weighted = value * dot(lhs, spread[:, at])
            end_x = dot(lhs[rows - 16 :], spread[:, inner + j : inner + j + 256])[15:16]
            state[:, at] = state[:, at] * end_x + dot(key_t, weighted.astype(BF16))
            fall[:, at] = fall[:, at] * end_x
        return 0

    lax.fori_loop(0, me, chunk, 0)


def decay_rows(fall):
    high, low = split(fall)
    lines = iota((EXTRA, fall.shape[1]), 0)
    return jnp.where(lines == 0, high, jnp.where(lines == 1, low, 0.0)).astype(BF16)


def state_and_decay(ordered, u):
    states = ordered.shape[1] - EXTRA
    tail = ordered[u, states:].astype(F32)
    return ordered[u, :states].astype(F32), tail[0:1] + tail[1:2]


def join_kernel(radix, stride, last, *refs):
    deeper = stride > 1
    parts, before = refs[:radix], refs[radix] if deeper else None
    outs, ordered = refs[radix + 1 + deeper : -1], refs[-1]
    me = lax.rem(lax.div(lax.axis_index("tile"), stride), radix)
    states, width = parts[0].shape[0] - EXTRA, parts[0].shape[1]
    for k in range(radix):
        ordered[me ^ k] = parts[k][...]
    earlier = (jnp.zeros((states, width), F32), jnp.ones((1, width), F32))
    whole = None
    for u in range(radix if not last else radix - 1):
        one, fall = state_and_decay(ordered, u)
        if u < radix - 1:
            took = jnp.where(me > u, 1.0, 0.0)
            keep = jnp.where(me > u, fall, 1.0)
            earlier = (earlier[0] * keep + one * took, earlier[1] * keep)
        if not last:
            whole = (one, fall) if u == 0 else (whole[0] * fall + one, whole[1] * fall)
    state, fall = earlier
    if deeper:
        state = state * before[states : states + 1] + before[:states]
        fall = fall * before[states : states + 1]
    if last:
        outs[0][...] = state.astype(BF16)
        return
    outs[0][:states] = state
    outs[0][states:] = jnp.broadcast_to(fall, (8, width))
    outs[1][:states] = whole[0].astype(BF16)
    outs[1][states:] = decay_rows(whole[1])


def end_kernel(ks, final, *refs):
    pieces, refs = refs[: len(ks)], refs[len(ks) :]
    local, gate, query, decay, earlier, fall, gate_g, w_out = refs[:8]
    me = lax.axis_index("curve")
    rows, inner = local.shape
    part = pieces[0].shape[1]
    squares = jnp.zeros((rows, 1), F32)
    update = None
    for k, piece in zip(ks, pieces):
        at = pl.ds(pl.multiple_of((me ^ k) * part, 128), part)
        state = piece[...].astype(F32) * fall[0:1, at] + earlier[:, at]
        head_out = dot(query[...], state.astype(BF16)) * decay[:, at] + local[:, at]
        gated = head_out * gate[:, at]
        squares += jnp.sum(gated * gated, axis=-1, keepdims=True)
        of_part = dot((gated * gate_g[1:2, at]).astype(BF16), w_out[at, :])
        update = of_part if update is None else update + of_part
    if not final:
        update_out, squares_out = refs[8:]
        update_out[...] = update
        squares_out[...] = jnp.broadcast_to(squares, squares_out.shape)
        return
    x, live, update_in, squares_in, out = refs[8:]
    squares = jnp.broadcast_to(squares, live.shape) + squares_in[...]
    factor = live[...] * lax.rsqrt(squares * (1.0 / inner) + EPS)
    for j in range(0, x.shape[1], 128):
        at = slice(j, j + 128)
        total = update[:, at] + update_in[:, at]
        out[0, :, at] = (x[:, at].astype(F32) + factor * total).astype(BF16)


def call(kernel, outs, scratch, *args, in_hbm=(), free=(), aliases={}, out_fixed=True):
    vmem = pl.BlockSpec(memory_space=pltpu.VMEM)
    spaces = [pltpu.HBM if i in in_hbm else pltpu.VMEM for i in range(len(args))]
    spaces = [pltpu.SMEM if i in free else space for i, space in enumerate(spaces)]
    args = [
        arg if space == pltpu.SMEM else pltpu.with_memory_space_constraint(arg, space)
        for arg, space in zip(args, spaces)
    ]
    return pl.pallas_call(
        kernel,
        out_shape=[(pltpu.VMEM if out_fixed else jax.ShapeDtypeStruct)(shape, kind) for shape, kind in outs],
        in_specs=[pl.BlockSpec(memory_space=space) for space in spaces],
        out_specs=[vmem] * len(outs),
        scratch_shapes=scratch,
        input_output_aliases=aliases,
        compiler_params=pltpu.CompilerParams(vmem_limit_bytes=VMEM_BYTES),
    )(*args)


def swap(value, axis, mask, size, up_only=False):
    pairs = [(i, i ^ mask) for i in range(size)]
    return lax.ppermute(value, axis, [(i, j) for i, j in pairs if i < j or not up_only])


def levels(size):
    steps, stride = [], 1
    while stride < size:
        radix = 4 if stride > 1 and size // stride >= 4 else 2
        steps.append((radix, stride))
        stride *= radix
    return steps


def local(
    tiles,
    points,
    valid_rows,
    dest_shard,
    dest_slot,
    norm_gain,
    w_xz,
    w_bc,
    w_dt,
    dt_bias,
    decay_rate,
    skip_gain,
    gate_gain,
    w_out,
):
    n = lax.axis_size("curve")
    rows, width = points.shape[1:]
    heads, inner, key_width = w_dt.shape[2], w_out.shape[1], w_bc.shape[2] // 2
    part = inner // n
    params = (norm_gain, w_bc, jnp.swapaxes(w_dt, 1, 2), dt_bias, decay_rate, skip_gain, gate_gain)
    packed, spread, norm_gain, w_bc, w_dt, dt_bias, decay_rate, skip_gain, gate_gain = call(
        functools.partial(pack_kernel, len(params), heads, inner),
        [((rows + EXTRA, width), BF16), ((128, 2 * inner + 128 * heads), BF16)] + [(p.shape, p.dtype) for p in params],
        [pltpu.SemaphoreType.DMA((len(params) + 1,))],
        points,
        valid_rows,
        dest_shard,
        dest_slot,
        *params,
        in_hbm=(0, *range(4, 4 + len(params))),
        free=(1, 2, 3),
    )
    pieces = [packed] + [None] * (n - 1)
    for k in range(2, n, 2):
        pieces[k] = swap(packed, "curve", k, n)
    pieces[1] = swap(packed, "curve", 1, n)
    work = [
        ((n, rows, inner), F32),
        ((n, rows, inner), F32),
        ((n, rows, inner), F32),
        ((n, key_width, inner), F32),
        ((n, rows, key_width), BF16),
    ]
    w_held, skip, *work_done = call(
        begin_kernel,
        [(w_xz.shape[1:], BF16), ((8 * skip_gain.shape[0], inner), F32)] + work,
        [pltpu.SemaphoreType.DMA((2 * inner // 256,))],
        packed,
        norm_gain,
        w_bc,
        w_dt,
        dt_bias,
        decay_rate,
        skip_gain,
        spread,
        w_xz,
        in_hbm=(8,),
    )
    for k in range(3, n, 2):
        (passed,) = call(relay_kernel, [(packed.shape, BF16)], [], pieces[k - 1], skip)
        pieces[k] = swap(passed, "curve", 1, n)
    shared = (norm_gain, w_held, w_bc, w_dt, dt_bias, decay_rate, spread, skip)
    work_done = call(
        sibling_kernel,
        work,
        [],
        pieces[1],
        pieces[2],
        *shared,
        *work_done,
        aliases={10 + i: i for i in range(5)},
    )
    first = n + 11
    got = call(
        functools.partial(tile_kernel, n),
        work
        + [
            (w_xz.shape[1:], BF16),
            (w_out.shape[1:], BF16),
            ((key_width + EXTRA, part), BF16),
            ((rows, width), BF16),
            ((rows, 128), F32),
            ((n, rows, width), BF16),
            ((n, rows, key_width), BF16),
            ((rows, key_width), BF16),
            ((n, heads, rows), F32),
            ((n, heads, rows), F32),
            ((n, heads, rows), F32),
        ],
        [
            pltpu.VMEM(w_out.shape[1:], BF16),
            pltpu.VMEM((n, rows, inner), BF16),
            pltpu.VMEM((n, rows, 128), F32),
            pltpu.VMEM((n, rows, width), BF16),
            pltpu.VMEM((n, 8, 128), F32),
            pltpu.VMEM((key_width, inner), F32),
            pltpu.SemaphoreType.DMA((3,)),
        ],
        *pieces,
        *shared,
        gate_gain,
        w_xz,
        w_out,
        *work_done,
        in_hbm=(first - 2, first - 1),
        aliases={first + i: i for i in range(5)},
    )
    w_two, w_out_two, send, own_x, own_live, normed_two, key_two, own_query = got[5:13]
    to_end_two, running_two, seen_two = got[13:]
    own, gate, decay = call(
        own_kernel,
        [((rows, inner), F32)] * 3,
        [],
        normed_two,
        key_two,
        own_query,
        to_end_two,
        running_two,
        seen_two,
        spread,
        skip,
        w_two,
    )
    earlier, fall = call(
        earlier_kernel,
        [((key_width, inner), F32), ((8, inner), F32)],
        [],
        normed_two,
        key_two,
        to_end_two,
        running_two,
        spread,
        w_two,
    )
    before = []
    steps = levels(tiles)
    for i, (radix, stride) in enumerate(steps):
        last = i == len(steps) - 1
        parts = [send] + [swap(send, "tile", k * stride, tiles, last) for k in range(1, radix)]
        outs = [((key_width, part), BF16)]
        if not last:
            outs = [((key_width + 8, part), F32), ((key_width + EXTRA, part), BF16)]
        got = call(
            functools.partial(join_kernel, radix, stride, last),
            outs,
            [pltpu.VMEM((radix, key_width + EXTRA, part), BF16)],
            *parts,
            *before,
            fall if last else decay,
        )
        if not last:
            before, send = [got[0]], got[1]
    incoming = got[0]
    states = [incoming] + [swap(incoming, "curve", k, n) for k in range(1, n)]
    common = (own, gate, own_query, decay, earlier, fall, gate_gain, w_out_two)
    partial = call(
        functools.partial(end_kernel, [0, 1], False),
        [((rows, width), F32), ((rows, 128), F32)],
        [],
        *states[:2],
        *common,
    )
    (out,) = call(
        functools.partial(end_kernel, list(range(2, n)), True),
        [((1, rows, width), BF16)],
        [],
        *states[2:],
        *common,
        own_x,
        own_live,
        *partial,
        out_fixed=False,
    )
    return out


def solution(mesh):
    in_specs = (
        P("tile", "curve", None),
        P("tile", "curve"),
        P("tile", "curve", None),
        P("tile", "curve", None),
    ) + (P(),) * 9
    return jax.shard_map(
        functools.partial(local, mesh.shape["tile"]),
        mesh=mesh,
        in_specs=in_specs,
        out_specs=P("tile", "curve", None),
        check_vma=False,
    )
```

```python
import functools

import jax
import jax.numpy as jnp
from jax import lax
from jax.experimental import pallas as pl
from jax.experimental.pallas import tpu as pltpu
from jax.sharding import PartitionSpec as P

F32, BF16 = jnp.float32, jnp.bfloat16
EPS = 1e-5
LOG2E = 1.4426950408889634
EXTRA = 16
VMEM_BYTES = 20 * 1024 * 1024


def dot(a, b):
    return jnp.dot(a, b, preferred_element_type=F32)


def dot_nt(a, b):
    return lax.dot_general(a, b, (((1,), (1,)), ((), ())), preferred_element_type=F32)


def turn(x):
    return x.astype(F32).T.astype(x.dtype)


def silu(x):
    half = 0.5 * x
    return half + half * jnp.tanh(half)


def split(x):
    hi = x.astype(BF16).astype(F32)
    return hi, x - hi


def normalise(x, gain):
    wide = x.astype(F32)
    return (wide * lax.rsqrt(jnp.mean(wide * wide, axis=-1, keepdims=True) + EPS) * gain).astype(BF16)


def iota(shape, axis):
    return lax.broadcasted_iota(jnp.int32, shape, axis)


def column(row):
    heads = row.shape[1]
    same = iota((heads, heads), 0) == iota((heads, heads), 1)
    return jnp.sum(jnp.where(same, row, 0.0), axis=1, keepdims=True)


def head_steps(normed, valids, w_dt_t, bias, rate):
    heads = w_dt_t.shape[0]
    rows = normed.shape[0] // len(valids)
    raw = dot_nt(w_dt_t, normed) + column(bias)
    steps = jnp.maximum(raw, 0.0) + jnp.log1p(jnp.exp(-jnp.abs(raw)))
    lane = iota((heads, rows), 1).astype(F32)
    steps = jnp.concatenate(
        [
            jnp.where(lane < valid, steps[:, c * rows : (c + 1) * rows], 0.0)
            for c, valid in enumerate(valids)
        ],
        axis=0,
    )
    falls = -steps * jnp.concatenate([column(rate) * LOG2E] * len(valids), axis=0)
    upper = jnp.where(iota((rows, rows), 0) <= iota((rows, rows), 1), 1.0, 0.0).astype(BF16)
    high, rest = split(falls)
    middle, low = split(rest)
    running = (
        dot(high.astype(BF16), upper) + dot(middle.astype(BF16), upper) + dot(low.astype(BF16), upper)
    )
    to_end = jnp.exp2(running[:, rows - 1 : rows] - running) * steps
    return steps, to_end, running


def by_rows(to_end, running):
    parts = [*split(to_end), *split(jnp.exp2(running)), running]
    used = len(parts) * running.shape[0]
    stack = jnp.concatenate(parts + [jnp.zeros((128 - used, running.shape[1]), F32)], axis=0)
    return stack.T


def seen_from(steps, running):
    return running - jnp.where(steps > 0.0, jnp.log2(jnp.maximum(steps, 1e-37)), -1e30)


def inside_pair(turned, seen, scores, value, head, heads):
    rows = turned.shape[0]
    at = 4 * heads + head
    weights = [
        (jnp.exp2(jnp.minimum(turned[:, at + k : at + k + 1] - seen[head + k : head + k + 1], 120.0)) * scores).astype(BF16)
        for k in range(2)
    ]
    left = iota((rows, 128), 1) < 64
    zero = jnp.zeros_like(value)
    both = jnp.concatenate([jnp.where(left, value, zero), jnp.where(left, zero, value)], axis=0)
    return dot(jnp.concatenate(weights, axis=1), both)


def masked_scores(query, key):
    rows = query.shape[0]
    return jnp.where(iota((rows, rows), 0) >= iota((rows, rows), 1), dot_nt(query, key), 0.0)


def make_spread(spread, heads):
    inner = spread.shape[1] // 2
    head = lax.shift_right_logical(iota((128, inner), 1), (inner // heads).bit_length() - 1)
    row = iota((128, inner), 0)
    for g in range(2):
        hit = (row == head + 2 * heads * g) | (row == head + 2 * heads * g + heads)
        spread[:, g * inner : (g + 1) * inner] = jnp.where(hit, 1.0, 0.0).astype(BF16)


def make_skip(skip_g, skip):
    layers, heads = skip_g.shape
    inner = skip.shape[1]
    head = lax.shift_right_logical(iota((heads, inner), 1), (inner // heads).bit_length() - 1)
    ones = jnp.where(head == iota((heads, inner), 0), 1.0, 0.0)
    for layer in range(layers):
        wide = jnp.broadcast_to(skip_g[layer : layer + 1, :], (8, heads))
        skip[8 * layer : 8 * layer + 8, :] = jnp.dot(
            wide, ones, preferred_element_type=F32, precision=lax.Precision.HIGHEST
        )


def pack_kernel(count, x, valid, shard, slot, w_xz, *refs):
    sources, (out, spread, skip, w_held), refs = refs[:count], refs[count : count + 4], refs[count + 4 :]
    held, sems = refs[:-1], refs[-1]
    rows, width = x.shape[1:]
    copies = [pltpu.make_async_copy(x.at[0], out.at[pl.ds(0, rows)], sems.at[count])]
    copies += [pltpu.make_async_copy(a, b, sems.at[i]) for i, (a, b) in enumerate(zip(sources, held))]
    copies.append(pltpu.make_async_copy(w_xz.at[0], w_held, sems.at[count + 1]))
    for copy in copies:
        copy.start()
    line, lane = iota((EXTRA, width), 0), iota((EXTRA, width), 1)
    live = valid[0, 0].astype(F32)
    place = (shard[0, 0, 0] + slot[0, 0, 0]).astype(F32)
    first = jnp.where(lane == 0, live, jnp.where(lane == 1, place, 0.0))
    out[rows:] = jnp.where(line == 0, first, 0.0).astype(BF16)
    make_spread(spread, held[5].shape[1])
    for copy in copies[:-1]:
        copy.wait()
    make_skip(held[5], skip)
    copies[-1].wait()


def live_count(packed):
    at = packed.shape[0] - EXTRA
    return packed[at:, :128].astype(F32)[0:1, 0:1]


def place_of(packed):
    extra = packed[packed.shape[0] - EXTRA :, :128].astype(F32)
    hit = (iota((EXTRA, 128), 0) == 0) & (iota((EXTRA, 128), 1) == 1)
    return jnp.sum(jnp.where(hit, extra, 0.0)).astype(jnp.int32)


def block_of(packed):
    return packed[: packed.shape[0] - EXTRA]


def pieces_work(xs, valids, slots, params, work):
    norm_g, w_xz, w_bc, w_dt, bias, rate, spread, skip = params
    gates, local, decay, grown, queries = work
    rows = xs[0].shape[0]
    heads, inner, key_width = w_dt.shape[1], w_xz.shape[1] // 2, w_bc.shape[2] // 2
    normed = normalise(jnp.concatenate(xs, axis=0), norm_g[0:1, :])
    bc = silu(dot(normed, w_bc[0])).astype(BF16)
    steps, to_end, running = head_steps(normed, valids, w_dt[0], bias[0:1, :], rate[0:1, :])
    seen = seen_from(steps, running)
    parts = []
    for i, slot in enumerate(slots):
        at, of = slice(i * rows, (i + 1) * rows), slice(i * heads, (i + 1) * heads)
        key, query = bc[at, :key_width], bc[at, key_width:]
        queries[slot] = query
        turned = by_rows(to_end[of], running[of])
        parts.append((slot, at, turned, turned.astype(BF16), seen[of], masked_scores(query, key), turn(key)))
    for j in range(0, inner, 256):
        cols, ends = slice(j, j + 256), slice(inner + j, inner + j + 256)
        values = silu(dot(normed, w_xz[:, cols])).astype(BF16)
        gate = silu(dot(normed, w_xz[:, ends]))
        for slot, at, turned, lhs, seen_here, scores, key_t in parts:
            value = values[at]
            wide = value.astype(F32)
            gates[slot, :, cols] = gate[at]
            decay[slot, :, cols] = dot(lhs, spread[:, ends])
            grown[slot, :, cols] = dot(key_t, (wide * dot(lhs, spread[:, cols])).astype(BF16))
            base = skip[0:1, cols] * wide
            for k in range(2):
                half = slice(128 * k, 128 * k + 128)
                head = (j + 128 * k) * heads // inner
                local[slot, :, j + 128 * k : j + 128 * k + 128] = (
                    inside_pair(turned, seen_here, scores, value[:, half], head, heads) + base[:, half]
                )


def own_piece_kernel(packed, *refs):
    pieces_work([block_of(packed)], [live_count(packed)], [0], refs[:8], refs[8:])


def sibling_kernel(packed, late, *refs):
    pieces_work([block_of(packed)], [live_count(packed)], [1], refs[:8], refs[-5:])


def relay_kernel(x, *refs):
    refs[-1][...] = x[...]


def tile_kernel(n, *refs):
    pieces, refs = refs[:n], refs[n:]
    norm_g, w_held, w_bc, w_dt, bias, rate, spread, skip, gate_g, w_xz, w_out = refs[:11]
    refs = refs[16:]
    work, refs = refs[:5], refs[5:]
    (
        w_two,
        w_out_two,
        send,
        own_x,
        own_live,
        normed_two,
        key_two,
        own_query,
        to_end_two,
        running_two,
        seen_two,
        w_out_one,
        x_one,
        x_two,
        valid_one,
        valid_two,
        state,
        dest,
        sems,
    ) = refs
    gates, local, decay, grown, queries = work
    me = lax.axis_index("curve")
    rows, width = x_two.shape[1:]
    heads = w_dt.shape[1]
    inner = w_out.shape[1]
    key_width = w_bc.shape[2] // 2
    part = inner // n
    copies = [
        pltpu.make_async_copy(w_out.at[0], w_out_one, sems.at[0]),
        pltpu.make_async_copy(w_xz.at[1], w_two, sems.at[1]),
        pltpu.make_async_copy(w_out.at[1], w_out_two, sems.at[2]),
    ]
    for copy in copies:
        copy.start()
    valid = [live_count(piece) for piece in pieces]
    xs = [block_of(piece) for piece in pieces]
    for k in range(n):
        x_one[k] = xs[k]
        dest[k] = place_of(pieces[k])
        valid_one[k] = jnp.broadcast_to(valid[k], (8, 128))
        valid_two[dest[k]] = jnp.broadcast_to(valid[k], (8, 128))
    params = (norm_g, w_held, w_bc, w_dt, bias, rate, spread, skip)
    pieces_work(xs[2:], valid[2:], list(range(2, n)), params, work)

    copies[0].wait()
    row = iota((rows, 128), 0).astype(F32)
    for c in range(n):
        k = me ^ c
        query = queries[k]
        squares = jnp.zeros((rows, 1), F32)
        update = None
        for j in range(0, inner, 256):
            at = slice(j, j + 256)
            out = local[k, :, at]
            if c:
                old = state[:, at]
                out += dot(query, old.astype(BF16)) * decay[k, :, at]
                if c < n - 1:
                    state[:, at] = old * decay[k, rows - 1 :, at] + grown[k, :, at]
            else:
                state[:, at] = grown[k, :, at]
            gated = out * gates[k, :, at]
            squares += jnp.sum(gated * gated, axis=-1, keepdims=True)
            of_part = dot((gated * gate_g[0:1, at]).astype(BF16), w_out_one[at, :])
            update = of_part if update is None else update + of_part
        scale = jnp.broadcast_to(lax.rsqrt(squares * (1.0 / inner) + EPS), (rows, 128))
        factor = jnp.where(row < valid_one[k][0:1], scale, 0.0)
        factor = jnp.concatenate([factor] * (width // 128), axis=1)
        new = (x_one[k].astype(F32) + update * factor).astype(BF16)
        x_two[dest[k]] = new
        normed_two[dest[k]] = normalise(new, norm_g[1:2, :])

    own_x[...] = x_two[me]
    own_live[...] = jnp.where(row < valid_two[me][0:1], 1.0, 0.0)
    normed = normed_two[...].reshape(n * rows, width)
    steps, to_end, running = head_steps(
        normed, [valid_two[c][0:1, 0:1] for c in range(n)], w_dt[1], bias[1:2, :], rate[1:2, :]
    )
    bc = silu(dot(normed, w_bc[1])).astype(BF16)
    copies[1].wait()
    at = pl.ds(pl.multiple_of(me * part, 128), part)
    value = silu(dot(normed, w_two[:, at])).astype(BF16).astype(F32)
    after = jnp.zeros((heads, 1), F32)
    suffixes = [None] * n
    for c in reversed(range(n)):
        suffixes[c] = after
        after = after + running[c * heads : (c + 1) * heads, rows - 1 :]
    whole = jnp.broadcast_to(after, (heads, rows))
    turned = [
        by_rows(to_end[c * heads : (c + 1) * heads] * jnp.exp2(suffixes[c]), whole).astype(BF16) for c in range(n)
    ]
    to_end_x = dot(jnp.concatenate(turned, axis=0), spread[:, at])
    fall = dot(turned[0][:16], spread[:, pl.ds(pl.multiple_of(inner + me * part, 128), part)])[0:1]
    send[:key_width] = dot(turn(bc[:, :key_width]), (value * to_end_x).astype(BF16)).astype(BF16)
    send[key_width:] = decay_rows(fall)
    seen = seen_from(steps, running)
    for c in range(n):
        chunk, of = slice(c * rows, (c + 1) * rows), slice(c * heads, (c + 1) * heads)
        key_two[c] = bc[chunk, :key_width]
        queries[c] = bc[chunk, key_width:]
        to_end_two[c] = to_end[of]
        running_two[c] = running[of]
        seen_two[c] = seen[of]
    own_query[...] = queries[me]
    copies[2].wait()


def own_kernel(
    normed_two, key_two, query, to_end_two, running_two, seen_two, spread, skip, w_xz, local, gate, decay
):
    me = lax.axis_index("curve")
    inner = local.shape[1]
    heads = seen_two.shape[1]
    normed = normed_two[me]
    turned = by_rows(to_end_two[me], running_two[me])
    lhs = turned.astype(BF16)
    seen = seen_two[me]
    scores = masked_scores(query[...], key_two[me])
    for j in range(0, inner, 256):
        at = slice(j, j + 256)
        value = silu(dot(normed, w_xz[:, at])).astype(BF16)
        gate[:, at] = silu(dot(normed, w_xz[:, inner + j : inner + j + 256]))
        decay[:, at] = dot(lhs, spread[:, inner + j : inner + j + 256])
        base = skip[8:9, at] * value.astype(F32)
        for k in range(2):
            half = slice(128 * k, 128 * k + 128)
            head = (j + 128 * k) * heads // inner
            local[:, j + 128 * k : j + 128 * k + 128] = (
                inside_pair(turned, seen, scores, value[:, half], head, heads) + base[:, half]
            )


def earlier_kernel(normed_two, key_two, to_end_two, running_two, spread, w_xz, state, fall):
    me = lax.axis_index("curve")
    inner = state.shape[1]
    rows = normed_two.shape[1]
    state[...] = jnp.zeros_like(state)
    fall[...] = jnp.ones_like(fall)

    def chunk(c, _):
        normed = normed_two[c]
        lhs = by_rows(to_end_two[c], running_two[c]).astype(BF16)
        key_t = turn(key_two[c])
        for j in range(0, inner, 256):
            at = slice(j, j + 256)
            value = silu(dot(normed, w_xz[:, at])).astype(BF16).astype(F32)
            weighted = value * dot(lhs, spread[:, at])
            end_x = dot(lhs[rows - 16 :], spread[:, inner + j : inner + j + 256])[15:16]
            state[:, at] = state[:, at] * end_x + dot(key_t, weighted.astype(BF16))
            fall[:, at] = fall[:, at] * end_x
        return 0

    lax.fori_loop(0, me, chunk, 0)


def decay_rows(fall):
    high, low = split(fall)
    lines = iota((EXTRA, fall.shape[1]), 0)
    return jnp.where(lines == 0, high, jnp.where(lines == 1, low, 0.0)).astype(BF16)


def state_and_decay(ordered, u):
    states = ordered.shape[1] - EXTRA
    tail = ordered[u, states:].astype(F32)
    return ordered[u, :states].astype(F32), tail[0:1] + tail[1:2]


def join_kernel(radix, stride, last, *refs):
    deeper = stride > 1
    parts, before = refs[:radix], refs[radix] if deeper else None
    outs, ordered = refs[radix + 1 + deeper : -1], refs[-1]
    me = lax.rem(lax.div(lax.axis_index("tile"), stride), radix)
    states, width = parts[0].shape[0] - EXTRA, parts[0].shape[1]
    for k in range(radix):
        ordered[me ^ k] = parts[k][...]
    earlier = (jnp.zeros((states, width), F32), jnp.ones((1, width), F32))
    whole = None
    for u in range(radix if not last else radix - 1):
        one, fall = state_and_decay(ordered, u)
        if u < radix - 1:
            took = jnp.where(me > u, 1.0, 0.0)
            keep = jnp.where(me > u, fall, 1.0)
            earlier = (earlier[0] * keep + one * took, earlier[1] * keep)
        if not last:
            whole = (one, fall) if u == 0 else (whole[0] * fall + one, whole[1] * fall)
    state, fall = earlier
    if deeper:
        state = state * before[states : states + 1] + before[:states]
        fall = fall * before[states : states + 1]
    if last:
        outs[0][...] = state.astype(BF16)
        return
    outs[0][:states] = state
    outs[0][states:] = jnp.broadcast_to(fall, (8, width))
    outs[1][:states] = whole[0].astype(BF16)
    outs[1][states:] = decay_rows(whole[1])


def end_kernel(ks, final, *refs):
    pieces, refs = refs[: len(ks)], refs[len(ks) :]
    local, gate, query, decay, earlier, fall, gate_g, w_out = refs[:8]
    me = lax.axis_index("curve")
    rows, inner = local.shape
    part = pieces[0].shape[1]
    squares = jnp.zeros((rows, 1), F32)
    update = None
    for k, piece in zip(ks, pieces):
        at = pl.ds(pl.multiple_of((me ^ k) * part, 128), part)
        state = piece[...].astype(F32) * fall[0:1, at] + earlier[:, at]
        head_out = dot(query[...], state.astype(BF16)) * decay[:, at] + local[:, at]
        gated = head_out * gate[:, at]
        squares += jnp.sum(gated * gated, axis=-1, keepdims=True)
        of_part = dot((gated * gate_g[1:2, at]).astype(BF16), w_out[at, :])
        update = of_part if update is None else update + of_part
    if not final:
        update_out, squares_out = refs[8:]
        update_out[...] = update
        squares_out[...] = jnp.broadcast_to(squares, squares_out.shape)
        return
    x, live, update_in, squares_in, out = refs[8:]
    squares = jnp.broadcast_to(squares, live.shape) + squares_in[...]
    factor = live[...] * lax.rsqrt(squares * (1.0 / inner) + EPS)
    for j in range(0, x.shape[1], 128):
        at = slice(j, j + 128)
        total = update[:, at] + update_in[:, at]
        out[0, :, at] = (x[:, at].astype(F32) + factor * total).astype(BF16)


def call(kernel, outs, scratch, *args, in_hbm=(), free=(), aliases={}, out_fixed=True):
    vmem = pl.BlockSpec(memory_space=pltpu.VMEM)
    spaces = [pltpu.HBM if i in in_hbm else pltpu.VMEM for i in range(len(args))]
    spaces = [pltpu.SMEM if i in free else space for i, space in enumerate(spaces)]
    args = [
        arg if space == pltpu.SMEM else pltpu.with_memory_space_constraint(arg, space)
        for arg, space in zip(args, spaces)
    ]
    return pl.pallas_call(
        kernel,
        out_shape=[(pltpu.VMEM if out_fixed else jax.ShapeDtypeStruct)(shape, kind) for shape, kind in outs],
        in_specs=[pl.BlockSpec(memory_space=space) for space in spaces],
        out_specs=[vmem] * len(outs),
        scratch_shapes=scratch,
        input_output_aliases=aliases,
        compiler_params=pltpu.CompilerParams(vmem_limit_bytes=VMEM_BYTES),
    )(*args)


def swap(value, axis, mask, size):
    return lax.ppermute(value, axis, [(i, i ^ mask) for i in range(size)])


def levels(size):
    steps, stride = [], 1
    while stride < size:
        radix = 4 if stride > 1 and size // stride >= 4 else 2
        steps.append((radix, stride))
        stride *= radix
    return steps


def local(
    tiles,
    points,
    valid_rows,
    dest_shard,
    dest_slot,
    norm_gain,
    w_xz,
    w_bc,
    w_dt,
    dt_bias,
    decay_rate,
    skip_gain,
    gate_gain,
    w_out,
):
    n = lax.axis_size("curve")
    rows, width = points.shape[1:]
    heads, inner, key_width = w_dt.shape[2], w_out.shape[1], w_bc.shape[2] // 2
    part = inner // n
    params = (norm_gain, w_bc, jnp.swapaxes(w_dt, 1, 2), dt_bias, decay_rate, skip_gain, gate_gain)
    packed, spread, skip, w_held, norm_gain, w_bc, w_dt, dt_bias, decay_rate, _, gate_gain = call(
        functools.partial(pack_kernel, len(params)),
        [
            ((rows + EXTRA, width), BF16),
            ((128, 2 * inner), BF16),
            ((8 * skip_gain.shape[0], inner), F32),
            (w_xz.shape[1:], BF16),
        ]
        + [(p.shape, p.dtype) for p in params],
        [pltpu.SemaphoreType.DMA((len(params) + 2,))],
        points,
        valid_rows,
        dest_shard,
        dest_slot,
        w_xz,
        *params,
        in_hbm=(0, *range(4, 5 + len(params))),
        free=(1, 2, 3),
    )
    pieces = [packed] + [None] * (n - 1)
    for k in range(2, n, 2):
        pieces[k] = swap(packed, "curve", k, n)
    pieces[1] = swap(packed, "curve", 1, n)
    work = [
        ((n, rows, inner), F32),
        ((n, rows, inner), F32),
        ((n, rows, inner), F32),
        ((n, key_width, inner), F32),
        ((n, rows, key_width), BF16),
    ]
    shared = (norm_gain, w_held, w_bc, w_dt, dt_bias, decay_rate, spread, skip)
    work_done = call(own_piece_kernel, work, [], packed, *shared)
    for k in range(3, n, 2):
        (passed,) = call(relay_kernel, [(packed.shape, BF16)], [], pieces[k - 1], work_done[4])
        pieces[k] = swap(passed, "curve", 1, n)
    work_done = call(
        sibling_kernel,
        work,
        [],
        pieces[1],
        pieces[2],
        *shared,
        *work_done,
        aliases={10 + i: i for i in range(5)},
    )
    first = n + 11
    got = call(
        functools.partial(tile_kernel, n),
        work
        + [
            (w_xz.shape[1:], BF16),
            (w_out.shape[1:], BF16),
            ((key_width + EXTRA, part), BF16),
            ((rows, width), BF16),
            ((rows, 128), F32),
            ((n, rows, width), BF16),
            ((n, rows, key_width), BF16),
            ((rows, key_width), BF16),
            ((n, heads, rows), F32),
            ((n, heads, rows), F32),
            ((n, heads, rows), F32),
        ],
        [
            pltpu.VMEM(w_out.shape[1:], BF16),
            pltpu.VMEM((n, rows, width), BF16),
            pltpu.VMEM((n, rows, width), BF16),
            pltpu.VMEM((n, 8, 128), F32),
            pltpu.VMEM((n, 8, 128), F32),
            pltpu.VMEM((key_width, inner), F32),
            pltpu.SMEM((n,), jnp.int32),
            pltpu.SemaphoreType.DMA((3,)),
        ],
        *pieces,
        *shared,
        gate_gain,
        w_xz,
        w_out,
        *work_done,
        in_hbm=(first - 2, first - 1),
        aliases={first + i: i for i in range(5)},
    )
    w_two, w_out_two, send, own_x, own_live, normed_two, key_two, own_query = got[5:13]
    to_end_two, running_two, seen_two = got[13:]
    own, gate, decay = call(
        own_kernel,
        [((rows, inner), F32)] * 3,
        [],
        normed_two,
        key_two,
        own_query,
        to_end_two,
        running_two,
        seen_two,
        spread,
        skip,
        w_two,
    )
    earlier, fall = call(
        earlier_kernel,
        [((key_width, inner), F32), ((8, inner), F32)],
        [],
        normed_two,
        key_two,
        to_end_two,
        running_two,
        spread,
        w_two,
    )
    before = []
    steps = levels(tiles)
    for i, (radix, stride) in enumerate(steps):
        last = i == len(steps) - 1
        parts = [send] + [swap(send, "tile", k * stride, tiles) for k in range(1, radix)]
        outs = [((key_width, part), BF16)]
        if not last:
            outs = [((key_width + 8, part), F32), ((key_width + EXTRA, part), BF16)]
        got = call(
            functools.partial(join_kernel, radix, stride, last),
            outs,
            [pltpu.VMEM((radix, key_width + EXTRA, part), BF16)],
            *parts,
            *before,
            fall if last else decay,
        )
        if not last:
            before, send = [got[0]], got[1]
    incoming = got[0]
    states = [incoming] + [swap(incoming, "curve", k, n) for k in range(1, n)]
    common = (own, gate, own_query, decay, earlier, fall, gate_gain, w_out_two)
    partial = call(
        functools.partial(end_kernel, [0, 1], False),
        [((rows, width), F32), ((rows, 128), F32)],
        [],
        *states[:2],
        *common,
    )
    (out,) = call(
        functools.partial(end_kernel, list(range(2, n)), True),
        [((1, rows, width), BF16)],
        [],
        *states[2:],
        *common,
        own_x,
        own_live,
        *partial,
        out_fixed=False,
    )
    return out


def solution(mesh):
    in_specs = (
        P("tile", "curve", None),
        P("tile", "curve"),
        P("tile", "curve", None),
        P("tile", "curve", None),
    ) + (P(),) * 9
    return jax.shard_map(
        functools.partial(local, mesh.shape["tile"]),
        mesh=mesh,
        in_specs=in_specs,
        out_specs=P("tile", "curve", None),
        check_vma=False,
    )
```

```python
import functools

import jax
import jax.numpy as jnp
from jax import lax
from jax.experimental import pallas as pl
from jax.experimental.pallas import tpu as pltpu
from jax.sharding import PartitionSpec as P

F32, BF16 = jnp.float32, jnp.bfloat16
EPS = 1e-5
LOG2E = 1.4426950408889634
EXTRA = 16
VMEM_BYTES = 20 * 1024 * 1024


def dot(a, b):
    return jnp.dot(a, b, preferred_element_type=F32)


def dot_nt(a, b):
    return lax.dot_general(a, b, (((1,), (1,)), ((), ())), preferred_element_type=F32)


def turn(x):
    return x.astype(F32).T.astype(x.dtype)


def silu(x):
    half = 0.5 * x
    return half + half * jnp.tanh(half)


def split(x):
    hi = x.astype(BF16).astype(F32)
    return hi, x - hi


def normalise(x, gain):
    wide = x.astype(F32)
    return (wide * lax.rsqrt(jnp.mean(wide * wide, axis=-1, keepdims=True) + EPS) * gain).astype(BF16)


def iota(shape, axis):
    return lax.broadcasted_iota(jnp.int32, shape, axis)


def column(row):
    heads = row.shape[1]
    same = iota((heads, heads), 0) == iota((heads, heads), 1)
    return jnp.sum(jnp.where(same, row, 0.0), axis=1, keepdims=True)


def head_steps(normed, valids, w_dt_t, bias, rate):
    heads = w_dt_t.shape[0]
    rows = normed.shape[0] // len(valids)
    raw = dot_nt(w_dt_t, normed) + column(bias)
    steps = jnp.maximum(raw, 0.0) + jnp.log1p(jnp.exp(-jnp.abs(raw)))
    lane = iota((heads, rows), 1).astype(F32)
    steps = jnp.concatenate(
        [
            jnp.where(lane < valid, steps[:, c * rows : (c + 1) * rows], 0.0)
            for c, valid in enumerate(valids)
        ],
        axis=0,
    )
    falls = -steps * jnp.concatenate([column(rate) * LOG2E] * len(valids), axis=0)
    upper = jnp.where(iota((rows, rows), 0) <= iota((rows, rows), 1), 1.0, 0.0).astype(BF16)
    high, rest = split(falls)
    middle, low = split(rest)
    running = (
        dot(high.astype(BF16), upper) + dot(middle.astype(BF16), upper) + dot(low.astype(BF16), upper)
    )
    to_end = jnp.exp2(running[:, rows - 1 : rows] - running) * steps
    return steps, to_end, running


def by_rows(to_end, running):
    parts = [*split(to_end), *split(jnp.exp2(running)), running]
    used = len(parts) * running.shape[0]
    stack = jnp.concatenate(parts + [jnp.zeros((128 - used, running.shape[1]), F32)], axis=0)
    return stack.T


def seen_from(steps, running):
    return running - jnp.where(steps > 0.0, jnp.log2(jnp.maximum(steps, 1e-37)), -1e30)


def inside_pair(turned, seen, scores, value, head, heads):
    rows = turned.shape[0]
    at = 4 * heads + head
    weights = [
        (jnp.exp2(jnp.minimum(turned[:, at + k : at + k + 1] - seen[head + k : head + k + 1], 120.0)) * scores).astype(BF16)
        for k in range(2)
    ]
    left = iota((rows, 128), 1) < 64
    zero = jnp.zeros_like(value)
    both = jnp.concatenate([jnp.where(left, value, zero), jnp.where(left, zero, value)], axis=0)
    return dot(jnp.concatenate(weights, axis=1), both)


def masked_scores(query, key):
    rows = query.shape[0]
    return jnp.where(iota((rows, rows), 0) >= iota((rows, rows), 1), dot_nt(query, key), 0.0)


def make_spread(spread, heads):
    inner = spread.shape[1] // 2
    head = lax.shift_right_logical(iota((128, inner), 1), (inner // heads).bit_length() - 1)
    row = iota((128, inner), 0)
    for g in range(2):
        hit = (row == head + 2 * heads * g) | (row == head + 2 * heads * g + heads)
        spread[:, g * inner : (g + 1) * inner] = jnp.where(hit, 1.0, 0.0).astype(BF16)


def make_skip(skip_g, skip):
    layers, heads = skip_g.shape
    inner = skip.shape[1]
    head = lax.shift_right_logical(iota((heads, inner), 1), (inner // heads).bit_length() - 1)
    ones = jnp.where(head == iota((heads, inner), 0), 1.0, 0.0)
    for layer in range(layers):
        wide = jnp.broadcast_to(skip_g[layer : layer + 1, :], (8, heads))
        skip[8 * layer : 8 * layer + 8, :] = jnp.dot(
            wide, ones, preferred_element_type=F32, precision=lax.Precision.HIGHEST
        )


def pack_kernel(count, x, valid, shard, slot, *refs):
    sources, (out, spread, skip), refs = refs[:count], refs[count : count + 3], refs[count + 3 :]
    held, sems = refs[:-1], refs[-1]
    rows, width = x.shape[1:]
    copies = [pltpu.make_async_copy(x.at[0], out.at[pl.ds(0, rows)], sems.at[count])]
    copies += [pltpu.make_async_copy(a, b, sems.at[i]) for i, (a, b) in enumerate(zip(sources, held))]
    for copy in copies:
        copy.start()
    line, lane = iota((EXTRA, width), 0), iota((EXTRA, width), 1)
    live = valid[0, 0].astype(F32)
    place = (shard[0, 0, 0] + slot[0, 0, 0]).astype(F32)
    first = jnp.where(lane == 0, live, jnp.where(lane == 1, place, 0.0))
    out[rows:] = jnp.where(line == 0, first, 0.0).astype(BF16)
    make_spread(spread, held[5].shape[1])
    for copy in copies[1:]:
        copy.wait()
    make_skip(held[5], skip)
    copies[0].wait()


def live_count(packed):
    at = packed.shape[0] - EXTRA
    return packed[at:, :128].astype(F32)[0:1, 0:1]


def place_of(packed):
    extra = packed[packed.shape[0] - EXTRA :, :128].astype(F32)
    hit = (iota((EXTRA, 128), 0) == 0) & (iota((EXTRA, 128), 1) == 1)
    return jnp.sum(jnp.where(hit, extra, 0.0)).astype(jnp.int32)


def block_of(packed):
    return packed[: packed.shape[0] - EXTRA]


def pieces_work(xs, valids, slots, params, work, ready=lambda: None):
    norm_g, w_xz, w_bc, w_dt, bias, rate, spread, skip = params
    gates, local, decay, grown, queries = work
    rows = xs[0].shape[0]
    heads, inner, key_width = w_dt.shape[1], w_xz.shape[1] // 2, w_bc.shape[2] // 2
    normed = normalise(jnp.concatenate(xs, axis=0), norm_g[0:1, :])
    bc = silu(dot(normed, w_bc[0])).astype(BF16)
    steps, to_end, running = head_steps(normed, valids, w_dt[0], bias[0:1, :], rate[0:1, :])
    seen = seen_from(steps, running)
    parts = []
    for i, slot in enumerate(slots):
        at, of = slice(i * rows, (i + 1) * rows), slice(i * heads, (i + 1) * heads)
        key, query = bc[at, :key_width], bc[at, key_width:]
        queries[slot] = query
        turned = by_rows(to_end[of], running[of])
        parts.append((slot, at, turned, turned.astype(BF16), seen[of], masked_scores(query, key), turn(key)))
    ready()
    for j in range(0, inner, 256):
        cols, ends = slice(j, j + 256), slice(inner + j, inner + j + 256)
        values = silu(dot(normed, w_xz[:, cols])).astype(BF16)
        gate = silu(dot(normed, w_xz[:, ends]))
        for slot, at, turned, lhs, seen_here, scores, key_t in parts:
            value = values[at]
            wide = value.astype(F32)
            gates[slot, :, cols] = gate[at]
            decay[slot, :, cols] = dot(lhs, spread[:, ends])
            grown[slot, :, cols] = dot(key_t, (wide * dot(lhs, spread[:, cols])).astype(BF16))
            base = skip[0:1, cols] * wide
            for k in range(2):
                half = slice(128 * k, 128 * k + 128)
                head = (j + 128 * k) * heads // inner
                local[slot, :, j + 128 * k : j + 128 * k + 128] = (
                    inside_pair(turned, seen_here, scores, value[:, half], head, heads) + base[:, half]
                )


def begin_kernel(packed, norm_g, w_bc, w_dt, bias, rate, spread, skip, w_xz, w_held, *refs):
    work, sem = refs[:-1], refs[-1]
    copy = pltpu.make_async_copy(w_xz.at[0], w_held, sem)
    copy.start()
    params = (norm_g, w_held, w_bc, w_dt, bias, rate, spread, skip)
    pieces_work([block_of(packed)], [live_count(packed)], [0], params, work, copy.wait)


def piece_kernel(slot, packed, late, *refs):
    pieces_work([block_of(packed)], [live_count(packed)], [slot], refs[:8], refs[-5:])


def relay_kernel(x, *refs):
    refs[-1][...] = x[...]


def tile_kernel(n, *refs):
    pieces, refs = refs[:n], refs[n:]
    norm_g, w_held, w_bc, w_dt, bias, rate, spread, skip, gate_g, w_xz, w_out = refs[:11]
    refs = refs[16:]
    work, refs = refs[:5], refs[5:]
    (
        w_two,
        w_out_two,
        send,
        own_x,
        own_live,
        normed_two,
        key_two,
        own_query,
        to_end_two,
        running_two,
        seen_two,
        w_out_one,
        x_one,
        x_two,
        valid_one,
        valid_two,
        state,
        dest,
        sems,
    ) = refs
    gates, local, decay, grown, queries = work
    me = lax.axis_index("curve")
    rows, width = x_two.shape[1:]
    heads = w_dt.shape[1]
    inner = w_out.shape[1]
    key_width = w_bc.shape[2] // 2
    part = inner // n
    copies = [
        pltpu.make_async_copy(w_out.at[0], w_out_one, sems.at[0]),
        pltpu.make_async_copy(w_xz.at[1], w_two, sems.at[1]),
        pltpu.make_async_copy(w_out.at[1], w_out_two, sems.at[2]),
    ]
    for copy in copies:
        copy.start()
    valid = [live_count(piece) for piece in pieces]
    xs = [block_of(piece) for piece in pieces]
    for k in range(n):
        x_one[k] = xs[k]
        dest[k] = place_of(pieces[k])
        valid_one[k] = jnp.broadcast_to(valid[k], (8, 128))
        valid_two[dest[k]] = jnp.broadcast_to(valid[k], (8, 128))
    params = (norm_g, w_held, w_bc, w_dt, bias, rate, spread, skip)
    pieces_work(xs[3:], valid[3:], list(range(3, n)), params, work)

    copies[0].wait()
    row = iota((rows, 128), 0).astype(F32)
    for c in range(n):
        k = me ^ c
        query = queries[k]
        squares = jnp.zeros((rows, 1), F32)
        update = None
        for j in range(0, inner, 256):
            at = slice(j, j + 256)
            out = local[k, :, at]
            if c:
                old = state[:, at]
                out += dot(query, old.astype(BF16)) * decay[k, :, at]
                if c < n - 1:
                    state[:, at] = old * decay[k, rows - 1 :, at] + grown[k, :, at]
            else:
                state[:, at] = grown[k, :, at]
            gated = out * gates[k, :, at]
            squares += jnp.sum(gated * gated, axis=-1, keepdims=True)
            of_part = dot((gated * gate_g[0:1, at]).astype(BF16), w_out_one[at, :])
            update = of_part if update is None else update + of_part
        scale = jnp.broadcast_to(lax.rsqrt(squares * (1.0 / inner) + EPS), (rows, 128))
        factor = jnp.where(row < valid_one[k][0:1], scale, 0.0)
        factor = jnp.concatenate([factor] * (width // 128), axis=1)
        new = (x_one[k].astype(F32) + update * factor).astype(BF16)
        x_two[dest[k]] = new
        normed_two[dest[k]] = normalise(new, norm_g[1:2, :])

    own_x[...] = x_two[me]
    own_live[...] = jnp.where(row < valid_two[me][0:1], 1.0, 0.0)
    normed = normed_two[...].reshape(n * rows, width)
    steps, to_end, running = head_steps(
        normed, [valid_two[c][0:1, 0:1] for c in range(n)], w_dt[1], bias[1:2, :], rate[1:2, :]
    )
    bc = silu(dot(normed, w_bc[1])).astype(BF16)
    copies[1].wait()
    at = pl.ds(pl.multiple_of(me * part, 128), part)
    value = silu(dot(normed, w_two[:, at])).astype(BF16).astype(F32)
    after = jnp.zeros((heads, 1), F32)
    suffixes = [None] * n
    for c in reversed(range(n)):
        suffixes[c] = after
        after = after + running[c * heads : (c + 1) * heads, rows - 1 :]
    whole = jnp.broadcast_to(after, (heads, rows))
    turned = [
        by_rows(to_end[c * heads : (c + 1) * heads] * jnp.exp2(suffixes[c]), whole).astype(BF16) for c in range(n)
    ]
    to_end_x = dot(jnp.concatenate(turned, axis=0), spread[:, at])
    fall = dot(turned[0][:16], spread[:, pl.ds(pl.multiple_of(inner + me * part, 128), part)])[0:1]
    send[:key_width] = dot(turn(bc[:, :key_width]), (value * to_end_x).astype(BF16)).astype(BF16)
    send[key_width:] = decay_rows(fall)
    seen = seen_from(steps, running)
    for c in range(n):
        chunk, of = slice(c * rows, (c + 1) * rows), slice(c * heads, (c + 1) * heads)
        key_two[c] = bc[chunk, :key_width]
        queries[c] = bc[chunk, key_width:]
        to_end_two[c] = to_end[of]
        running_two[c] = running[of]
        seen_two[c] = seen[of]
    own_query[...] = queries[me]
    copies[2].wait()


def own_kernel(
    normed_two, key_two, query, to_end_two, running_two, seen_two, spread, skip, w_xz, local, gate, decay
):
    me = lax.axis_index("curve")
    inner = local.shape[1]
    heads = seen_two.shape[1]
    normed = normed_two[me]
    turned = by_rows(to_end_two[me], running_two[me])
    lhs = turned.astype(BF16)
    seen = seen_two[me]
    scores = masked_scores(query[...], key_two[me])
    for j in range(0, inner, 256):
        at = slice(j, j + 256)
        value = silu(dot(normed, w_xz[:, at])).astype(BF16)
        gate[:, at] = silu(dot(normed, w_xz[:, inner + j : inner + j + 256]))
        decay[:, at] = dot(lhs, spread[:, inner + j : inner + j + 256])
        base = skip[8:9, at] * value.astype(F32)
        for k in range(2):
            half = slice(128 * k, 128 * k + 128)
            head = (j + 128 * k) * heads // inner
            local[:, j + 128 * k : j + 128 * k + 128] = (
                inside_pair(turned, seen, scores, value[:, half], head, heads) + base[:, half]
            )


def earlier_kernel(normed_two, key_two, to_end_two, running_two, spread, w_xz, state, fall):
    me = lax.axis_index("curve")
    inner = state.shape[1]
    rows = normed_two.shape[1]
    state[...] = jnp.zeros_like(state)
    fall[...] = jnp.ones_like(fall)

    def chunk(c, _):
        normed = normed_two[c]
        lhs = by_rows(to_end_two[c], running_two[c]).astype(BF16)
        key_t = turn(key_two[c])
        for j in range(0, inner, 256):
            at = slice(j, j + 256)
            value = silu(dot(normed, w_xz[:, at])).astype(BF16).astype(F32)
            weighted = value * dot(lhs, spread[:, at])
            end_x = dot(lhs[rows - 16 :], spread[:, inner + j : inner + j + 256])[15:16]
            state[:, at] = state[:, at] * end_x + dot(key_t, weighted.astype(BF16))
            fall[:, at] = fall[:, at] * end_x
        return 0

    lax.fori_loop(0, me, chunk, 0)


def decay_rows(fall):
    high, low = split(fall)
    lines = iota((EXTRA, fall.shape[1]), 0)
    return jnp.where(lines == 0, high, jnp.where(lines == 1, low, 0.0)).astype(BF16)


def state_and_decay(ordered, u):
    states = ordered.shape[1] - EXTRA
    tail = ordered[u, states:].astype(F32)
    return ordered[u, :states].astype(F32), tail[0:1] + tail[1:2]


def join_kernel(radix, stride, last, *refs):
    deeper = stride > 1
    parts, before = refs[:radix], refs[radix] if deeper else None
    outs, ordered = refs[radix + 1 + deeper : -1], refs[-1]
    me = lax.rem(lax.div(lax.axis_index("tile"), stride), radix)
    states, width = parts[0].shape[0] - EXTRA, parts[0].shape[1]
    for k in range(radix):
        ordered[me ^ k] = parts[k][...]
    earlier = (jnp.zeros((states, width), F32), jnp.ones((1, width), F32))
    whole = None
    for u in range(radix if not last else radix - 1):
        one, fall = state_and_decay(ordered, u)
        if u < radix - 1:
            took = jnp.where(me > u, 1.0, 0.0)
            keep = jnp.where(me > u, fall, 1.0)
            earlier = (earlier[0] * keep + one * took, earlier[1] * keep)
        if not last:
            whole = (one, fall) if u == 0 else (whole[0] * fall + one, whole[1] * fall)
    state, fall = earlier
    if deeper:
        state = state * before[states : states + 1] + before[:states]
        fall = fall * before[states : states + 1]
    if last:
        outs[0][...] = state.astype(BF16)
        return
    outs[0][:states] = state
    outs[0][states:] = jnp.broadcast_to(fall, (8, width))
    outs[1][:states] = whole[0].astype(BF16)
    outs[1][states:] = decay_rows(whole[1])


def end_kernel(ks, first, final, *refs):
    pieces, refs = refs[: len(ks)], refs[len(ks) :]
    local, gate, query, decay, earlier, fall, gate_g, w_out = refs[:8]
    me = lax.axis_index("curve")
    rows, inner = local.shape
    part = pieces[0].shape[1]
    squares = jnp.zeros((rows, 1), F32)
    update = None
    for k, piece in zip(ks, pieces):
        at = pl.ds(pl.multiple_of((me ^ k) * part, 128), part)
        state = piece[...].astype(F32) * fall[0:1, at] + earlier[:, at]
        head_out = dot(query[...], state.astype(BF16)) * decay[:, at] + local[:, at]
        gated = head_out * gate[:, at]
        squares += jnp.sum(gated * gated, axis=-1, keepdims=True)
        of_part = dot((gated * gate_g[1:2, at]).astype(BF16), w_out[at, :])
        update = of_part if update is None else update + of_part
    refs = refs[8:]
    squares = jnp.broadcast_to(squares, (rows, 128))
    if not first:
        update, squares, refs = update + refs[0][...], squares + refs[1][...], refs[2:]
    if not final:
        refs[0][...] = update
        refs[1][...] = squares
        return
    x, live, out = refs
    factor = live[...] * lax.rsqrt(squares * (1.0 / inner) + EPS)
    for j in range(0, x.shape[1], 128):
        at = slice(j, j + 128)
        out[0, :, at] = (x[:, at].astype(F32) + factor * update[:, at]).astype(BF16)


def call(kernel, outs, scratch, *args, in_hbm=(), free=(), aliases={}, out_fixed=True):
    vmem = pl.BlockSpec(memory_space=pltpu.VMEM)
    spaces = [pltpu.HBM if i in in_hbm else pltpu.VMEM for i in range(len(args))]
    spaces = [pltpu.SMEM if i in free else space for i, space in enumerate(spaces)]
    args = [
        arg if space == pltpu.SMEM else pltpu.with_memory_space_constraint(arg, space)
        for arg, space in zip(args, spaces)
    ]
    return pl.pallas_call(
        kernel,
        out_shape=[(pltpu.VMEM if out_fixed else jax.ShapeDtypeStruct)(shape, kind) for shape, kind in outs],
        in_specs=[pl.BlockSpec(memory_space=space) for space in spaces],
        out_specs=[vmem] * len(outs),
        scratch_shapes=scratch,
        input_output_aliases=aliases,
        compiler_params=pltpu.CompilerParams(vmem_limit_bytes=VMEM_BYTES),
    )(*args)


def swap(value, axis, mask, size):
    return lax.ppermute(value, axis, [(i, i ^ mask) for i in range(size)])


def levels(size):
    steps, stride = [], 1
    while stride < size:
        radix = 4 if stride > 1 and size // stride >= 4 else 2
        steps.append((radix, stride))
        stride *= radix
    return steps


def local(
    tiles,
    points,
    valid_rows,
    dest_shard,
    dest_slot,
    norm_gain,
    w_xz,
    w_bc,
    w_dt,
    dt_bias,
    decay_rate,
    skip_gain,
    gate_gain,
    w_out,
):
    n = lax.axis_size("curve")
    rows, width = points.shape[1:]
    heads, inner, key_width = w_dt.shape[2], w_out.shape[1], w_bc.shape[2] // 2
    part = inner // n
    params = (norm_gain, w_bc, jnp.swapaxes(w_dt, 1, 2), dt_bias, decay_rate, skip_gain, gate_gain)
    packed, spread, skip, norm_gain, w_bc, w_dt, dt_bias, decay_rate, _, gate_gain = call(
        functools.partial(pack_kernel, len(params)),
        [((rows + EXTRA, width), BF16), ((128, 2 * inner), BF16), ((8 * skip_gain.shape[0], inner), F32)]
        + [(p.shape, p.dtype) for p in params],
        [pltpu.SemaphoreType.DMA((len(params) + 1,))],
        points,
        valid_rows,
        dest_shard,
        dest_slot,
        *params,
        in_hbm=(0, *range(4, 4 + len(params))),
        free=(1, 2, 3),
    )
    pieces = [packed] + [None] * (n - 1)
    for k in range(2, n, 2):
        pieces[k] = swap(packed, "curve", k, n)
    pieces[1] = swap(packed, "curve", 1, n)
    work = [
        ((n, rows, inner), F32),
        ((n, rows, inner), F32),
        ((n, rows, inner), F32),
        ((n, key_width, inner), F32),
        ((n, rows, key_width), BF16),
    ]
    w_held, *done = call(
        begin_kernel,
        [(w_xz.shape[1:], BF16)] + work,
        [pltpu.SemaphoreType.DMA],
        packed,
        norm_gain,
        w_bc,
        w_dt,
        dt_bias,
        decay_rate,
        spread,
        skip,
        w_xz,
        in_hbm=(8,),
    )
    shared = (norm_gain, w_held, w_bc, w_dt, dt_bias, decay_rate, spread, skip)
    aliases = {10 + i: i for i in range(5)}
    done = call(functools.partial(piece_kernel, 1), work, [], pieces[1], packed, *shared, *done, aliases=aliases)
    for k in range(3, n, 2):
        (passed,) = call(relay_kernel, [(packed.shape, BF16)], [], pieces[k - 1], done[4])
        pieces[k] = swap(passed, "curve", 1, n)
    done = call(functools.partial(piece_kernel, 2), work, [], pieces[2], passed, *shared, *done, aliases=aliases)
    first = n + 11
    got = call(
        functools.partial(tile_kernel, n),
        work
        + [
            (w_xz.shape[1:], BF16),
            (w_out.shape[1:], BF16),
            ((key_width + EXTRA, part), BF16),
            ((rows, width), BF16),
            ((rows, 128), F32),
            ((n, rows, width), BF16),
            ((n, rows, key_width), BF16),
            ((rows, key_width), BF16),
            ((n, heads, rows), F32),
            ((n, heads, rows), F32),
            ((n, heads, rows), F32),
        ],
        [
            pltpu.VMEM(w_out.shape[1:], BF16),
            pltpu.VMEM((n, rows, width), BF16),
            pltpu.VMEM((n, rows, width), BF16),
            pltpu.VMEM((n, 8, 128), F32),
            pltpu.VMEM((n, 8, 128), F32),
            pltpu.VMEM((key_width, inner), F32),
            pltpu.SMEM((n,), jnp.int32),
            pltpu.SemaphoreType.DMA((3,)),
        ],
        *pieces,
        *shared,
        gate_gain,
        w_xz,
        w_out,
        *done,
        in_hbm=(first - 2, first - 1),
        aliases={first + i: i for i in range(5)},
    )
    w_two, w_out_two, send, own_x, own_live, normed_two, key_two, own_query = got[5:13]
    to_end_two, running_two, seen_two = got[13:]
    own, gate, decay = call(
        own_kernel,
        [((rows, inner), F32)] * 3,
        [],
        normed_two,
        key_two,
        own_query,
        to_end_two,
        running_two,
        seen_two,
        spread,
        skip,
        w_two,
    )
    earlier, fall = call(
        earlier_kernel,
        [((key_width, inner), F32), ((8, inner), F32)],
        [],
        normed_two,
        key_two,
        to_end_two,
        running_two,
        spread,
        w_two,
    )
    before = []
    steps = levels(tiles)
    for i, (radix, stride) in enumerate(steps):
        last = i == len(steps) - 1
        parts = [send] + [swap(send, "tile", k * stride, tiles) for k in range(1, radix)]
        outs = [((key_width, part), BF16)]
        if not last:
            outs = [((key_width + 8, part), F32), ((key_width + EXTRA, part), BF16)]
        got = call(
            functools.partial(join_kernel, radix, stride, last),
            outs,
            [pltpu.VMEM((radix, key_width + EXTRA, part), BF16)],
            *parts,
            *before,
            fall if last else decay,
        )
        if not last:
            before, send = [got[0]], got[1]
    incoming = got[0]
    states = [incoming] + [swap(incoming, "curve", k, n) for k in range(1, n)]
    common = (own, gate, own_query, decay, earlier, fall, gate_gain, w_out_two)
    partial = []
    for ks in ([0, 1], list(range(3, n))):
        partial = call(
            functools.partial(end_kernel, ks, not partial, False),
            [((rows, width), F32), ((rows, 128), F32)],
            [],
            *[states[k] for k in ks],
            *common,
            *partial,
        )
    (out,) = call(
        functools.partial(end_kernel, [2], False, True),
        [((1, rows, width), BF16)],
        [],
        states[2],
        *common,
        *partial,
        own_x,
        own_live,
        out_fixed=False,
    )
    return out


def solution(mesh):
    in_specs = (
        P("tile", "curve", None),
        P("tile", "curve"),
        P("tile", "curve", None),
        P("tile", "curve", None),
    ) + (P(),) * 9
    return jax.shard_map(
        functools.partial(local, mesh.shape["tile"]),
        mesh=mesh,
        in_specs=in_specs,
        out_specs=P("tile", "curve", None),
        check_vma=False,
    )
```

```python
import functools

import jax
import jax.numpy as jnp
from jax import lax
from jax.experimental import pallas as pl
from jax.experimental.pallas import tpu as pltpu
from jax.sharding import PartitionSpec as P

F32, BF16 = jnp.float32, jnp.bfloat16
EPS = 1e-5
LOG2E = 1.4426950408889634
EXTRA = 16
VMEM_BYTES = 20 * 1024 * 1024


def dot(a, b):
    return jnp.dot(a, b, preferred_element_type=F32)


def dot_nt(a, b):
    return lax.dot_general(a, b, (((1,), (1,)), ((), ())), preferred_element_type=F32)


def turn(x):
    return x.astype(F32).T.astype(x.dtype)


def silu(x):
    half = 0.5 * x
    return half + half * jnp.tanh(half)


def split(x):
    hi = x.astype(BF16).astype(F32)
    return hi, x - hi


def normalise(x, gain):
    wide = x.astype(F32)
    return (wide * lax.rsqrt(jnp.mean(wide * wide, axis=-1, keepdims=True) + EPS) * gain).astype(BF16)


def iota(shape, axis):
    return lax.broadcasted_iota(jnp.int32, shape, axis)


def column(row):
    heads = row.shape[1]
    same = iota((heads, heads), 0) == iota((heads, heads), 1)
    return jnp.sum(jnp.where(same, row, 0.0), axis=1, keepdims=True)


def head_steps(normed, valids, w_dt_t, bias, rate):
    heads = w_dt_t.shape[0]
    rows = normed.shape[0] // len(valids)
    raw = dot_nt(w_dt_t, normed) + column(bias)
    steps = jnp.maximum(raw, 0.0) + jnp.log1p(jnp.exp(-jnp.abs(raw)))
    lane = iota((heads, rows), 1).astype(F32)
    steps = jnp.concatenate(
        [
            jnp.where(lane < valid, steps[:, c * rows : (c + 1) * rows], 0.0)
            for c, valid in enumerate(valids)
        ],
        axis=0,
    )
    falls = -steps * jnp.concatenate([column(rate) * LOG2E] * len(valids), axis=0)
    upper = jnp.where(iota((rows, rows), 0) <= iota((rows, rows), 1), 1.0, 0.0).astype(BF16)
    high, rest = split(falls)
    middle, low = split(rest)
    running = (
        dot(high.astype(BF16), upper) + dot(middle.astype(BF16), upper) + dot(low.astype(BF16), upper)
    )
    to_end = jnp.exp2(running[:, rows - 1 : rows] - running) * steps
    return steps, to_end, running


def by_rows(to_end, running):
    parts = [*split(to_end), *split(jnp.exp2(running)), running]
    used = len(parts) * running.shape[0]
    stack = jnp.concatenate(parts + [jnp.zeros((128 - used, running.shape[1]), F32)], axis=0)
    return stack.T


def seen_from(steps, running):
    return running - jnp.where(steps > 0.0, jnp.log2(jnp.maximum(steps, 1e-37)), -1e30)


def inside_pair(turned, seen, scores, value, head, heads):
    rows = turned.shape[0]
    at = 4 * heads + head
    weights = [
        (jnp.exp2(jnp.minimum(turned[:, at + k : at + k + 1] - seen[head + k : head + k + 1], 120.0)) * scores).astype(BF16)
        for k in range(2)
    ]
    left = iota((rows, 128), 1) < 64
    zero = jnp.zeros_like(value)
    both = jnp.concatenate([jnp.where(left, value, zero), jnp.where(left, zero, value)], axis=0)
    return dot(jnp.concatenate(weights, axis=1), both)


def masked_scores(query, key):
    rows = query.shape[0]
    return jnp.where(iota((rows, rows), 0) >= iota((rows, rows), 1), dot_nt(query, key), 0.0)


def make_spread(spread, heads):
    inner = spread.shape[1] // 2
    head = lax.shift_right_logical(iota((128, inner), 1), (inner // heads).bit_length() - 1)
    row = iota((128, inner), 0)
    for g in range(2):
        hit = (row == head + 2 * heads * g) | (row == head + 2 * heads * g + heads)
        spread[:, g * inner : (g + 1) * inner] = jnp.where(hit, 1.0, 0.0).astype(BF16)


def make_skip(skip_g, spread, skip):
    layers, heads = skip_g.shape
    inner = skip.shape[1]
    for layer in range(layers):
        parts = [part for part in split(skip_g[layer : layer + 1, :])]
        row = jnp.concatenate(parts + [jnp.zeros((1, 128 - 2 * heads), F32)], axis=1)
        wide = jnp.broadcast_to(row, (16, 128)).astype(BF16)
        skip[8 * layer : 8 * layer + 8, :] = dot(wide, spread[:, :inner])[:8]


def pack_kernel(count, x, valid, shard, slot, *refs):
    sources, out, held, sems = refs[:count], refs[count], refs[count + 1 : -1], refs[-1]
    rows, width = x.shape[1:]
    copies = [pltpu.make_async_copy(x.at[0], out.at[pl.ds(0, rows)], sems.at[count])]
    copies += [pltpu.make_async_copy(a, b, sems.at[i]) for i, (a, b) in enumerate(zip(sources, held))]
    for copy in copies:
        copy.start()
    line, lane = iota((EXTRA, width), 0), iota((EXTRA, width), 1)
    live = valid[0, 0].astype(F32)
    place = (shard[0, 0, 0] + slot[0, 0, 0]).astype(F32)
    first = jnp.where(lane == 0, live, jnp.where(lane == 1, place, 0.0))
    out[rows:] = jnp.where(line == 0, first, 0.0).astype(BF16)
    for copy in copies:
        copy.wait()


def live_count(packed):
    at = packed.shape[0] - EXTRA
    return packed[at:, :128].astype(F32)[0:1, 0:1]


def place_of(packed):
    extra = packed[packed.shape[0] - EXTRA :, :128].astype(F32)
    hit = (iota((EXTRA, 128), 0) == 0) & (iota((EXTRA, 128), 1) == 1)
    return jnp.sum(jnp.where(hit, extra, 0.0)).astype(jnp.int32)


def block_of(packed):
    return packed[: packed.shape[0] - EXTRA]


def pieces_work(xs, valids, slots, params, work, ready=None):
    norm_g, w_xz, w_bc, w_dt, bias, rate, spread, skip = params
    gates, local, decay, grown, queries = work
    rows = xs[0].shape[0]
    heads, inner, key_width = w_dt.shape[1], w_xz.shape[1] // 2, w_bc.shape[2] // 2
    normed = normalise(jnp.concatenate(xs, axis=0), norm_g[0:1, :])
    bc = silu(dot(normed, w_bc[0])).astype(BF16)

    def project():
        values = []
        for j in range(0, inner, 256):
            values.append(silu(dot(normed, w_xz[:, j : j + 256])).astype(BF16))
            gate = silu(dot(normed, w_xz[:, inner + j : inner + j + 256]))
            for i, slot in enumerate(slots):
                gates[slot, :, j : j + 256] = gate[i * rows : (i + 1) * rows]
        return values

    if ready is None:
        values = project()
    steps, to_end, running = head_steps(normed, valids, w_dt[0], bias[0:1, :], rate[0:1, :])
    seen = seen_from(steps, running)
    parts = []
    for i, slot in enumerate(slots):
        at, of = slice(i * rows, (i + 1) * rows), slice(i * heads, (i + 1) * heads)
        key, query = bc[at, :key_width], bc[at, key_width:]
        queries[slot] = query
        turned = by_rows(to_end[of], running[of])
        parts.append((slot, at, turned, turned.astype(BF16), seen[of], masked_scores(query, key), turn(key)))
    if ready is not None:
        ready()
        values = project()
    for j in range(0, inner, 256):
        cols, ends = slice(j, j + 256), slice(inner + j, inner + j + 256)
        for slot, at, turned, lhs, seen_here, scores, key_t in parts:
            value = values[j // 256][at]
            wide = value.astype(F32)
            decay[slot, :, cols] = dot(lhs, spread[:, ends])
            grown[slot, :, cols] = dot(key_t, (wide * dot(lhs, spread[:, cols])).astype(BF16))
            base = skip[0:1, cols] * wide
            for k in range(2):
                half = slice(128 * k, 128 * k + 128)
                head = (j + 128 * k) * heads // inner
                local[slot, :, j + 128 * k : j + 128 * k + 128] = (
                    inside_pair(turned, seen_here, scores, value[:, half], head, heads) + base[:, half]
                )


def begin_kernel(packed, norm_g, w_bc, w_dt, bias, rate, skip_g, w_xz, w_held, spread, skip, *refs):
    work, sem = refs[:-1], refs[-1]
    copy = pltpu.make_async_copy(w_xz.at[0], w_held, sem)
    copy.start()
    make_spread(spread, w_dt.shape[1])
    make_skip(skip_g, spread, skip)
    params = (norm_g, w_held, w_bc, w_dt, bias, rate, spread, skip)
    pieces_work([block_of(packed)], [live_count(packed)], [0], params, work, copy.wait)


def piece_kernel(slot, packed, late, *refs):
    pieces_work([block_of(packed)], [live_count(packed)], [slot], refs[:8], refs[-5:])


def relay_kernel(x, *refs):
    refs[-1][...] = x[...]


def tile_kernel(n, *refs):
    pieces, refs = refs[:n], refs[n:]
    norm_g, w_held, w_bc, w_dt, bias, rate, spread, skip, gate_g, w_xz, w_out = refs[:11]
    refs = refs[16:]
    work, refs = refs[:5], refs[5:]
    (
        w_two,
        w_out_two,
        send,
        own_x,
        own_live,
        normed_two,
        key_two,
        own_query,
        to_end_two,
        running_two,
        seen_two,
        w_out_one,
        x_one,
        x_two,
        valid_one,
        valid_two,
        state,
        dest,
        sems,
    ) = refs
    gates, local, decay, grown, queries = work
    me = lax.axis_index("curve")
    rows, width = x_two.shape[1:]
    heads = w_dt.shape[1]
    inner = w_out.shape[1]
    key_width = w_bc.shape[2] // 2
    part = inner // n
    copies = [
        pltpu.make_async_copy(w_out.at[0], w_out_one, sems.at[0]),
        pltpu.make_async_copy(w_xz.at[1], w_two, sems.at[1]),
        pltpu.make_async_copy(w_out.at[1], w_out_two, sems.at[2]),
    ]
    for copy in copies:
        copy.start()
    valid = [live_count(piece) for piece in pieces]
    xs = [block_of(piece) for piece in pieces]
    for k in range(n):
        x_one[k] = xs[k]
        dest[k] = place_of(pieces[k])
        valid_one[k] = jnp.broadcast_to(valid[k], (8, 128))
        valid_two[dest[k]] = jnp.broadcast_to(valid[k], (8, 128))
    params = (norm_g, w_held, w_bc, w_dt, bias, rate, spread, skip)
    pieces_work(xs[3:], valid[3:], list(range(3, n)), params, work)

    copies[0].wait()
    row = iota((rows, 128), 0).astype(F32)
    for c in range(n):
        k = me ^ c
        query = queries[k]
        squares = jnp.zeros((rows, 1), F32)
        update = None
        for j in range(0, inner, 256):
            at = slice(j, j + 256)
            out = local[k, :, at]
            if c:
                old = state[:, at]
                out += dot(query, old.astype(BF16)) * decay[k, :, at]
                if c < n - 1:
                    state[:, at] = old * decay[k, rows - 1 :, at] + grown[k, :, at]
            else:
                state[:, at] = grown[k, :, at]
            gated = out * gates[k, :, at]
            squares += jnp.sum(gated * gated, axis=-1, keepdims=True)
            of_part = dot((gated * gate_g[0:1, at]).astype(BF16), w_out_one[at, :])
            update = of_part if update is None else update + of_part
        scale = jnp.broadcast_to(lax.rsqrt(squares * (1.0 / inner) + EPS), (rows, 128))
        factor = jnp.where(row < valid_one[k][0:1], scale, 0.0)
        factor = jnp.concatenate([factor] * (width // 128), axis=1)
        new = (x_one[k].astype(F32) + update * factor).astype(BF16)
        x_two[dest[k]] = new
        normed_two[dest[k]] = normalise(new, norm_g[1:2, :])

    own_x[...] = x_two[me]
    own_live[...] = jnp.where(row < valid_two[me][0:1], 1.0, 0.0)
    normed = normed_two[...].reshape(n * rows, width)
    steps, to_end, running = head_steps(
        normed, [valid_two[c][0:1, 0:1] for c in range(n)], w_dt[1], bias[1:2, :], rate[1:2, :]
    )
    bc = silu(dot(normed, w_bc[1])).astype(BF16)
    copies[1].wait()
    at = pl.ds(pl.multiple_of(me * part, 128), part)
    value = silu(dot(normed, w_two[:, at])).astype(BF16).astype(F32)
    after = jnp.zeros((heads, 1), F32)
    suffixes = [None] * n
    for c in reversed(range(n)):
        suffixes[c] = after
        after = after + running[c * heads : (c + 1) * heads, rows - 1 :]
    whole = jnp.broadcast_to(after, (heads, rows))
    turned = [
        by_rows(to_end[c * heads : (c + 1) * heads] * jnp.exp2(suffixes[c]), whole).astype(BF16) for c in range(n)
    ]
    to_end_x = dot(jnp.concatenate(turned, axis=0), spread[:, at])
    fall = dot(turned[0][:16], spread[:, pl.ds(pl.multiple_of(inner + me * part, 128), part)])[0:1]
    send[:key_width] = dot(turn(bc[:, :key_width]), (value * to_end_x).astype(BF16)).astype(BF16)
    send[key_width:] = decay_rows(fall)
    seen = seen_from(steps, running)
    for c in range(n):
        chunk, of = slice(c * rows, (c + 1) * rows), slice(c * heads, (c + 1) * heads)
        key_two[c] = bc[chunk, :key_width]
        queries[c] = bc[chunk, key_width:]
        to_end_two[c] = to_end[of]
        running_two[c] = running[of]
        seen_two[c] = seen[of]
    own_query[...] = queries[me]
    copies[2].wait()


def own_kernel(
    normed_two, key_two, query, to_end_two, running_two, seen_two, spread, skip, w_xz, local, gate, decay
):
    me = lax.axis_index("curve")
    inner = local.shape[1]
    heads = seen_two.shape[1]
    normed = normed_two[me]
    turned = by_rows(to_end_two[me], running_two[me])
    lhs = turned.astype(BF16)
    seen = seen_two[me]
    scores = masked_scores(query[...], key_two[me])
    for j in range(0, inner, 256):
        at = slice(j, j + 256)
        value = silu(dot(normed, w_xz[:, at])).astype(BF16)
        gate[:, at] = silu(dot(normed, w_xz[:, inner + j : inner + j + 256]))
        decay[:, at] = dot(lhs, spread[:, inner + j : inner + j + 256])
        base = skip[8:9, at] * value.astype(F32)
        for k in range(2):
            half = slice(128 * k, 128 * k + 128)
            head = (j + 128 * k) * heads // inner
            local[:, j + 128 * k : j + 128 * k + 128] = (
                inside_pair(turned, seen, scores, value[:, half], head, heads) + base[:, half]
            )


def earlier_kernel(normed_two, key_two, to_end_two, running_two, spread, w_xz, state, fall):
    me = lax.axis_index("curve")
    inner = state.shape[1]
    rows = normed_two.shape[1]
    state[...] = jnp.zeros_like(state)
    fall[...] = jnp.ones_like(fall)

    def chunk(c, _):
        normed = normed_two[c]
        lhs = by_rows(to_end_two[c], running_two[c]).astype(BF16)
        key_t = turn(key_two[c])
        for j in range(0, inner, 256):
            at = slice(j, j + 256)
            value = silu(dot(normed, w_xz[:, at])).astype(BF16).astype(F32)
            weighted = value * dot(lhs, spread[:, at])
            end_x = dot(lhs[rows - 16 :], spread[:, inner + j : inner + j + 256])[15:16]
            state[:, at] = state[:, at] * end_x + dot(key_t, weighted.astype(BF16))
            fall[:, at] = fall[:, at] * end_x
        return 0

    lax.fori_loop(0, me, chunk, 0)


def decay_rows(fall):
    high, low = split(fall)
    lines = iota((EXTRA, fall.shape[1]), 0)
    return jnp.where(lines == 0, high, jnp.where(lines == 1, low, 0.0)).astype(BF16)


def state_and_decay(ordered, u):
    states = ordered.shape[1] - EXTRA
    tail = ordered[u, states:].astype(F32)
    return ordered[u, :states].astype(F32), tail[0:1] + tail[1:2]


def join_kernel(radix, stride, last, *refs):
    deeper = stride > 1
    parts, before = refs[:radix], refs[radix] if deeper else None
    outs, ordered = refs[radix + 1 + deeper : -1], refs[-1]
    me = lax.rem(lax.div(lax.axis_index("tile"), stride), radix)
    states, width = parts[0].shape[0] - EXTRA, parts[0].shape[1]
    for k in range(radix):
        ordered[me ^ k] = parts[k][...]
    earlier = (jnp.zeros((states, width), F32), jnp.ones((1, width), F32))
    whole = None
    for u in range(radix if not last else radix - 1):
        one, fall = state_and_decay(ordered, u)
        if u < radix - 1:
            took = jnp.where(me > u, 1.0, 0.0)
            keep = jnp.where(me > u, fall, 1.0)
            earlier = (earlier[0] * keep + one * took, earlier[1] * keep)
        if not last:
            whole = (one, fall) if u == 0 else (whole[0] * fall + one, whole[1] * fall)
    state, fall = earlier
    if deeper:
        state = state * before[states : states + 1] + before[:states]
        fall = fall * before[states : states + 1]
    if last:
        outs[0][...] = state.astype(BF16)
        return
    outs[0][:states] = state
    outs[0][states:] = jnp.broadcast_to(fall, (8, width))
    outs[1][:states] = whole[0].astype(BF16)
    outs[1][states:] = decay_rows(whole[1])


def end_kernel(ks, first, final, *refs):
    pieces, refs = refs[: len(ks)], refs[len(ks) :]
    local, gate, query, decay, earlier, fall, gate_g, w_out = refs[:8]
    me = lax.axis_index("curve")
    rows, inner = local.shape
    part = pieces[0].shape[1]
    squares = jnp.zeros((rows, 1), F32)
    update = None
    for k, piece in zip(ks, pieces):
        at = pl.ds(pl.multiple_of((me ^ k) * part, 128), part)
        state = piece[...].astype(F32) * fall[0:1, at] + earlier[:, at]
        head_out = dot(query[...], state.astype(BF16)) * decay[:, at] + local[:, at]
        gated = head_out * gate[:, at]
        squares += jnp.sum(gated * gated, axis=-1, keepdims=True)
        of_part = dot((gated * gate_g[1:2, at]).astype(BF16), w_out[at, :])
        update = of_part if update is None else update + of_part
    refs = refs[8:]
    squares = jnp.broadcast_to(squares, (rows, 128))
    if not first:
        update, squares, refs = update + refs[0][...], squares + refs[1][...], refs[2:]
    if not final:
        refs[0][...] = update
        refs[1][...] = squares
        return
    x, live, out = refs
    factor = live[...] * lax.rsqrt(squares * (1.0 / inner) + EPS)
    for j in range(0, x.shape[1], 128):
        at = slice(j, j + 128)
        out[0, :, at] = (x[:, at].astype(F32) + factor * update[:, at]).astype(BF16)


def call(kernel, outs, scratch, *args, in_hbm=(), free=(), aliases={}, out_fixed=True):
    vmem = pl.BlockSpec(memory_space=pltpu.VMEM)
    spaces = [pltpu.HBM if i in in_hbm else pltpu.VMEM for i in range(len(args))]
    spaces = [pltpu.SMEM if i in free else space for i, space in enumerate(spaces)]
    args = [
        arg if space == pltpu.SMEM else pltpu.with_memory_space_constraint(arg, space)
        for arg, space in zip(args, spaces)
    ]
    return pl.pallas_call(
        kernel,
        out_shape=[(pltpu.VMEM if out_fixed else jax.ShapeDtypeStruct)(shape, kind) for shape, kind in outs],
        in_specs=[pl.BlockSpec(memory_space=space) for space in spaces],
        out_specs=[vmem] * len(outs),
        scratch_shapes=scratch,
        input_output_aliases=aliases,
        compiler_params=pltpu.CompilerParams(vmem_limit_bytes=VMEM_BYTES),
    )(*args)


def swap(value, axis, mask, size):
    return lax.ppermute(value, axis, [(i, i ^ mask) for i in range(size)])


def levels(size):
    steps, stride = [], 1
    while stride < size:
        radix = 4 if stride > 1 and size // stride >= 4 else 2
        steps.append((radix, stride))
        stride *= radix
    return steps


def local(
    tiles,
    points,
    valid_rows,
    dest_shard,
    dest_slot,
    norm_gain,
    w_xz,
    w_bc,
    w_dt,
    dt_bias,
    decay_rate,
    skip_gain,
    gate_gain,
    w_out,
):
    n = lax.axis_size("curve")
    rows, width = points.shape[1:]
    heads, inner, key_width = w_dt.shape[2], w_out.shape[1], w_bc.shape[2] // 2
    part = inner // n
    params = (norm_gain, w_bc, jnp.swapaxes(w_dt, 1, 2), dt_bias, decay_rate, skip_gain, gate_gain)
    packed, norm_gain, w_bc, w_dt, dt_bias, decay_rate, skip_gain, gate_gain = call(
        functools.partial(pack_kernel, len(params)),
        [((rows + EXTRA, width), BF16)] + [(p.shape, p.dtype) for p in params],
        [pltpu.SemaphoreType.DMA((len(params) + 1,))],
        points,
        valid_rows,
        dest_shard,
        dest_slot,
        *params,
        in_hbm=(0, *range(4, 4 + len(params))),
        free=(1, 2, 3),
    )
    pieces = [packed] + [None] * (n - 1)
    for k in range(2, n, 2):
        pieces[k] = swap(packed, "curve", k, n)
    pieces[1] = swap(packed, "curve", 1, n)
    work = [
        ((n, rows, inner), F32),
        ((n, rows, inner), F32),
        ((n, rows, inner), F32),
        ((n, key_width, inner), F32),
        ((n, rows, key_width), BF16),
    ]
    w_held, spread, skip, *done = call(
        begin_kernel,
        [(w_xz.shape[1:], BF16), ((128, 2 * inner), BF16), ((8 * skip_gain.shape[0], inner), F32)] + work,
        [pltpu.SemaphoreType.DMA],
        packed,
        norm_gain,
        w_bc,
        w_dt,
        dt_bias,
        decay_rate,
        skip_gain,
        w_xz,
        in_hbm=(7,),
    )
    shared = (norm_gain, w_held, w_bc, w_dt, dt_bias, decay_rate, spread, skip)
    aliases = {10 + i: i for i in range(5)}
    done = call(functools.partial(piece_kernel, 1), work, [], pieces[1], packed, *shared, *done, aliases=aliases)
    for k in range(3, n, 2):
        (passed,) = call(relay_kernel, [(packed.shape, BF16)], [], pieces[k - 1], done[4])
        pieces[k] = swap(passed, "curve", 1, n)
    done = call(functools.partial(piece_kernel, 2), work, [], pieces[2], passed, *shared, *done, aliases=aliases)
    first = n + 11
    got = call(
        functools.partial(tile_kernel, n),
        work
        + [
            (w_xz.shape[1:], BF16),
            (w_out.shape[1:], BF16),
            ((key_width + EXTRA, part), BF16),
            ((rows, width), BF16),
            ((rows, 128), F32),
            ((n, rows, width), BF16),
            ((n, rows, key_width), BF16),
            ((rows, key_width), BF16),
            ((n, heads, rows), F32),
            ((n, heads, rows), F32),
            ((n, heads, rows), F32),
        ],
        [
            pltpu.VMEM(w_out.shape[1:], BF16),
            pltpu.VMEM((n, rows, width), BF16),
            pltpu.VMEM((n, rows, width), BF16),
            pltpu.VMEM((n, 8, 128), F32),
            pltpu.VMEM((n, 8, 128), F32),
            pltpu.VMEM((key_width, inner), F32),
            pltpu.SMEM((n,), jnp.int32),
            pltpu.SemaphoreType.DMA((3,)),
        ],
        *pieces,
        *shared,
        gate_gain,
        w_xz,
        w_out,
        *done,
        in_hbm=(first - 2, first - 1),
        aliases={first + i: i for i in range(5)},
    )
    w_two, w_out_two, send, own_x, own_live, normed_two, key_two, own_query = got[5:13]
    to_end_two, running_two, seen_two = got[13:]
    own, gate, decay = call(
        own_kernel,
        [((rows, inner), F32)] * 3,
        [],
        normed_two,
        key_two,
        own_query,
        to_end_two,
        running_two,
        seen_two,
        spread,
        skip,
        w_two,
    )
    earlier, fall = call(
        earlier_kernel,
        [((key_width, inner), F32), ((8, inner), F32)],
        [],
        normed_two,
        key_two,
        to_end_two,
        running_two,
        spread,
        w_two,
    )
    before = []
    steps = levels(tiles)
    for i, (radix, stride) in enumerate(steps):
        last = i == len(steps) - 1
        parts = [send] + [swap(send, "tile", k * stride, tiles) for k in range(1, radix)]
        outs = [((key_width, part), BF16)]
        if not last:
            outs = [((key_width + 8, part), F32), ((key_width + EXTRA, part), BF16)]
        got = call(
            functools.partial(join_kernel, radix, stride, last),
            outs,
            [pltpu.VMEM((radix, key_width + EXTRA, part), BF16)],
            *parts,
            *before,
            fall if last else decay,
        )
        if not last:
            before, send = [got[0]], got[1]
    incoming = got[0]
    states = [incoming] + [swap(incoming, "curve", k, n) for k in range(1, n)]
    common = (own, gate, own_query, decay, earlier, fall, gate_gain, w_out_two)
    partial = []
    for ks in ([0, 1], list(range(3, n))):
        partial = call(
            functools.partial(end_kernel, ks, not partial, False),
            [((rows, width), F32), ((rows, 128), F32)],
            [],
            *[states[k] for k in ks],
            *common,
            *partial,
        )
    (out,) = call(
        functools.partial(end_kernel, [2], False, True),
        [((1, rows, width), BF16)],
        [],
        states[2],
        *common,
        *partial,
        own_x,
        own_live,
        out_fixed=False,
    )
    return out


def solution(mesh):
    in_specs = (
        P("tile", "curve", None),
        P("tile", "curve"),
        P("tile", "curve", None),
        P("tile", "curve", None),
    ) + (P(),) * 9
    return jax.shard_map(
        functools.partial(local, mesh.shape["tile"]),
        mesh=mesh,
        in_specs=in_specs,
        out_specs=P("tile", "curve", None),
        check_vma=False,
    )
```

```python
import functools

import jax
import jax.numpy as jnp
from jax import lax
from jax.experimental import pallas as pl
from jax.experimental.pallas import tpu as pltpu
from jax.sharding import PartitionSpec as P

F32, BF16 = jnp.float32, jnp.bfloat16
EPS = 1e-5
LOG2E = 1.4426950408889634
EXTRA = 16
VMEM_BYTES = 20 * 1024 * 1024


def dot(a, b):
    return jnp.dot(a, b, preferred_element_type=F32)


def dot_nt(a, b):
    return lax.dot_general(a, b, (((1,), (1,)), ((), ())), preferred_element_type=F32)


def turn(x):
    return x.astype(F32).T.astype(x.dtype)


def silu(x):
    half = 0.5 * x
    return half + half * jnp.tanh(half)


def split(x):
    hi = x.astype(BF16).astype(F32)
    return hi, x - hi


def normalise(x, gain):
    wide = x.astype(F32)
    return (wide * lax.rsqrt(jnp.mean(wide * wide, axis=-1, keepdims=True) + EPS) * gain).astype(BF16)


def iota(shape, axis):
    return lax.broadcasted_iota(jnp.int32, shape, axis)


def column(row):
    heads = row.shape[1]
    same = iota((heads, heads), 0) == iota((heads, heads), 1)
    return jnp.sum(jnp.where(same, row, 0.0), axis=1, keepdims=True)


def head_steps(normed, valids, w_dt_t, bias, rate):
    heads = w_dt_t.shape[0]
    rows = normed.shape[0] // len(valids)
    raw = dot_nt(w_dt_t, normed) + column(bias)
    steps = jnp.maximum(raw, 0.0) + jnp.log1p(jnp.exp(-jnp.abs(raw)))
    lane = iota((heads, rows), 1).astype(F32)
    steps = jnp.concatenate(
        [
            jnp.where(lane < valid, steps[:, c * rows : (c + 1) * rows], 0.0)
            for c, valid in enumerate(valids)
        ],
        axis=0,
    )
    falls = -steps * jnp.concatenate([column(rate) * LOG2E] * len(valids), axis=0)
    upper = jnp.where(iota((rows, rows), 0) <= iota((rows, rows), 1), 1.0, 0.0).astype(BF16)
    high, rest = split(falls)
    middle, low = split(rest)
    running = (
        dot(high.astype(BF16), upper) + dot(middle.astype(BF16), upper) + dot(low.astype(BF16), upper)
    )
    to_end = jnp.exp2(running[:, rows - 1 : rows] - running) * steps
    return steps, to_end, running


def by_rows(to_end, running):
    parts = [*split(to_end), *split(jnp.exp2(running)), running]
    used = len(parts) * running.shape[0]
    stack = jnp.concatenate(parts + [jnp.zeros((128 - used, running.shape[1]), F32)], axis=0)
    return stack.T


def seen_from(steps, running):
    return running - jnp.where(steps > 0.0, jnp.log2(jnp.maximum(steps, 1e-37)), -1e30)


def inside_pair(turned, seen, scores, value, head, heads):
    rows = turned.shape[0]
    at = 4 * heads + head
    weights = [
        (jnp.exp2(jnp.minimum(turned[:, at + k : at + k + 1] - seen[head + k : head + k + 1], 120.0)) * scores).astype(BF16)
        for k in range(2)
    ]
    left = iota((rows, 128), 1) < 64
    zero = jnp.zeros_like(value)
    both = jnp.concatenate([jnp.where(left, value, zero), jnp.where(left, zero, value)], axis=0)
    return dot(jnp.concatenate(weights, axis=1), both)


def masked_scores(query, key):
    rows = query.shape[0]
    return jnp.where(iota((rows, rows), 0) >= iota((rows, rows), 1), dot_nt(query, key), 0.0)


def make_spread(spread, heads):
    inner = spread.shape[1] // 2
    head = lax.shift_right_logical(iota((128, inner), 1), (inner // heads).bit_length() - 1)
    row = iota((128, inner), 0)
    for g in range(2):
        hit = (row == head + 2 * heads * g) | (row == head + 2 * heads * g + heads)
        spread[:, g * inner : (g + 1) * inner] = jnp.where(hit, 1.0, 0.0).astype(BF16)


def make_skip(skip_g, spread, skip):
    layers, heads = skip_g.shape
    inner = skip.shape[1]
    for layer in range(layers):
        parts = [part for part in split(skip_g[layer : layer + 1, :])]
        row = jnp.concatenate(parts + [jnp.zeros((1, 128 - 2 * heads), F32)], axis=1)
        wide = jnp.broadcast_to(row, (16, 128)).astype(BF16)
        skip[8 * layer : 8 * layer + 8, :] = dot(wide, spread[:, :inner])[:8]


def pack_kernel(count, x, valid, shard, slot, *refs):
    sources, out, held, sems = refs[:count], refs[count], refs[count + 1 : -1], refs[-1]
    rows, width = x.shape[1:]
    copies = [pltpu.make_async_copy(x.at[0], out.at[pl.ds(0, rows)], sems.at[count])]
    copies += [pltpu.make_async_copy(a, b, sems.at[i]) for i, (a, b) in enumerate(zip(sources, held))]
    for copy in copies:
        copy.start()
    line, lane = iota((EXTRA, width), 0), iota((EXTRA, width), 1)
    live = valid[0, 0].astype(F32)
    place = (shard[0, 0, 0] + slot[0, 0, 0]).astype(F32)
    first = jnp.where(lane == 0, live, jnp.where(lane == 1, place, 0.0))
    out[rows:] = jnp.where(line == 0, first, 0.0).astype(BF16)
    for copy in copies:
        copy.wait()


def live_count(packed):
    at = packed.shape[0] - EXTRA
    return packed[at:, :128].astype(F32)[0:1, 0:1]


def place_of(packed):
    extra = packed[packed.shape[0] - EXTRA :, :128].astype(F32)
    hit = (iota((EXTRA, 128), 0) == 0) & (iota((EXTRA, 128), 1) == 1)
    return jnp.sum(jnp.where(hit, extra, 0.0)).astype(jnp.int32)


def block_of(packed):
    return packed[: packed.shape[0] - EXTRA]


def pieces_work(xs, valids, slots, params, work, ready=lambda: None):
    norm_g, w_xz, w_bc, w_dt, bias, rate, spread, skip = params
    gates, local, decay, grown, queries = work
    rows = xs[0].shape[0]
    heads, inner, key_width = w_dt.shape[1], w_xz.shape[1] // 2, w_bc.shape[2] // 2
    normed = normalise(jnp.concatenate(xs, axis=0), norm_g[0:1, :])
    bc = silu(dot(normed, w_bc[0])).astype(BF16)
    steps, to_end, running = head_steps(normed, valids, w_dt[0], bias[0:1, :], rate[0:1, :])
    seen = seen_from(steps, running)
    parts = []
    for i, slot in enumerate(slots):
        at, of = slice(i * rows, (i + 1) * rows), slice(i * heads, (i + 1) * heads)
        key, query = bc[at, :key_width], bc[at, key_width:]
        queries[slot] = query
        turned = by_rows(to_end[of], running[of])
        parts.append((slot, at, turned, turned.astype(BF16), seen[of], masked_scores(query, key), turn(key)))
    ready()
    for j in range(0, inner, 256):
        cols, ends = slice(j, j + 256), slice(inner + j, inner + j + 256)
        values = silu(dot(normed, w_xz[:, cols])).astype(BF16)
        gate = silu(dot(normed, w_xz[:, ends]))
        for slot, at, turned, lhs, seen_here, scores, key_t in parts:
            value = values[at]
            wide = value.astype(F32)
            gates[slot, :, cols] = gate[at]
            decay[slot, :, cols] = dot(lhs, spread[:, ends])
            grown[slot, :, cols] = dot(key_t, (wide * dot(lhs, spread[:, cols])).astype(BF16))
            base = skip[0:1, cols] * wide
            for k in range(2):
                half = slice(128 * k, 128 * k + 128)
                head = (j + 128 * k) * heads // inner
                local[slot, :, j + 128 * k : j + 128 * k + 128] = (
                    inside_pair(turned, seen_here, scores, value[:, half], head, heads) + base[:, half]
                )


def begin_kernel(packed, norm_g, w_bc, w_dt, bias, rate, skip_g, w_xz, w_held, spread, skip, *refs):
    work, sem = refs[:-1], refs[-1]
    copy = pltpu.make_async_copy(w_xz.at[0], w_held, sem)
    copy.start()
    make_spread(spread, w_dt.shape[1])
    make_skip(skip_g, spread, skip)
    params = (norm_g, w_held, w_bc, w_dt, bias, rate, spread, skip)
    pieces_work([block_of(packed)], [live_count(packed)], [0], params, work, copy.wait)


def piece_kernel(slot, packed, late, *refs):
    pieces_work([block_of(packed)], [live_count(packed)], [slot], refs[:8], refs[-5:])


def relay_kernel(x, *refs):
    refs[-1][...] = x[...]


def tile_kernel(n, *refs):
    pieces, refs = refs[:n], refs[n:]
    norm_g, w_held, w_bc, w_dt, bias, rate, spread, skip, gate_g, w_xz, w_out = refs[:11]
    refs = refs[16:]
    work, refs = refs[:5], refs[5:]
    (
        w_two,
        w_out_two,
        send,
        own_x,
        own_live,
        normed_two,
        key_two,
        own_query,
        to_end_two,
        running_two,
        seen_two,
        w_out_one,
        x_one,
        x_two,
        valid_one,
        valid_two,
        state,
        dest,
        sems,
    ) = refs
    gates, local, decay, grown, queries = work
    me = lax.axis_index("curve")
    rows, width = x_two.shape[1:]
    heads = w_dt.shape[1]
    inner = w_out.shape[1]
    key_width = w_bc.shape[2] // 2
    part = inner // n
    copies = [
        pltpu.make_async_copy(w_out.at[0], w_out_one, sems.at[0]),
        pltpu.make_async_copy(w_xz.at[1], w_two, sems.at[1]),
        pltpu.make_async_copy(w_out.at[1], w_out_two, sems.at[2]),
    ]
    for copy in copies:
        copy.start()
    valid = [live_count(piece) for piece in pieces]
    xs = [block_of(piece) for piece in pieces]
    for k in range(n):
        x_one[k] = xs[k]
        dest[k] = place_of(pieces[k])
        valid_one[k] = jnp.broadcast_to(valid[k], (8, 128))
        valid_two[dest[k]] = jnp.broadcast_to(valid[k], (8, 128))
    params = (norm_g, w_held, w_bc, w_dt, bias, rate, spread, skip)
    pieces_work(xs[3:], valid[3:], list(range(3, n)), params, work)

    copies[0].wait()
    row = iota((rows, 128), 0).astype(F32)
    for c in range(n):
        k = me ^ c
        query = queries[k]
        squares = jnp.zeros((rows, 1), F32)
        update = None
        for j in range(0, inner, 256):
            at = slice(j, j + 256)
            out = local[k, :, at]
            if c:
                old = state[:, at]
                out += dot(query, old.astype(BF16)) * decay[k, :, at]
                if c < n - 1:
                    state[:, at] = old * decay[k, rows - 1 :, at] + grown[k, :, at]
            else:
                state[:, at] = grown[k, :, at]
            gated = out * gates[k, :, at]
            squares += jnp.sum(gated * gated, axis=-1, keepdims=True)
            of_part = dot((gated * gate_g[0:1, at]).astype(BF16), w_out_one[at, :])
            update = of_part if update is None else update + of_part
        scale = jnp.broadcast_to(lax.rsqrt(squares * (1.0 / inner) + EPS), (rows, 128))
        factor = jnp.where(row < valid_one[k][0:1], scale, 0.0)
        factor = jnp.concatenate([factor] * (width // 128), axis=1)
        new = (x_one[k].astype(F32) + update * factor).astype(BF16)
        x_two[dest[k]] = new
        normed_two[dest[k]] = normalise(new, norm_g[1:2, :])

    own_x[...] = x_two[me]
    own_live[...] = jnp.where(row < valid_two[me][0:1], 1.0, 0.0)
    normed = normed_two[...].reshape(n * rows, width)
    steps, to_end, running = head_steps(
        normed, [valid_two[c][0:1, 0:1] for c in range(n)], w_dt[1], bias[1:2, :], rate[1:2, :]
    )
    bc = silu(dot(normed, w_bc[1])).astype(BF16)
    copies[1].wait()
    at = pl.ds(pl.multiple_of(me * part, 128), part)
    value = silu(dot(normed, w_two[:, at])).astype(BF16).astype(F32)
    after = jnp.zeros((heads, 1), F32)
    suffixes = [None] * n
    for c in reversed(range(n)):
        suffixes[c] = after
        after = after + running[c * heads : (c + 1) * heads, rows - 1 :]
    whole = jnp.broadcast_to(after, (heads, rows))
    turned = [
        by_rows(to_end[c * heads : (c + 1) * heads] * jnp.exp2(suffixes[c]), whole).astype(BF16) for c in range(n)
    ]
    to_end_x = dot(jnp.concatenate(turned, axis=0), spread[:, at])
    fall = dot(turned[0][:16], spread[:, pl.ds(pl.multiple_of(inner + me * part, 128), part)])[0:1]
    send[:key_width] = dot(turn(bc[:, :key_width]), (value * to_end_x).astype(BF16)).astype(BF16)
    send[key_width:] = decay_rows(fall)
    seen = seen_from(steps, running)
    for c in range(n):
        chunk, of = slice(c * rows, (c + 1) * rows), slice(c * heads, (c + 1) * heads)
        key_two[c] = bc[chunk, :key_width]
        queries[c] = bc[chunk, key_width:]
        to_end_two[c] = to_end[of]
        running_two[c] = running[of]
        seen_two[c] = seen[of]
    own_query[...] = queries[me]
    copies[2].wait()


def own_kernel(
    normed_two, key_two, query, to_end_two, running_two, seen_two, spread, skip, w_xz, local, gate, decay
):
    me = lax.axis_index("curve")
    inner = local.shape[1]
    heads = seen_two.shape[1]
    normed = normed_two[me]
    turned = by_rows(to_end_two[me], running_two[me])
    lhs = turned.astype(BF16)
    seen = seen_two[me]
    scores = masked_scores(query[...], key_two[me])
    for j in range(0, inner, 256):
        at = slice(j, j + 256)
        value = silu(dot(normed, w_xz[:, at])).astype(BF16)
        gate[:, at] = silu(dot(normed, w_xz[:, inner + j : inner + j + 256]))
        decay[:, at] = dot(lhs, spread[:, inner + j : inner + j + 256])
        base = skip[8:9, at] * value.astype(F32)
        for k in range(2):
            half = slice(128 * k, 128 * k + 128)
            head = (j + 128 * k) * heads // inner
            local[:, j + 128 * k : j + 128 * k + 128] = (
                inside_pair(turned, seen, scores, value[:, half], head, heads) + base[:, half]
            )


def earlier_kernel(normed_two, key_two, to_end_two, running_two, spread, w_xz, state, fall):
    me = lax.axis_index("curve")
    inner = state.shape[1]
    rows = normed_two.shape[1]
    state[...] = jnp.zeros_like(state)
    fall[...] = jnp.ones_like(fall)

    def chunk(c, _):
        normed = normed_two[c]
        lhs = by_rows(to_end_two[c], running_two[c]).astype(BF16)
        key_t = turn(key_two[c])
        for j in range(0, inner, 256):
            at = slice(j, j + 256)
            value = silu(dot(normed, w_xz[:, at])).astype(BF16).astype(F32)
            weighted = value * dot(lhs, spread[:, at])
            end_x = dot(lhs[rows - 16 :], spread[:, inner + j : inner + j + 256])[15:16]
            state[:, at] = state[:, at] * end_x + dot(key_t, weighted.astype(BF16))
            fall[:, at] = fall[:, at] * end_x
        return 0

    lax.fori_loop(0, me, chunk, 0)


def decay_rows(fall):
    high, low = split(fall)
    lines = iota((EXTRA, fall.shape[1]), 0)
    return jnp.where(lines == 0, high, jnp.where(lines == 1, low, 0.0)).astype(BF16)


def state_and_decay(ordered, u):
    states = ordered.shape[1] - EXTRA
    tail = ordered[u, states:].astype(F32)
    return ordered[u, :states].astype(F32), tail[0:1] + tail[1:2]


def join_kernel(radix, stride, last, *refs):
    deeper = stride > 1
    parts, before = refs[:radix], refs[radix] if deeper else None
    outs, ordered = refs[radix + 1 + deeper : -1], refs[-1]
    me = lax.rem(lax.div(lax.axis_index("tile"), stride), radix)
    states, width = parts[0].shape[0] - EXTRA, parts[0].shape[1]
    for k in range(radix):
        ordered[me ^ k] = parts[k][...]
    earlier = (jnp.zeros((states, width), F32), jnp.ones((1, width), F32))
    whole = None
    for u in range(radix if not last else radix - 1):
        one, fall = state_and_decay(ordered, u)
        if u < radix - 1:
            took = jnp.where(me > u, 1.0, 0.0)
            keep = jnp.where(me > u, fall, 1.0)
            earlier = (earlier[0] * keep + one * took, earlier[1] * keep)
        if not last:
            whole = (one, fall) if u == 0 else (whole[0] * fall + one, whole[1] * fall)
    state, fall = earlier
    if deeper:
        state = state * before[states : states + 1] + before[:states]
        fall = fall * before[states : states + 1]
    if last:
        outs[0][...] = state.astype(BF16)
        return
    outs[0][:states] = state
    outs[0][states:] = jnp.broadcast_to(fall, (8, width))
    outs[1][:states] = whole[0].astype(BF16)
    outs[1][states:] = decay_rows(whole[1])


def end_kernel(ks, first, final, *refs):
    pieces, refs = refs[: len(ks)], refs[len(ks) :]
    local, gate, query, decay, earlier, fall, gate_g, w_out = refs[:8]
    me = lax.axis_index("curve")
    rows, inner = local.shape
    part = pieces[0].shape[1]
    squares = jnp.zeros((rows, 1), F32)
    update = None
    for k, piece in zip(ks, pieces):
        at = pl.ds(pl.multiple_of((me ^ k) * part, 128), part)
        state = piece[...].astype(F32) * fall[0:1, at] + earlier[:, at]
        head_out = dot(query[...], state.astype(BF16)) * decay[:, at] + local[:, at]
        gated = head_out * gate[:, at]
        squares += jnp.sum(gated * gated, axis=-1, keepdims=True)
        of_part = dot((gated * gate_g[1:2, at]).astype(BF16), w_out[at, :])
        update = of_part if update is None else update + of_part
    refs = refs[8:]
    squares = jnp.broadcast_to(squares, (rows, 128))
    if not first:
        update, squares, refs = update + refs[0][...], squares + refs[1][...], refs[2:]
    if not final:
        refs[0][...] = update
        refs[1][...] = squares
        return
    x, live, out = refs
    factor = live[...] * lax.rsqrt(squares * (1.0 / inner) + EPS)
    for j in range(0, x.shape[1], 128):
        at = slice(j, j + 128)
        out[0, :, at] = (x[:, at].astype(F32) + factor * update[:, at]).astype(BF16)


def call(kernel, outs, scratch, *args, in_hbm=(), free=(), aliases={}, out_fixed=True):
    vmem = pl.BlockSpec(memory_space=pltpu.VMEM)
    spaces = [pltpu.HBM if i in in_hbm else pltpu.VMEM for i in range(len(args))]
    spaces = [pltpu.SMEM if i in free else space for i, space in enumerate(spaces)]
    args = [
        arg if space == pltpu.SMEM else pltpu.with_memory_space_constraint(arg, space)
        for arg, space in zip(args, spaces)
    ]
    return pl.pallas_call(
        kernel,
        out_shape=[(pltpu.VMEM if out_fixed else jax.ShapeDtypeStruct)(shape, kind) for shape, kind in outs],
        in_specs=[pl.BlockSpec(memory_space=space) for space in spaces],
        out_specs=[vmem] * len(outs),
        scratch_shapes=scratch,
        input_output_aliases=aliases,
        compiler_params=pltpu.CompilerParams(vmem_limit_bytes=VMEM_BYTES),
    )(*args)


def swap(value, axis, mask, size):
    return lax.ppermute(value, axis, [(i, i ^ mask) for i in range(size)])


def levels(size):
    steps, stride = [], 1
    while stride < size:
        radix = 4 if size // stride >= 4 else 2
        steps.append((radix, stride))
        stride *= radix
    return steps


def local(
    tiles,
    points,
    valid_rows,
    dest_shard,
    dest_slot,
    norm_gain,
    w_xz,
    w_bc,
    w_dt,
    dt_bias,
    decay_rate,
    skip_gain,
    gate_gain,
    w_out,
):
    n = lax.axis_size("curve")
    rows, width = points.shape[1:]
    heads, inner, key_width = w_dt.shape[2], w_out.shape[1], w_bc.shape[2] // 2
    part = inner // n
    params = (norm_gain, w_bc, jnp.swapaxes(w_dt, 1, 2), dt_bias, decay_rate, skip_gain, gate_gain)
    packed, norm_gain, w_bc, w_dt, dt_bias, decay_rate, skip_gain, gate_gain = call(
        functools.partial(pack_kernel, len(params)),
        [((rows + EXTRA, width), BF16)] + [(p.shape, p.dtype) for p in params],
        [pltpu.SemaphoreType.DMA((len(params) + 1,))],
        points,
        valid_rows,
        dest_shard,
        dest_slot,
        *params,
        in_hbm=(0, *range(4, 4 + len(params))),
        free=(1, 2, 3),
    )
    pieces = [packed] + [None] * (n - 1)
    for k in range(2, n, 2):
        pieces[k] = swap(packed, "curve", k, n)
    pieces[1] = swap(packed, "curve", 1, n)
    work = [
        ((n, rows, inner), F32),
        ((n, rows, inner), F32),
        ((n, rows, inner), F32),
        ((n, key_width, inner), F32),
        ((n, rows, key_width), BF16),
    ]
    w_held, spread, skip, *done = call(
        begin_kernel,
        [(w_xz.shape[1:], BF16), ((128, 2 * inner), BF16), ((8 * skip_gain.shape[0], inner), F32)] + work,
        [pltpu.SemaphoreType.DMA],
        packed,
        norm_gain,
        w_bc,
        w_dt,
        dt_bias,
        decay_rate,
        skip_gain,
        w_xz,
        in_hbm=(7,),
    )
    shared = (norm_gain, w_held, w_bc, w_dt, dt_bias, decay_rate, spread, skip)
    aliases = {10 + i: i for i in range(5)}
    done = call(functools.partial(piece_kernel, 1), work, [], pieces[1], packed, *shared, *done, aliases=aliases)
    for k in range(3, n, 2):
        (passed,) = call(relay_kernel, [(packed.shape, BF16)], [], pieces[k - 1], done[4])
        pieces[k] = swap(passed, "curve", 1, n)
    done = call(functools.partial(piece_kernel, 2), work, [], pieces[2], passed, *shared, *done, aliases=aliases)
    first = n + 11
    got = call(
        functools.partial(tile_kernel, n),
        work
        + [
            (w_xz.shape[1:], BF16),
            (w_out.shape[1:], BF16),
            ((key_width + EXTRA, part), BF16),
            ((rows, width), BF16),
            ((rows, 128), F32),
            ((n, rows, width), BF16),
            ((n, rows, key_width), BF16),
            ((rows, key_width), BF16),
            ((n, heads, rows), F32),
            ((n, heads, rows), F32),
            ((n, heads, rows), F32),
        ],
        [
            pltpu.VMEM(w_out.shape[1:], BF16),
            pltpu.VMEM((n, rows, width), BF16),
            pltpu.VMEM((n, rows, width), BF16),
            pltpu.VMEM((n, 8, 128), F32),
            pltpu.VMEM((n, 8, 128), F32),
            pltpu.VMEM((key_width, inner), F32),
            pltpu.SMEM((n,), jnp.int32),
            pltpu.SemaphoreType.DMA((3,)),
        ],
        *pieces,
        *shared,
        gate_gain,
        w_xz,
        w_out,
        *done,
        in_hbm=(first - 2, first - 1),
        aliases={first + i: i for i in range(5)},
    )
    w_two, w_out_two, send, own_x, own_live, normed_two, key_two, own_query = got[5:13]
    to_end_two, running_two, seen_two = got[13:]
    own, gate, decay = call(
        own_kernel,
        [((rows, inner), F32)] * 3,
        [],
        normed_two,
        key_two,
        own_query,
        to_end_two,
        running_two,
        seen_two,
        spread,
        skip,
        w_two,
    )
    earlier, fall = call(
        earlier_kernel,
        [((key_width, inner), F32), ((8, inner), F32)],
        [],
        normed_two,
        key_two,
        to_end_two,
        running_two,
        spread,
        w_two,
    )
    before = []
    steps = levels(tiles)
    for i, (radix, stride) in enumerate(steps):
        last = i == len(steps) - 1
        parts = [send] + [swap(send, "tile", k * stride, tiles) for k in range(1, radix)]
        outs = [((key_width, part), BF16)]
        if not last:
            outs = [((key_width + 8, part), F32), ((key_width + EXTRA, part), BF16)]
        got = call(
            functools.partial(join_kernel, radix, stride, last),
            outs,
            [pltpu.VMEM((radix, key_width + EXTRA, part), BF16)],
            *parts,
            *before,
            fall if last else decay,
        )
        if not last:
            before, send = [got[0]], got[1]
    incoming = got[0]
    states = [incoming] + [swap(incoming, "curve", k, n) for k in range(1, n)]
    common = (own, gate, own_query, decay, earlier, fall, gate_gain, w_out_two)
    partial = []
    for ks in ([0, 1], list(range(3, n))):
        partial = call(
            functools.partial(end_kernel, ks, not partial, False),
            [((rows, width), F32), ((rows, 128), F32)],
            [],
            *[states[k] for k in ks],
            *common,
            *partial,
        )
    (out,) = call(
        functools.partial(end_kernel, [2], False, True),
        [((1, rows, width), BF16)],
        [],
        states[2],
        *common,
        *partial,
        own_x,
        own_live,
        out_fixed=False,
    )
    return out


def solution(mesh):
    in_specs = (
        P("tile", "curve", None),
        P("tile", "curve"),
        P("tile", "curve", None),
        P("tile", "curve", None),
    ) + (P(),) * 9
    return jax.shard_map(
        functools.partial(local, mesh.shape["tile"]),
        mesh=mesh,
        in_specs=in_specs,
        out_specs=P("tile", "curve", None),
        check_vma=False,
    )
```

```python
import functools

import jax
import jax.numpy as jnp
from jax import lax
from jax.experimental import pallas as pl
from jax.experimental.pallas import tpu as pltpu
from jax.sharding import PartitionSpec as P

F32, BF16 = jnp.float32, jnp.bfloat16
EPS = 1e-5
LOG2E = 1.4426950408889634
EXTRA = 16
VMEM_BYTES = 20 * 1024 * 1024


def dot(a, b):
    return jnp.dot(a, b, preferred_element_type=F32)


def dot_nt(a, b):
    return lax.dot_general(a, b, (((1,), (1,)), ((), ())), preferred_element_type=F32)


def turn(x):
    return x.astype(F32).T.astype(x.dtype)


def silu(x):
    half = 0.5 * x
    return half + half * jnp.tanh(half)


def split(x):
    hi = x.astype(BF16).astype(F32)
    return hi, x - hi


def normalise(x, gain):
    wide = x.astype(F32)
    return (wide * lax.rsqrt(jnp.mean(wide * wide, axis=-1, keepdims=True) + EPS) * gain).astype(BF16)


def iota(shape, axis):
    return lax.broadcasted_iota(jnp.int32, shape, axis)


def column(row):
    heads = row.shape[1]
    same = iota((heads, heads), 0) == iota((heads, heads), 1)
    return jnp.sum(jnp.where(same, row, 0.0), axis=1, keepdims=True)


def head_steps(normed, valids, w_dt_t, bias, rate):
    heads = w_dt_t.shape[0]
    rows = normed.shape[0] // len(valids)
    raw = dot_nt(w_dt_t, normed) + column(bias)
    steps = jnp.maximum(raw, 0.0) + jnp.log1p(jnp.exp(-jnp.abs(raw)))
    lane = iota((heads, rows), 1).astype(F32)
    steps = jnp.concatenate(
        [
            jnp.where(lane < valid, steps[:, c * rows : (c + 1) * rows], 0.0)
            for c, valid in enumerate(valids)
        ],
        axis=0,
    )
    falls = -steps * jnp.concatenate([column(rate) * LOG2E] * len(valids), axis=0)
    upper = jnp.where(iota((rows, rows), 0) <= iota((rows, rows), 1), 1.0, 0.0).astype(BF16)
    high, rest = split(falls)
    middle, low = split(rest)
    running = (
        dot(high.astype(BF16), upper) + dot(middle.astype(BF16), upper) + dot(low.astype(BF16), upper)
    )
    to_end = jnp.exp2(running[:, rows - 1 : rows] - running) * steps
    return steps, to_end, running


def by_rows(to_end, running):
    parts = [*split(to_end), *split(jnp.exp2(running)), running]
    used = len(parts) * running.shape[0]
    stack = jnp.concatenate(parts + [jnp.zeros((128 - used, running.shape[1]), F32)], axis=0)
    return stack.T


def seen_from(steps, running):
    return running - jnp.where(steps > 0.0, jnp.log2(jnp.maximum(steps, 1e-37)), -1e30)


def inside_pair(turned, seen, scores, value, head, heads):
    rows = turned.shape[0]
    at = 4 * heads + head
    weights = [
        (jnp.exp2(jnp.minimum(turned[:, at + k : at + k + 1] - seen[head + k : head + k + 1], 120.0)) * scores).astype(BF16)
        for k in range(2)
    ]
    left = iota((rows, 128), 1) < 64
    zero = jnp.zeros_like(value)
    both = jnp.concatenate([jnp.where(left, value, zero), jnp.where(left, zero, value)], axis=0)
    return dot(jnp.concatenate(weights, axis=1), both)


def masked_scores(query, key):
    rows = query.shape[0]
    return jnp.where(iota((rows, rows), 0) >= iota((rows, rows), 1), dot_nt(query, key), 0.0)


def make_spread(spread, heads):
    inner = spread.shape[1] // 2
    head = lax.shift_right_logical(iota((128, inner), 1), (inner // heads).bit_length() - 1)
    row = iota((128, inner), 0)
    for g in range(2):
        hit = (row == head + 2 * heads * g) | (row == head + 2 * heads * g + heads)
        spread[:, g * inner : (g + 1) * inner] = jnp.where(hit, 1.0, 0.0).astype(BF16)


def make_skip(skip_g, spread, skip):
    layers, heads = skip_g.shape
    inner = skip.shape[1]
    for layer in range(layers):
        parts = [part for part in split(skip_g[layer : layer + 1, :])]
        row = jnp.concatenate(parts + [jnp.zeros((1, 128 - 2 * heads), F32)], axis=1)
        wide = jnp.broadcast_to(row, (16, 128)).astype(BF16)
        skip[8 * layer : 8 * layer + 8, :] = dot(wide, spread[:, :inner])[:8]


def pack_kernel(count, x, valid, shard, slot, *refs):
    sources, out, held, sems = refs[:count], refs[count], refs[count + 1 : -1], refs[-1]
    rows, width = x.shape[1:]
    copies = [pltpu.make_async_copy(x.at[0], out.at[pl.ds(0, rows)], sems.at[count])]
    copies += [pltpu.make_async_copy(a, b, sems.at[i]) for i, (a, b) in enumerate(zip(sources, held))]
    for copy in copies:
        copy.start()
    line, lane = iota((EXTRA, width), 0), iota((EXTRA, width), 1)
    live = valid[0, 0].astype(F32)
    place = (shard[0, 0, 0] + slot[0, 0, 0]).astype(F32)
    first = jnp.where(lane == 0, live, jnp.where(lane == 1, place, 0.0))
    out[rows:] = jnp.where(line == 0, first, 0.0).astype(BF16)
    for copy in copies:
        copy.wait()


def live_count(packed):
    at = packed.shape[0] - EXTRA
    return packed[at:, :128].astype(F32)[0:1, 0:1]


def place_of(packed):
    extra = packed[packed.shape[0] - EXTRA :, :128].astype(F32)
    hit = (iota((EXTRA, 128), 0) == 0) & (iota((EXTRA, 128), 1) == 1)
    return jnp.sum(jnp.where(hit, extra, 0.0)).astype(jnp.int32)


def block_of(packed):
    return packed[: packed.shape[0] - EXTRA]


def pieces_work(xs, valids, slots, params, work, ready=lambda: None):
    norm_g, w_xz, w_bc, w_dt, bias, rate, spread, skip = params
    gates, local, decay, grown, queries = work
    rows = xs[0].shape[0]
    heads, inner, key_width = w_dt.shape[1], w_xz.shape[1] // 2, w_bc.shape[2] // 2
    normed = normalise(jnp.concatenate(xs, axis=0), norm_g[0:1, :])
    bc = silu(dot(normed, w_bc[0])).astype(BF16)
    steps, to_end, running = head_steps(normed, valids, w_dt[0], bias[0:1, :], rate[0:1, :])
    seen = seen_from(steps, running)
    parts = []
    for i, slot in enumerate(slots):
        at, of = slice(i * rows, (i + 1) * rows), slice(i * heads, (i + 1) * heads)
        key, query = bc[at, :key_width], bc[at, key_width:]
        queries[slot] = query
        turned = by_rows(to_end[of], running[of])
        parts.append((slot, at, turned, turned.astype(BF16), seen[of], masked_scores(query, key), turn(key)))
    ready()
    for j in range(0, inner, 256):
        cols, ends = slice(j, j + 256), slice(inner + j, inner + j + 256)
        values = silu(dot(normed, w_xz[:, cols])).astype(BF16)
        gate = silu(dot(normed, w_xz[:, ends]))
        for slot, at, turned, lhs, seen_here, scores, key_t in parts:
            value = values[at]
            wide = value.astype(F32)
            gates[slot, :, cols] = gate[at]
            decay[slot, :, cols] = dot(lhs, spread[:, ends])
            grown[slot, :, cols] = dot(key_t, (wide * dot(lhs, spread[:, cols])).astype(BF16))
            base = skip[0:1, cols] * wide
            for k in range(2):
                half = slice(128 * k, 128 * k + 128)
                head = (j + 128 * k) * heads // inner
                local[slot, :, j + 128 * k : j + 128 * k + 128] = (
                    inside_pair(turned, seen_here, scores, value[:, half], head, heads) + base[:, half]
                )


def begin_kernel(packed, norm_g, w_bc, w_dt, bias, rate, skip_g, w_xz, w_held, spread, skip, *refs):
    work, sem = refs[:-1], refs[-1]
    copy = pltpu.make_async_copy(w_xz.at[0], w_held, sem)
    copy.start()
    make_spread(spread, w_dt.shape[1])
    make_skip(skip_g, spread, skip)
    params = (norm_g, w_held, w_bc, w_dt, bias, rate, spread, skip)
    pieces_work([block_of(packed)], [live_count(packed)], [0], params, work, copy.wait)


def piece_kernel(slot, packed, late, *refs):
    pieces_work([block_of(packed)], [live_count(packed)], [slot], refs[:8], refs[-5:])


def relay_kernel(x, *refs):
    refs[-1][...] = x[...]


def tile_kernel(n, *refs):
    pieces, refs = refs[:n], refs[n:]
    norm_g, w_held, w_bc, w_dt, bias, rate, spread, skip, gate_g, w_xz, w_out = refs[:11]
    refs = refs[16:]
    work, refs = refs[:5], refs[5:]
    (
        w_two,
        w_out_two,
        send,
        x_two,
        valid_two,
        normed_two,
        bc_two,
        steps_two,
        to_end_two,
        running_two,
        w_out_one,
        x_one,
        valid_one,
        state,
        dest,
        sems,
    ) = refs
    gates, local, decay, grown, queries = work
    me = lax.axis_index("curve")
    rows, width = x_two.shape[1:]
    heads = w_dt.shape[1]
    inner = w_out.shape[1]
    key_width = w_bc.shape[2] // 2
    part = inner // n
    copies = [
        pltpu.make_async_copy(w_out.at[0], w_out_one, sems.at[0]),
        pltpu.make_async_copy(w_xz.at[1], w_two, sems.at[1]),
        pltpu.make_async_copy(w_out.at[1], w_out_two, sems.at[2]),
    ]
    for copy in copies:
        copy.start()
    valid = [live_count(piece) for piece in pieces]
    xs = [block_of(piece) for piece in pieces]
    for k in range(n):
        x_one[k] = xs[k]
        dest[k] = place_of(pieces[k])
        valid_one[k] = jnp.broadcast_to(valid[k], (8, 128))
        valid_two[dest[k]] = jnp.broadcast_to(valid[k], (8, 128))
    params = (norm_g, w_held, w_bc, w_dt, bias, rate, spread, skip)
    pieces_work(xs[3:], valid[3:], list(range(3, n)), params, work)

    copies[0].wait()
    row = iota((rows, 128), 0).astype(F32)
    for c in range(n):
        k = me ^ c
        query = queries[k]
        squares = jnp.zeros((rows, 1), F32)
        update = None
        for j in range(0, inner, 256):
            at = slice(j, j + 256)
            out = local[k, :, at]
            if c:
                old = state[:, at]
                out += dot(query, old.astype(BF16)) * decay[k, :, at]
                if c < n - 1:
                    state[:, at] = old * decay[k, rows - 1 :, at] + grown[k, :, at]
            else:
                state[:, at] = grown[k, :, at]
            gated = out * gates[k, :, at]
            squares += jnp.sum(gated * gated, axis=-1, keepdims=True)
            of_part = dot((gated * gate_g[0:1, at]).astype(BF16), w_out_one[at, :])
            update = of_part if update is None else update + of_part
        scale = jnp.broadcast_to(lax.rsqrt(squares * (1.0 / inner) + EPS), (rows, 128))
        factor = jnp.where(row < valid_one[k][0:1], scale, 0.0)
        factor = jnp.concatenate([factor] * (width // 128), axis=1)
        new = (x_one[k].astype(F32) + update * factor).astype(BF16)
        x_two[dest[k]] = new
        normed_two[dest[k]] = normalise(new, norm_g[1:2, :])

    normed = normed_two[...].reshape(n * rows, width)
    steps, to_end, running = head_steps(
        normed, [valid_two[c][0:1, 0:1] for c in range(n)], w_dt[1], bias[1:2, :], rate[1:2, :]
    )
    for c in range(n):
        of = slice(c * heads, (c + 1) * heads)
        steps_two[c] = steps[of]
        to_end_two[c] = to_end[of]
        running_two[c] = running[of]
    bc = silu(dot(normed, w_bc[1])).astype(BF16)
    bc_two[...] = bc.reshape(n, rows, 2 * key_width)
    copies[1].wait()
    at = pl.ds(pl.multiple_of(me * part, 128), part)
    value = silu(dot(normed, w_two[:, at])).astype(BF16).astype(F32)
    after = jnp.zeros((heads, 1), F32)
    suffixes = [None] * n
    for c in reversed(range(n)):
        suffixes[c] = after
        after = after + running[c * heads : (c + 1) * heads, rows - 1 :]
    whole = jnp.broadcast_to(after, (heads, rows))
    turned = [
        by_rows(to_end[c * heads : (c + 1) * heads] * jnp.exp2(suffixes[c]), whole).astype(BF16) for c in range(n)
    ]
    to_end_x = dot(jnp.concatenate(turned, axis=0), spread[:, at])
    fall = dot(turned[0][:16], spread[:, pl.ds(pl.multiple_of(inner + me * part, 128), part)])[0:1]
    send[:key_width] = dot(turn(bc[:, :key_width]), (value * to_end_x).astype(BF16)).astype(BF16)
    send[key_width:] = decay_rows(fall)
    copies[2].wait()


def own_kernel(
    normed_two, bc_two, steps_two, to_end_two, running_two, spread, skip, w_xz, local, gate, decay, query_out
):
    me = lax.axis_index("curve")
    inner = local.shape[1]
    heads = steps_two.shape[1]
    key_width = query_out.shape[1]
    normed = normed_two[me]
    turned = by_rows(to_end_two[me], running_two[me])
    lhs = turned.astype(BF16)
    seen = seen_from(steps_two[me], running_two[me])
    bc = bc_two[me]
    query_out[...] = bc[:, key_width:]
    scores = masked_scores(bc[:, key_width:], bc[:, :key_width])
    for j in range(0, inner, 256):
        at = slice(j, j + 256)
        value = silu(dot(normed, w_xz[:, at])).astype(BF16)
        gate[:, at] = silu(dot(normed, w_xz[:, inner + j : inner + j + 256]))
        decay[:, at] = dot(lhs, spread[:, inner + j : inner + j + 256])
        base = skip[8:9, at] * value.astype(F32)
        for k in range(2):
            half = slice(128 * k, 128 * k + 128)
            head = (j + 128 * k) * heads // inner
            local[:, j + 128 * k : j + 128 * k + 128] = (
                inside_pair(turned, seen, scores, value[:, half], head, heads) + base[:, half]
            )


def earlier_kernel(normed_two, bc_two, to_end_two, running_two, spread, w_xz, state, fall):
    me = lax.axis_index("curve")
    inner = state.shape[1]
    rows = normed_two.shape[1]
    state[...] = jnp.zeros_like(state)
    fall[...] = jnp.ones_like(fall)

    def chunk(c, _):
        normed = normed_two[c]
        lhs = by_rows(to_end_two[c], running_two[c]).astype(BF16)
        key_t = turn(bc_two[c][:, : state.shape[0]])
        for j in range(0, inner, 256):
            at = slice(j, j + 256)
            value = silu(dot(normed, w_xz[:, at])).astype(BF16).astype(F32)
            weighted = value * dot(lhs, spread[:, at])
            end_x = dot(lhs[rows - 16 :], spread[:, inner + j : inner + j + 256])[15:16]
            state[:, at] = state[:, at] * end_x + dot(key_t, weighted.astype(BF16))
            fall[:, at] = fall[:, at] * end_x
        return 0

    lax.fori_loop(0, me, chunk, 0)


def decay_rows(fall):
    high, low = split(fall)
    lines = iota((EXTRA, fall.shape[1]), 0)
    return jnp.where(lines == 0, high, jnp.where(lines == 1, low, 0.0)).astype(BF16)


def state_and_decay(ordered, u):
    states = ordered.shape[1] - EXTRA
    tail = ordered[u, states:].astype(F32)
    return ordered[u, :states].astype(F32), tail[0:1] + tail[1:2]


def join_kernel(radix, stride, last, *refs):
    deeper = stride > 1
    parts, before = refs[:radix], refs[radix] if deeper else None
    outs, ordered = refs[radix + 1 + deeper : -1], refs[-1]
    me = lax.rem(lax.div(lax.axis_index("tile"), stride), radix)
    states, width = parts[0].shape[0] - EXTRA, parts[0].shape[1]
    for k in range(radix):
        ordered[me ^ k] = parts[k][...]
    earlier = (jnp.zeros((states, width), F32), jnp.ones((1, width), F32))
    whole = None
    for u in range(radix if not last else radix - 1):
        one, fall = state_and_decay(ordered, u)
        if u < radix - 1:
            took = jnp.where(me > u, 1.0, 0.0)
            keep = jnp.where(me > u, fall, 1.0)
            earlier = (earlier[0] * keep + one * took, earlier[1] * keep)
        if not last:
            whole = (one, fall) if u == 0 else (whole[0] * fall + one, whole[1] * fall)
    state, fall = earlier
    if deeper:
        state = state * before[states : states + 1] + before[:states]
        fall = fall * before[states : states + 1]
    if last:
        outs[0][...] = state.astype(BF16)
        return
    outs[0][:states] = state
    outs[0][states:] = jnp.broadcast_to(fall, (8, width))
    outs[1][:states] = whole[0].astype(BF16)
    outs[1][states:] = decay_rows(whole[1])


def end_kernel(ks, first, final, *refs):
    pieces, refs = refs[: len(ks)], refs[len(ks) :]
    local, gate, query, decay, earlier, fall, gate_g, w_out = refs[:8]
    me = lax.axis_index("curve")
    rows, inner = local.shape
    part = pieces[0].shape[1]
    squares = jnp.zeros((rows, 1), F32)
    update = None
    for k, piece in zip(ks, pieces):
        at = pl.ds(pl.multiple_of((me ^ k) * part, 128), part)
        state = piece[...].astype(F32) * fall[0:1, at] + earlier[:, at]
        head_out = dot(query[...], state.astype(BF16)) * decay[:, at] + local[:, at]
        gated = head_out * gate[:, at]
        squares += jnp.sum(gated * gated, axis=-1, keepdims=True)
        of_part = dot((gated * gate_g[1:2, at]).astype(BF16), w_out[at, :])
        update = of_part if update is None else update + of_part
    refs = refs[8:]
    squares = jnp.broadcast_to(squares, (rows, 128))
    if not first:
        update, squares, refs = update + refs[0][...], squares + refs[1][...], refs[2:]
    if not final:
        refs[0][...] = update
        refs[1][...] = squares
        return
    x_two, valid_two, out = refs
    live = iota((rows, 128), 0).astype(F32) < valid_two[me][0:1]
    factor = jnp.where(live, lax.rsqrt(squares * (1.0 / inner) + EPS), 0.0)
    x = x_two[me]
    for j in range(0, x.shape[1], 128):
        at = slice(j, j + 128)
        out[0, :, at] = (x[:, at].astype(F32) + factor * update[:, at]).astype(BF16)


def call(kernel, outs, scratch, *args, in_hbm=(), free=(), aliases={}, out_fixed=True):
    vmem = pl.BlockSpec(memory_space=pltpu.VMEM)
    spaces = [pltpu.HBM if i in in_hbm else pltpu.VMEM for i in range(len(args))]
    spaces = [pltpu.SMEM if i in free else space for i, space in enumerate(spaces)]
    args = [
        arg if space == pltpu.SMEM else pltpu.with_memory_space_constraint(arg, space)
        for arg, space in zip(args, spaces)
    ]
    return pl.pallas_call(
        kernel,
        out_shape=[(pltpu.VMEM if out_fixed else jax.ShapeDtypeStruct)(shape, kind) for shape, kind in outs],
        in_specs=[pl.BlockSpec(memory_space=space) for space in spaces],
        out_specs=[vmem] * len(outs),
        scratch_shapes=scratch,
        input_output_aliases=aliases,
        compiler_params=pltpu.CompilerParams(vmem_limit_bytes=VMEM_BYTES),
    )(*args)


def swap(value, axis, mask, size):
    return lax.ppermute(value, axis, [(i, i ^ mask) for i in range(size)])


def levels(size):
    steps, stride = [], 1
    while stride < size:
        radix = 4 if size // stride >= 4 else 2
        steps.append((radix, stride))
        stride *= radix
    return steps


def local(
    tiles,
    points,
    valid_rows,
    dest_shard,
    dest_slot,
    norm_gain,
    w_xz,
    w_bc,
    w_dt,
    dt_bias,
    decay_rate,
    skip_gain,
    gate_gain,
    w_out,
):
    n = lax.axis_size("curve")
    rows, width = points.shape[1:]
    heads, inner, key_width = w_dt.shape[2], w_out.shape[1], w_bc.shape[2] // 2
    part = inner // n
    params = (norm_gain, w_bc, jnp.swapaxes(w_dt, 1, 2), dt_bias, decay_rate, skip_gain, gate_gain)
    packed, norm_gain, w_bc, w_dt, dt_bias, decay_rate, skip_gain, gate_gain = call(
        functools.partial(pack_kernel, len(params)),
        [((rows + EXTRA, width), BF16)] + [(p.shape, p.dtype) for p in params],
        [pltpu.SemaphoreType.DMA((len(params) + 1,))],
        points,
        valid_rows,
        dest_shard,
        dest_slot,
        *params,
        in_hbm=(0, *range(4, 4 + len(params))),
        free=(1, 2, 3),
    )
    pieces = [packed] + [None] * (n - 1)
    for k in range(2, n, 2):
        pieces[k] = swap(packed, "curve", k, n)
    pieces[1] = swap(packed, "curve", 1, n)
    work = [
        ((n, rows, inner), F32),
        ((n, rows, inner), F32),
        ((n, rows, inner), F32),
        ((n, key_width, inner), F32),
        ((n, rows, key_width), BF16),
    ]
    w_held, spread, skip, *done = call(
        begin_kernel,
        [(w_xz.shape[1:], BF16), ((128, 2 * inner), BF16), ((8 * skip_gain.shape[0], inner), F32)] + work,
        [pltpu.SemaphoreType.DMA],
        packed,
        norm_gain,
        w_bc,
        w_dt,
        dt_bias,
        decay_rate,
        skip_gain,
        w_xz,
        in_hbm=(7,),
    )
    shared = (norm_gain, w_held, w_bc, w_dt, dt_bias, decay_rate, spread, skip)
    aliases = {10 + i: i for i in range(5)}
    done = call(functools.partial(piece_kernel, 1), work, [], pieces[1], packed, *shared, *done, aliases=aliases)
    for k in range(3, n, 2):
        (passed,) = call(relay_kernel, [(packed.shape, BF16)], [], pieces[k - 1], done[4])
        pieces[k] = swap(passed, "curve", 1, n)
    done = call(functools.partial(piece_kernel, 2), work, [], pieces[2], passed, *shared, *done, aliases=aliases)
    first = n + 11
    got = call(
        functools.partial(tile_kernel, n),
        work
        + [
            (w_xz.shape[1:], BF16),
            (w_out.shape[1:], BF16),
            ((key_width + EXTRA, part), BF16),
            ((n, rows, width), BF16),
            ((n, 8, 128), F32),
            ((n, rows, width), BF16),
            ((n, rows, 2 * key_width), BF16),
            ((n, heads, rows), F32),
            ((n, heads, rows), F32),
            ((n, heads, rows), F32),
        ],
        [
            pltpu.VMEM(w_out.shape[1:], BF16),
            pltpu.VMEM((n, rows, width), BF16),
            pltpu.VMEM((n, 8, 128), F32),
            pltpu.VMEM((key_width, inner), F32),
            pltpu.SMEM((n,), jnp.int32),
            pltpu.SemaphoreType.DMA((3,)),
        ],
        *pieces,
        *shared,
        gate_gain,
        w_xz,
        w_out,
        *done,
        in_hbm=(first - 2, first - 1),
        aliases={first + i: i for i in range(5)},
    )
    w_two, w_out_two, send, x_two, valid_two, normed_two, bc_two, steps_two, to_end_two, running_two = got[5:]
    own, gate, decay, own_query = call(
        own_kernel,
        [((rows, inner), F32)] * 3 + [((rows, key_width), BF16)],
        [],
        normed_two,
        bc_two,
        steps_two,
        to_end_two,
        running_two,
        spread,
        skip,
        w_two,
    )
    earlier, fall = call(
        earlier_kernel,
        [((key_width, inner), F32), ((8, inner), F32)],
        [],
        normed_two,
        bc_two,
        to_end_two,
        running_two,
        spread,
        w_two,
    )
    before = []
    steps = levels(tiles)
    for i, (radix, stride) in enumerate(steps):
        last = i == len(steps) - 1
        parts = [send] + [swap(send, "tile", k * stride, tiles) for k in range(1, radix)]
        outs = [((key_width, part), BF16)]
        if not last:
            outs = [((key_width + 8, part), F32), ((key_width + EXTRA, part), BF16)]
        got = call(
            functools.partial(join_kernel, radix, stride, last),
            outs,
            [pltpu.VMEM((radix, key_width + EXTRA, part), BF16)],
            *parts,
            *before,
            fall if last else decay,
        )
        if not last:
            before, send = [got[0]], got[1]
    incoming = got[0]
    states = [incoming] + [swap(incoming, "curve", k, n) for k in range(1, n)]
    common = (own, gate, own_query, decay, earlier, fall, gate_gain, w_out_two)
    partial = []
    for ks in ([0, 1], list(range(3, n))):
        partial = call(
            functools.partial(end_kernel, ks, not partial, False),
            [((rows, width), F32), ((rows, 128), F32)],
            [],
            *[states[k] for k in ks],
            *common,
            *partial,
        )
    (out,) = call(
        functools.partial(end_kernel, [2], False, True),
        [((1, rows, width), BF16)],
        [],
        states[2],
        *common,
        *partial,
        x_two,
        valid_two,
        out_fixed=False,
    )
    return out


def solution(mesh):
    in_specs = (
        P("tile", "curve", None),
        P("tile", "curve"),
        P("tile", "curve", None),
        P("tile", "curve", None),
    ) + (P(),) * 9
    return jax.shard_map(
        functools.partial(local, mesh.shape["tile"]),
        mesh=mesh,
        in_specs=in_specs,
        out_specs=P("tile", "curve", None),
        check_vma=False,
    )
```

```python
import functools

import jax
import jax.numpy as jnp
from jax import lax
from jax.experimental import pallas as pl
from jax.experimental.pallas import tpu as pltpu
from jax.sharding import PartitionSpec as P

F32, BF16 = jnp.float32, jnp.bfloat16
EPS = 1e-5
LOG2E = 1.4426950408889634
EXTRA = 16
VMEM_BYTES = 20 * 1024 * 1024


def dot(a, b):
    return jnp.dot(a, b, preferred_element_type=F32)


def dot_nt(a, b):
    return lax.dot_general(a, b, (((1,), (1,)), ((), ())), preferred_element_type=F32)


def turn(x):
    return x.astype(F32).T.astype(x.dtype)


def silu(x):
    half = 0.5 * x
    return half + half * jnp.tanh(half)


def split(x):
    hi = x.astype(BF16).astype(F32)
    return hi, x - hi


def normalise(x, gain):
    wide = x.astype(F32)
    return (wide * lax.rsqrt(jnp.mean(wide * wide, axis=-1, keepdims=True) + EPS) * gain).astype(BF16)


def iota(shape, axis):
    return lax.broadcasted_iota(jnp.int32, shape, axis)


def column(row):
    heads = row.shape[1]
    same = iota((heads, heads), 0) == iota((heads, heads), 1)
    return jnp.sum(jnp.where(same, row, 0.0), axis=1, keepdims=True)


def head_steps(normed, valids, w_dt_t, bias, rate):
    heads = w_dt_t.shape[0]
    rows = normed.shape[0] // len(valids)
    raw = dot_nt(w_dt_t, normed) + column(bias)
    steps = jnp.maximum(raw, 0.0) + jnp.log1p(jnp.exp(-jnp.abs(raw)))
    lane = iota((heads, rows), 1).astype(F32)
    steps = jnp.concatenate(
        [
            jnp.where(lane < valid, steps[:, c * rows : (c + 1) * rows], 0.0)
            for c, valid in enumerate(valids)
        ],
        axis=0,
    )
    falls = -steps * jnp.concatenate([column(rate) * LOG2E] * len(valids), axis=0)
    upper = jnp.where(iota((rows, rows), 0) <= iota((rows, rows), 1), 1.0, 0.0).astype(BF16)
    high, rest = split(falls)
    middle, low = split(rest)
    running = (
        dot(high.astype(BF16), upper) + dot(middle.astype(BF16), upper) + dot(low.astype(BF16), upper)
    )
    to_end = jnp.exp2(running[:, rows - 1 : rows] - running) * steps
    return steps, to_end, running


def by_rows(to_end, running):
    parts = [*split(to_end), *split(jnp.exp2(running)), running]
    used = len(parts) * running.shape[0]
    stack = jnp.concatenate(parts + [jnp.zeros((128 - used, running.shape[1]), F32)], axis=0)
    return stack.T


def seen_from(steps, running):
    return running - jnp.where(steps > 0.0, jnp.log2(jnp.maximum(steps, 1e-37)), -1e30)


def inside_pair(turned, seen, scores, value, head, heads):
    rows = turned.shape[0]
    at = 4 * heads + head
    weights = [
        (jnp.exp2(jnp.minimum(turned[:, at + k : at + k + 1] - seen[head + k : head + k + 1], 120.0)) * scores).astype(BF16)
        for k in range(2)
    ]
    left = iota((rows, 128), 1) < 64
    zero = jnp.zeros_like(value)
    both = jnp.concatenate([jnp.where(left, value, zero), jnp.where(left, zero, value)], axis=0)
    return dot(jnp.concatenate(weights, axis=1), both)


def masked_scores(query, key):
    rows = query.shape[0]
    return jnp.where(iota((rows, rows), 0) >= iota((rows, rows), 1), dot_nt(query, key), 0.0)


def make_spread(spread, heads):
    inner = spread.shape[1] // 2
    head = lax.shift_right_logical(iota((128, inner), 1), (inner // heads).bit_length() - 1)
    row = iota((128, inner), 0)
    for g in range(2):
        hit = (row == head + 2 * heads * g) | (row == head + 2 * heads * g + heads)
        spread[:, g * inner : (g + 1) * inner] = jnp.where(hit, 1.0, 0.0).astype(BF16)


def make_skip(skip_g, spread, skip):
    layers, heads = skip_g.shape
    inner = skip.shape[1]
    for layer in range(layers):
        parts = [part for part in split(skip_g[layer : layer + 1, :])]
        row = jnp.concatenate(parts + [jnp.zeros((1, 128 - 2 * heads), F32)], axis=1)
        wide = jnp.broadcast_to(row, (16, 128)).astype(BF16)
        skip[8 * layer : 8 * layer + 8, :] = dot(wide, spread[:, :inner])[:8]


def pack_kernel(count, x, valid, shard, slot, *refs):
    sources, out, held, sems = refs[:count], refs[count], refs[count + 1 : -1], refs[-1]
    rows, width = x.shape[1:]
    copies = [pltpu.make_async_copy(x.at[0], out.at[pl.ds(0, rows)], sems.at[count])]
    copies += [pltpu.make_async_copy(a, b, sems.at[i]) for i, (a, b) in enumerate(zip(sources, held))]
    for copy in copies:
        copy.start()
    line, lane = iota((EXTRA, width), 0), iota((EXTRA, width), 1)
    live = valid[0, 0].astype(F32)
    place = (shard[0, 0, 0] + slot[0, 0, 0]).astype(F32)
    first = jnp.where(lane == 0, live, jnp.where(lane == 1, place, 0.0))
    out[rows:] = jnp.where(line == 0, first, 0.0).astype(BF16)
    for copy in copies:
        copy.wait()


def live_count(packed):
    at = packed.shape[0] - EXTRA
    return packed[at:, :128].astype(F32)[0:1, 0:1]


def place_of(packed):
    extra = packed[packed.shape[0] - EXTRA :, :128].astype(F32)
    hit = (iota((EXTRA, 128), 0) == 0) & (iota((EXTRA, 128), 1) == 1)
    return jnp.sum(jnp.where(hit, extra, 0.0)).astype(jnp.int32)


def block_of(packed):
    return packed[: packed.shape[0] - EXTRA]


def pieces_work(xs, valids, slots, params, work, ready=lambda: None):
    norm_g, w_xz, w_bc, w_dt, bias, rate, spread, skip = params
    gates, local, decay, grown, queries = work
    rows = xs[0].shape[0]
    heads, inner, key_width = w_dt.shape[1], w_xz.shape[1] // 2, w_bc.shape[2] // 2
    normed = normalise(jnp.concatenate(xs, axis=0), norm_g[0:1, :])
    bc = silu(dot(normed, w_bc[0])).astype(BF16)
    steps, to_end, running = head_steps(normed, valids, w_dt[0], bias[0:1, :], rate[0:1, :])
    seen = seen_from(steps, running)
    parts = []
    for i, slot in enumerate(slots):
        at, of = slice(i * rows, (i + 1) * rows), slice(i * heads, (i + 1) * heads)
        key, query = bc[at, :key_width], bc[at, key_width:]
        queries[slot] = query
        turned = by_rows(to_end[of], running[of])
        parts.append((slot, at, turned, turned.astype(BF16), seen[of], masked_scores(query, key), turn(key)))
    ready()
    for j in range(0, inner, 256):
        cols, ends = slice(j, j + 256), slice(inner + j, inner + j + 256)
        values = silu(dot(normed, w_xz[:, cols])).astype(BF16)
        gate = silu(dot(normed, w_xz[:, ends]))
        for slot, at, turned, lhs, seen_here, scores, key_t in parts:
            value = values[at]
            wide = value.astype(F32)
            gates[slot, :, cols] = gate[at]
            decay[slot, :, cols] = dot(lhs, spread[:, ends])
            grown[slot, :, cols] = dot(key_t, (wide * dot(lhs, spread[:, cols])).astype(BF16))
            base = skip[0:1, cols] * wide
            for k in range(2):
                half = slice(128 * k, 128 * k + 128)
                head = (j + 128 * k) * heads // inner
                local[slot, :, j + 128 * k : j + 128 * k + 128] = (
                    inside_pair(turned, seen_here, scores, value[:, half], head, heads) + base[:, half]
                )


def begin_kernel(packed, norm_g, w_bc, w_dt, bias, rate, skip_g, w_xz, w_held, spread, skip, *refs):
    work, sem = refs[:-1], refs[-1]
    copy = pltpu.make_async_copy(w_xz.at[0], w_held, sem)
    copy.start()
    make_spread(spread, w_dt.shape[1])
    make_skip(skip_g, spread, skip)
    params = (norm_g, w_held, w_bc, w_dt, bias, rate, spread, skip)
    pieces_work([block_of(packed)], [live_count(packed)], [0], params, work, copy.wait)


def piece_kernel(slot, layers, packed, late, *refs):
    held, sem = refs[-2:]
    copy = pltpu.make_async_copy(refs[13].at[layers], held, sem)
    copy.start()
    pieces_work([block_of(packed)], [live_count(packed)], [slot], refs[:8], refs[14:19])
    copy.wait()


def relay_kernel(x, *refs):
    refs[-1][...] = x[...]


def tile_kernel(n, *refs):
    pieces, refs = refs[:n], refs[n:]
    norm_g, w_held, w_bc, w_dt, bias, rate, spread, skip, gate_g, w_two, w_out = refs[:11]
    refs = refs[16:]
    work, refs = refs[:5], refs[5:]
    (
        send,
        own_x,
        own_live,
        normed_two,
        key_two,
        own_query,
        to_end_two,
        running_two,
        seen_two,
        x_one,
        x_two,
        valid_one,
        valid_two,
        state,
        dest,
    ) = refs
    gates, local, decay, grown, queries = work
    me = lax.axis_index("curve")
    rows, width = x_two.shape[1:]
    heads = w_dt.shape[1]
    inner = w_out.shape[1]
    key_width = w_bc.shape[2] // 2
    part = inner // n
    valid = [live_count(piece) for piece in pieces]
    xs = [block_of(piece) for piece in pieces]
    for k in range(n):
        x_one[k] = xs[k]
        dest[k] = place_of(pieces[k])
        valid_one[k] = jnp.broadcast_to(valid[k], (8, 128))
        valid_two[dest[k]] = jnp.broadcast_to(valid[k], (8, 128))
    params = (norm_g, w_held, w_bc, w_dt, bias, rate, spread, skip)
    pieces_work(xs[3:], valid[3:], list(range(3, n)), params, work)

    row = iota((rows, 128), 0).astype(F32)
    for c in range(n):
        k = me ^ c
        query = queries[k]
        squares = jnp.zeros((rows, 1), F32)
        update = None
        for j in range(0, inner, 256):
            at = slice(j, j + 256)
            out = local[k, :, at]
            if c:
                old = state[:, at]
                out += dot(query, old.astype(BF16)) * decay[k, :, at]
                if c < n - 1:
                    state[:, at] = old * decay[k, rows - 1 :, at] + grown[k, :, at]
            else:
                state[:, at] = grown[k, :, at]
            gated = out * gates[k, :, at]
            squares += jnp.sum(gated * gated, axis=-1, keepdims=True)
            of_part = dot((gated * gate_g[0:1, at]).astype(BF16), w_out[0, at, :])
            update = of_part if update is None else update + of_part
        scale = jnp.broadcast_to(lax.rsqrt(squares * (1.0 / inner) + EPS), (rows, 128))
        factor = jnp.where(row < valid_one[k][0:1], scale, 0.0)
        factor = jnp.concatenate([factor] * (width // 128), axis=1)
        new = (x_one[k].astype(F32) + update * factor).astype(BF16)
        x_two[dest[k]] = new
        normed_two[dest[k]] = normalise(new, norm_g[1:2, :])

    own_x[...] = x_two[me]
    own_live[...] = jnp.where(row < valid_two[me][0:1], 1.0, 0.0)
    normed = normed_two[...].reshape(n * rows, width)
    steps, to_end, running = head_steps(
        normed, [valid_two[c][0:1, 0:1] for c in range(n)], w_dt[1], bias[1:2, :], rate[1:2, :]
    )
    bc = silu(dot(normed, w_bc[1])).astype(BF16)
    at = pl.ds(pl.multiple_of(me * part, 128), part)
    value = silu(dot(normed, w_two[:, at])).astype(BF16).astype(F32)
    after = jnp.zeros((heads, 1), F32)
    suffixes = [None] * n
    for c in reversed(range(n)):
        suffixes[c] = after
        after = after + running[c * heads : (c + 1) * heads, rows - 1 :]
    whole = jnp.broadcast_to(after, (heads, rows))
    turned = [
        by_rows(to_end[c * heads : (c + 1) * heads] * jnp.exp2(suffixes[c]), whole).astype(BF16) for c in range(n)
    ]
    to_end_x = dot(jnp.concatenate(turned, axis=0), spread[:, at])
    fall = dot(turned[0][:16], spread[:, pl.ds(pl.multiple_of(inner + me * part, 128), part)])[0:1]
    send[:key_width] = dot(turn(bc[:, :key_width]), (value * to_end_x).astype(BF16)).astype(BF16)
    send[key_width:] = decay_rows(fall)
    seen = seen_from(steps, running)
    for c in range(n):
        chunk, of = slice(c * rows, (c + 1) * rows), slice(c * heads, (c + 1) * heads)
        key_two[c] = bc[chunk, :key_width]
        queries[c] = bc[chunk, key_width:]
        to_end_two[c] = to_end[of]
        running_two[c] = running[of]
        seen_two[c] = seen[of]
    own_query[...] = queries[me]


def own_kernel(
    normed_two, key_two, query, to_end_two, running_two, seen_two, spread, skip, w_xz, local, gate, decay
):
    me = lax.axis_index("curve")
    inner = local.shape[1]
    heads = seen_two.shape[1]
    normed = normed_two[me]
    turned = by_rows(to_end_two[me], running_two[me])
    lhs = turned.astype(BF16)
    seen = seen_two[me]
    scores = masked_scores(query[...], key_two[me])
    for j in range(0, inner, 256):
        at = slice(j, j + 256)
        value = silu(dot(normed, w_xz[:, at])).astype(BF16)
        gate[:, at] = silu(dot(normed, w_xz[:, inner + j : inner + j + 256]))
        decay[:, at] = dot(lhs, spread[:, inner + j : inner + j + 256])
        base = skip[8:9, at] * value.astype(F32)
        for k in range(2):
            half = slice(128 * k, 128 * k + 128)
            head = (j + 128 * k) * heads // inner
            local[:, j + 128 * k : j + 128 * k + 128] = (
                inside_pair(turned, seen, scores, value[:, half], head, heads) + base[:, half]
            )


def earlier_kernel(normed_two, key_two, to_end_two, running_two, spread, w_xz, state, fall):
    me = lax.axis_index("curve")
    inner = state.shape[1]
    rows = normed_two.shape[1]
    state[...] = jnp.zeros_like(state)
    fall[...] = jnp.ones_like(fall)

    def chunk(c, _):
        normed = normed_two[c]
        lhs = by_rows(to_end_two[c], running_two[c]).astype(BF16)
        key_t = turn(key_two[c])
        for j in range(0, inner, 256):
            at = slice(j, j + 256)
            value = silu(dot(normed, w_xz[:, at])).astype(BF16).astype(F32)
            weighted = value * dot(lhs, spread[:, at])
            end_x = dot(lhs[rows - 16 :], spread[:, inner + j : inner + j + 256])[15:16]
            state[:, at] = state[:, at] * end_x + dot(key_t, weighted.astype(BF16))
            fall[:, at] = fall[:, at] * end_x
        return 0

    lax.fori_loop(0, me, chunk, 0)


def decay_rows(fall):
    high, low = split(fall)
    lines = iota((EXTRA, fall.shape[1]), 0)
    return jnp.where(lines == 0, high, jnp.where(lines == 1, low, 0.0)).astype(BF16)


def state_and_decay(ordered, u):
    states = ordered.shape[1] - EXTRA
    tail = ordered[u, states:].astype(F32)
    return ordered[u, :states].astype(F32), tail[0:1] + tail[1:2]


def join_kernel(radix, stride, last, *refs):
    deeper = stride > 1
    parts, before = refs[:radix], refs[radix] if deeper else None
    outs, ordered = refs[radix + 1 + deeper : -1], refs[-1]
    me = lax.rem(lax.div(lax.axis_index("tile"), stride), radix)
    states, width = parts[0].shape[0] - EXTRA, parts[0].shape[1]
    for k in range(radix):
        ordered[me ^ k] = parts[k][...]
    earlier = (jnp.zeros((states, width), F32), jnp.ones((1, width), F32))
    whole = None
    for u in range(radix if not last else radix - 1):
        one, fall = state_and_decay(ordered, u)
        if u < radix - 1:
            took = jnp.where(me > u, 1.0, 0.0)
            keep = jnp.where(me > u, fall, 1.0)
            earlier = (earlier[0] * keep + one * took, earlier[1] * keep)
        if not last:
            whole = (one, fall) if u == 0 else (whole[0] * fall + one, whole[1] * fall)
    state, fall = earlier
    if deeper:
        state = state * before[states : states + 1] + before[:states]
        fall = fall * before[states : states + 1]
    if last:
        outs[0][...] = state.astype(BF16)
        return
    outs[0][:states] = state
    outs[0][states:] = jnp.broadcast_to(fall, (8, width))
    outs[1][:states] = whole[0].astype(BF16)
    outs[1][states:] = decay_rows(whole[1])


def end_kernel(ks, first, final, *refs):
    pieces, refs = refs[: len(ks)], refs[len(ks) :]
    local, gate, query, decay, earlier, fall, gate_g, w_out = refs[:8]
    me = lax.axis_index("curve")
    rows, inner = local.shape
    part = pieces[0].shape[1]
    squares = jnp.zeros((rows, 1), F32)
    update = None
    for k, piece in zip(ks, pieces):
        at = pl.ds(pl.multiple_of((me ^ k) * part, 128), part)
        state = piece[...].astype(F32) * fall[0:1, at] + earlier[:, at]
        head_out = dot(query[...], state.astype(BF16)) * decay[:, at] + local[:, at]
        gated = head_out * gate[:, at]
        squares += jnp.sum(gated * gated, axis=-1, keepdims=True)
        of_part = dot((gated * gate_g[1:2, at]).astype(BF16), w_out[1, at, :])
        update = of_part if update is None else update + of_part
    refs = refs[8:]
    squares = jnp.broadcast_to(squares, (rows, 128))
    if not first:
        update, squares, refs = update + refs[0][...], squares + refs[1][...], refs[2:]
    if not final:
        refs[0][...] = update
        refs[1][...] = squares
        return
    x, live, out = refs
    factor = live[...] * lax.rsqrt(squares * (1.0 / inner) + EPS)
    for j in range(0, x.shape[1], 128):
        at = slice(j, j + 128)
        out[0, :, at] = (x[:, at].astype(F32) + factor * update[:, at]).astype(BF16)


def call(kernel, outs, scratch, *args, in_hbm=(), free=(), aliases={}, out_fixed=True):
    vmem = pl.BlockSpec(memory_space=pltpu.VMEM)
    spaces = [pltpu.HBM if i in in_hbm else pltpu.VMEM for i in range(len(args))]
    spaces = [pltpu.SMEM if i in free else space for i, space in enumerate(spaces)]
    args = [
        arg if space == pltpu.SMEM else pltpu.with_memory_space_constraint(arg, space)
        for arg, space in zip(args, spaces)
    ]
    return pl.pallas_call(
        kernel,
        out_shape=[(pltpu.VMEM if out_fixed else jax.ShapeDtypeStruct)(shape, kind) for shape, kind in outs],
        in_specs=[pl.BlockSpec(memory_space=space) for space in spaces],
        out_specs=[vmem] * len(outs),
        scratch_shapes=scratch,
        input_output_aliases=aliases,
        compiler_params=pltpu.CompilerParams(vmem_limit_bytes=VMEM_BYTES),
    )(*args)


def swap(value, axis, mask, size):
    return lax.ppermute(value, axis, [(i, i ^ mask) for i in range(size)])


def levels(size):
    steps, stride = [], 1
    while stride < size:
        radix = 4 if size // stride >= 4 else 2
        steps.append((radix, stride))
        stride *= radix
    return steps


def local(
    tiles,
    points,
    valid_rows,
    dest_shard,
    dest_slot,
    norm_gain,
    w_xz,
    w_bc,
    w_dt,
    dt_bias,
    decay_rate,
    skip_gain,
    gate_gain,
    w_out,
):
    n = lax.axis_size("curve")
    rows, width = points.shape[1:]
    heads, inner, key_width = w_dt.shape[2], w_out.shape[1], w_bc.shape[2] // 2
    part = inner // n
    params = (norm_gain, w_bc, jnp.swapaxes(w_dt, 1, 2), dt_bias, decay_rate, skip_gain, gate_gain)
    packed, norm_gain, w_bc, w_dt, dt_bias, decay_rate, skip_gain, gate_gain = call(
        functools.partial(pack_kernel, len(params)),
        [((rows + EXTRA, width), BF16)] + [(p.shape, p.dtype) for p in params],
        [pltpu.SemaphoreType.DMA((len(params) + 1,))],
        points,
        valid_rows,
        dest_shard,
        dest_slot,
        *params,
        in_hbm=(0, *range(4, 4 + len(params))),
        free=(1, 2, 3),
    )
    pieces = [packed] + [None] * (n - 1)
    for k in range(2, n, 2):
        pieces[k] = swap(packed, "curve", k, n)
    pieces[1] = swap(packed, "curve", 1, n)
    work = [
        ((n, rows, inner), F32),
        ((n, rows, inner), F32),
        ((n, rows, inner), F32),
        ((n, key_width, inner), F32),
        ((n, rows, key_width), BF16),
    ]
    w_held, spread, skip, *done = call(
        begin_kernel,
        [(w_xz.shape[1:], BF16), ((128, 2 * inner), BF16), ((8 * skip_gain.shape[0], inner), F32)] + work,
        [pltpu.SemaphoreType.DMA],
        packed,
        norm_gain,
        w_bc,
        w_dt,
        dt_bias,
        decay_rate,
        skip_gain,
        w_xz,
        in_hbm=(7,),
    )
    shared = (norm_gain, w_held, w_bc, w_dt, dt_bias, decay_rate, spread, skip)
    aliases = {10 + i: i for i in range(5)}
    *done, w_out = call(
        functools.partial(piece_kernel, 1, pl.ds(0, w_out.shape[0])),
        work + [(w_out.shape, BF16)],
        [pltpu.SemaphoreType.DMA],
        pieces[1],
        packed,
        *shared,
        *done,
        w_out,
        in_hbm=(15,),
        aliases=aliases,
    )
    for k in range(3, n, 2):
        (passed,) = call(relay_kernel, [(packed.shape, BF16)], [], pieces[k - 1], done[4])
        pieces[k] = swap(passed, "curve", 1, n)
    *done, w_two = call(
        functools.partial(piece_kernel, 2, 1),
        work + [(w_xz.shape[1:], BF16)],
        [pltpu.SemaphoreType.DMA],
        pieces[2],
        passed,
        *shared,
        *done,
        w_xz,
        in_hbm=(15,),
        aliases=aliases,
    )
    first = n + 11
    got = call(
        functools.partial(tile_kernel, n),
        work
        + [
            ((key_width + EXTRA, part), BF16),
            ((rows, width), BF16),
            ((rows, 128), F32),
            ((n, rows, width), BF16),
            ((n, rows, key_width), BF16),
            ((rows, key_width), BF16),
            ((n, heads, rows), F32),
            ((n, heads, rows), F32),
            ((n, heads, rows), F32),
        ],
        [
            pltpu.VMEM((n, rows, width), BF16),
            pltpu.VMEM((n, rows, width), BF16),
            pltpu.VMEM((n, 8, 128), F32),
            pltpu.VMEM((n, 8, 128), F32),
            pltpu.VMEM((key_width, inner), F32),
            pltpu.SMEM((n,), jnp.int32),
        ],
        *pieces,
        *shared,
        gate_gain,
        w_two,
        w_out,
        *done,
        aliases={first + i: i for i in range(5)},
    )
    send, own_x, own_live, normed_two, key_two, own_query, to_end_two, running_two, seen_two = got[5:]
    own, gate, decay = call(
        own_kernel,
        [((rows, inner), F32)] * 3,
        [],
        normed_two,
        key_two,
        own_query,
        to_end_two,
        running_two,
        seen_two,
        spread,
        skip,
        w_two,
    )
    earlier, fall = call(
        earlier_kernel,
        [((key_width, inner), F32), ((8, inner), F32)],
        [],
        normed_two,
        key_two,
        to_end_two,
        running_two,
        spread,
        w_two,
    )
    before = []
    steps = levels(tiles)
    for i, (radix, stride) in enumerate(steps):
        last = i == len(steps) - 1
        parts = [send] + [swap(send, "tile", k * stride, tiles) for k in range(1, radix)]
        outs = [((key_width, part), BF16)]
        if not last:
            outs = [((key_width + 8, part), F32), ((key_width + EXTRA, part), BF16)]
        got = call(
            functools.partial(join_kernel, radix, stride, last),
            outs,
            [pltpu.VMEM((radix, key_width + EXTRA, part), BF16)],
            *parts,
            *before,
            fall if last else decay,
        )
        if not last:
            before, send = [got[0]], got[1]
    incoming = got[0]
    states = [incoming] + [swap(incoming, "curve", k, n) for k in range(1, n)]
    common = (own, gate, own_query, decay, earlier, fall, gate_gain, w_out)
    partial = []
    for ks in ([0, 1], list(range(3, n))):
        partial = call(
            functools.partial(end_kernel, ks, not partial, False),
            [((rows, width), F32), ((rows, 128), F32)],
            [],
            *[states[k] for k in ks],
            *common,
            *partial,
        )
    (out,) = call(
        functools.partial(end_kernel, [2], False, True),
        [((1, rows, width), BF16)],
        [],
        states[2],
        *common,
        *partial,
        own_x,
        own_live,
        out_fixed=False,
    )
    return out


def solution(mesh):
    in_specs = (
        P("tile", "curve", None),
        P("tile", "curve"),
        P("tile", "curve", None),
        P("tile", "curve", None),
    ) + (P(),) * 9
    return jax.shard_map(
        functools.partial(local, mesh.shape["tile"]),
        mesh=mesh,
        in_specs=in_specs,
        out_specs=P("tile", "curve", None),
        check_vma=False,
    )
```

```python
import functools

import jax
import jax.numpy as jnp
from jax import lax
from jax.experimental import pallas as pl
from jax.experimental.pallas import tpu as pltpu
from jax.sharding import PartitionSpec as P

F32, BF16 = jnp.float32, jnp.bfloat16
EPS = 1e-5
LOG2E = 1.4426950408889634
EXTRA = 16
VMEM_BYTES = 20 * 1024 * 1024


def dot(a, b):
    return jnp.dot(a, b, preferred_element_type=F32)


def dot_nt(a, b):
    return lax.dot_general(a, b, (((1,), (1,)), ((), ())), preferred_element_type=F32)


def turn(x):
    return x.astype(F32).T.astype(x.dtype)


def silu(x):
    half = 0.5 * x
    return half + half * jnp.tanh(half)


def split(x):
    hi = x.astype(BF16).astype(F32)
    return hi, x - hi


def normalise(x, gain):
    wide = x.astype(F32)
    return (wide * lax.rsqrt(jnp.mean(wide * wide, axis=-1, keepdims=True) + EPS) * gain).astype(BF16)


def iota(shape, axis):
    return lax.broadcasted_iota(jnp.int32, shape, axis)


def column(row):
    heads = row.shape[1]
    same = iota((heads, heads), 0) == iota((heads, heads), 1)
    return jnp.sum(jnp.where(same, row, 0.0), axis=1, keepdims=True)


def head_steps(normed, valids, w_dt_t, bias, rate):
    heads = w_dt_t.shape[0]
    rows = normed.shape[0] // len(valids)
    raw = dot_nt(w_dt_t, normed) + column(bias)
    steps = jnp.maximum(raw, 0.0) + jnp.log1p(jnp.exp(-jnp.abs(raw)))
    lane = iota((heads, rows), 1).astype(F32)
    steps = jnp.concatenate(
        [
            jnp.where(lane < valid, steps[:, c * rows : (c + 1) * rows], 0.0)
            for c, valid in enumerate(valids)
        ],
        axis=0,
    )
    falls = -steps * jnp.concatenate([column(rate) * LOG2E] * len(valids), axis=0)
    upper = jnp.where(iota((rows, rows), 0) <= iota((rows, rows), 1), 1.0, 0.0).astype(BF16)
    high, rest = split(falls)
    middle, low = split(rest)
    running = (
        dot(high.astype(BF16), upper) + dot(middle.astype(BF16), upper) + dot(low.astype(BF16), upper)
    )
    to_end = jnp.exp2(running[:, rows - 1 : rows] - running) * steps
    return steps, to_end, running


def by_rows(to_end, running):
    parts = [*split(to_end), *split(jnp.exp2(running)), running]
    used = len(parts) * running.shape[0]
    stack = jnp.concatenate(parts + [jnp.zeros((128 - used, running.shape[1]), F32)], axis=0)
    return stack.T


def seen_from(steps, running):
    return running - jnp.where(steps > 0.0, jnp.log2(jnp.maximum(steps, 1e-37)), -1e30)


def inside_pair(turned, seen, scores, value, head, heads):
    rows = turned.shape[0]
    at = 4 * heads + head
    weights = [
        (jnp.exp2(jnp.minimum(turned[:, at + k : at + k + 1] - seen[head + k : head + k + 1], 120.0)) * scores).astype(BF16)
        for k in range(2)
    ]
    left = iota((rows, 128), 1) < 64
    zero = jnp.zeros_like(value)
    both = jnp.concatenate([jnp.where(left, value, zero), jnp.where(left, zero, value)], axis=0)
    return dot(jnp.concatenate(weights, axis=1), both)


def masked_scores(query, key):
    rows = query.shape[0]
    return jnp.where(iota((rows, rows), 0) >= iota((rows, rows), 1), dot_nt(query, key), 0.0)


def make_spread(spread, heads):
    inner = spread.shape[1] // 2
    head = lax.shift_right_logical(iota((128, inner), 1), (inner // heads).bit_length() - 1)
    row = iota((128, inner), 0)
    for g in range(2):
        hit = (row == head + 2 * heads * g) | (row == head + 2 * heads * g + heads)
        spread[:, g * inner : (g + 1) * inner] = jnp.where(hit, 1.0, 0.0).astype(BF16)


def make_skip(skip_g, spread, skip):
    layers, heads = skip_g.shape
    inner = skip.shape[1]
    for layer in range(layers):
        parts = [part for part in split(skip_g[layer : layer + 1, :])]
        row = jnp.concatenate(parts + [jnp.zeros((1, 128 - 2 * heads), F32)], axis=1)
        wide = jnp.broadcast_to(row, (16, 128)).astype(BF16)
        skip[8 * layer : 8 * layer + 8, :] = dot(wide, spread[:, :inner])[:8]


def pack_kernel(count, x, valid, shard, slot, *refs):
    sources, out, held, sems = refs[:count], refs[count], refs[count + 1 : -1], refs[-1]
    rows, width = x.shape[1:]
    copies = [pltpu.make_async_copy(x.at[0], out.at[pl.ds(0, rows)], sems.at[count])]
    copies += [pltpu.make_async_copy(a, b, sems.at[i]) for i, (a, b) in enumerate(zip(sources, held))]
    for copy in copies:
        copy.start()
    line, lane = iota((EXTRA, width), 0), iota((EXTRA, width), 1)
    live = valid[0, 0].astype(F32)
    place = (shard[0, 0, 0] + slot[0, 0, 0]).astype(F32)
    first = jnp.where(lane == 0, live, jnp.where(lane == 1, place, 0.0))
    out[rows:] = jnp.where(line == 0, first, 0.0).astype(BF16)
    for copy in copies:
        copy.wait()


def live_count(packed):
    at = packed.shape[0] - EXTRA
    return packed[at:, :128].astype(F32)[0:1, 0:1]


def place_of(packed):
    extra = packed[packed.shape[0] - EXTRA :, :128].astype(F32)
    hit = (iota((EXTRA, 128), 0) == 0) & (iota((EXTRA, 128), 1) == 1)
    return jnp.sum(jnp.where(hit, extra, 0.0)).astype(jnp.int32)


def block_of(packed):
    return packed[: packed.shape[0] - EXTRA]


def pieces_work(xs, valids, slots, params, work, ready=lambda: None):
    norm_g, w_xz, w_bc, w_dt, bias, rate, spread, skip = params
    gates, local, decay, grown, queries = work
    rows = xs[0].shape[0]
    heads, inner, key_width = w_dt.shape[1], w_xz.shape[1] // 2, w_bc.shape[2] // 2
    normed = normalise(jnp.concatenate(xs, axis=0), norm_g[0:1, :])
    bc = silu(dot(normed, w_bc[0])).astype(BF16)
    steps, to_end, running = head_steps(normed, valids, w_dt[0], bias[0:1, :], rate[0:1, :])
    seen = seen_from(steps, running)
    parts = []
    for i, slot in enumerate(slots):
        at, of = slice(i * rows, (i + 1) * rows), slice(i * heads, (i + 1) * heads)
        key, query = bc[at, :key_width], bc[at, key_width:]
        queries[slot] = query
        turned = by_rows(to_end[of], running[of])
        parts.append((slot, at, turned, turned.astype(BF16), seen[of], masked_scores(query, key), turn(key)))
    ready()
    for j in range(0, inner, 256):
        cols, ends = slice(j, j + 256), slice(inner + j, inner + j + 256)
        values = silu(dot(normed, w_xz[:, cols])).astype(BF16)
        gate = silu(dot(normed, w_xz[:, ends]))
        for slot, at, turned, lhs, seen_here, scores, key_t in parts:
            value = values[at]
            wide = value.astype(F32)
            gates[slot, :, cols] = gate[at]
            decay[slot, :, cols] = dot(lhs, spread[:, ends])
            grown[slot, :, cols] = dot(key_t, (wide * dot(lhs, spread[:, cols])).astype(BF16))
            base = skip[0:1, cols] * wide
            for k in range(2):
                half = slice(128 * k, 128 * k + 128)
                head = (j + 128 * k) * heads // inner
                local[slot, :, j + 128 * k : j + 128 * k + 128] = (
                    inside_pair(turned, seen_here, scores, value[:, half], head, heads) + base[:, half]
                )


def begin_kernel(packed, norm_g, w_bc, w_dt, bias, rate, skip_g, w_xz, w_held, spread, skip, *refs):
    work, sem = refs[:-1], refs[-1]
    copy = pltpu.make_async_copy(w_xz.at[0], w_held, sem)
    copy.start()
    make_spread(spread, w_dt.shape[1])
    make_skip(skip_g, spread, skip)
    params = (norm_g, w_held, w_bc, w_dt, bias, rate, spread, skip)
    pieces_work([block_of(packed)], [live_count(packed)], [0], params, work, copy.wait)


def piece_kernel(slot, layers, packed, late, *refs):
    held, sem = refs[-2:]
    copy = pltpu.make_async_copy(refs[13].at[layers], held, sem)
    copy.start()
    pieces_work([block_of(packed)], [live_count(packed)], [slot], refs[:8], refs[14:19])
    copy.wait()


def relay_kernel(x, *refs):
    refs[-1][...] = x[...]


def tile_kernel(n, *refs):
    pieces, refs = refs[:n], refs[n:]
    norm_g, w_held, w_bc, w_dt, bias, rate, spread, skip, gate_g, w_two, w_out = refs[:11]
    refs = refs[16:]
    work, refs = refs[:5], refs[5:]
    (
        send,
        own_x,
        own_live,
        normed_two,
        key_two,
        own_query,
        to_end_two,
        running_two,
        seen_two,
        x_one,
        x_two,
        valid_one,
        valid_two,
        state,
        dest,
    ) = refs
    gates, local, decay, grown, queries = work
    me = lax.axis_index("curve")
    rows, width = x_two.shape[1:]
    heads = w_dt.shape[1]
    inner = w_out.shape[1]
    key_width = w_bc.shape[2] // 2
    part = inner // n
    valid = [live_count(piece) for piece in pieces]
    xs = [block_of(piece) for piece in pieces]
    for k in range(n):
        x_one[k] = xs[k]
        dest[k] = place_of(pieces[k])
        valid_one[k] = jnp.broadcast_to(valid[k], (8, 128))
        valid_two[dest[k]] = jnp.broadcast_to(valid[k], (8, 128))
    params = (norm_g, w_held, w_bc, w_dt, bias, rate, spread, skip)
    pieces_work(xs[3:], valid[3:], list(range(3, n)), params, work)

    row = iota((rows, 128), 0).astype(F32)
    for c in range(n):
        k = me ^ c
        query = queries[k]
        squares = jnp.zeros((rows, 1), F32)
        update = None
        for j in range(0, inner, 256):
            at = slice(j, j + 256)
            out = local[k, :, at]
            if c:
                old = state[:, at]
                out += dot(query, old.astype(BF16)) * decay[k, :, at]
                if c < n - 1:
                    state[:, at] = old * decay[k, rows - 1 :, at] + grown[k, :, at]
            else:
                state[:, at] = grown[k, :, at]
            gated = out * gates[k, :, at]
            squares += jnp.sum(gated * gated, axis=-1, keepdims=True)
            of_part = dot((gated * gate_g[0:1, at]).astype(BF16), w_out[0, at, :])
            update = of_part if update is None else update + of_part
        scale = jnp.broadcast_to(lax.rsqrt(squares * (1.0 / inner) + EPS), (rows, 128))
        factor = jnp.where(row < valid_one[k][0:1], scale, 0.0)
        factor = jnp.concatenate([factor] * (width // 128), axis=1)
        new = (x_one[k].astype(F32) + update * factor).astype(BF16)
        x_two[dest[k]] = new
        normed_two[dest[k]] = normalise(new, norm_g[1:2, :])

    own_x[...] = x_two[me]
    own_live[...] = jnp.where(row < valid_two[me][0:1], 1.0, 0.0)
    normed = normed_two[...].reshape(n * rows, width)
    steps, to_end, running = head_steps(
        normed, [valid_two[c][0:1, 0:1] for c in range(n)], w_dt[1], bias[1:2, :], rate[1:2, :]
    )
    bc = silu(dot(normed, w_bc[1])).astype(BF16)
    at = pl.ds(pl.multiple_of(me * part, 128), part)
    value = silu(dot(normed, w_two[:, at])).astype(BF16).astype(F32)
    after = jnp.zeros((heads, 1), F32)
    suffixes = [None] * n
    for c in reversed(range(n)):
        suffixes[c] = after
        after = after + running[c * heads : (c + 1) * heads, rows - 1 :]
    whole = jnp.broadcast_to(after, (heads, rows))
    turned = [
        by_rows(to_end[c * heads : (c + 1) * heads] * jnp.exp2(suffixes[c]), whole).astype(BF16) for c in range(n)
    ]
    to_end_x = dot(jnp.concatenate(turned, axis=0), spread[:, at])
    fall = dot(turned[0][:16], spread[:, pl.ds(pl.multiple_of(inner + me * part, 128), part)])[0:1]
    send[:key_width] = dot(turn(bc[:, :key_width]), (value * to_end_x).astype(BF16)).astype(BF16)
    send[key_width:] = decay_rows(fall)
    seen = seen_from(steps, running)
    for c in range(n):
        chunk, of = slice(c * rows, (c + 1) * rows), slice(c * heads, (c + 1) * heads)
        key_two[c] = bc[chunk, :key_width]
        queries[c] = bc[chunk, key_width:]
        to_end_two[c] = to_end[of]
        running_two[c] = running[of]
        seen_two[c] = seen[of]
    own_query[...] = queries[me]


def own_kernel(
    normed_two, key_two, query, to_end_two, running_two, seen_two, spread, skip, w_xz, local, gate, decay
):
    me = lax.axis_index("curve")
    inner = local.shape[1]
    heads = seen_two.shape[1]
    normed = normed_two[me]
    turned = by_rows(to_end_two[me], running_two[me])
    lhs = turned.astype(BF16)
    seen = seen_two[me]
    scores = masked_scores(query[...], key_two[me])
    for j in range(0, inner, 256):
        at = slice(j, j + 256)
        value = silu(dot(normed, w_xz[:, at])).astype(BF16)
        gate[:, at] = silu(dot(normed, w_xz[:, inner + j : inner + j + 256]))
        decay[:, at] = dot(lhs, spread[:, inner + j : inner + j + 256])
        base = skip[8:9, at] * value.astype(F32)
        for k in range(2):
            half = slice(128 * k, 128 * k + 128)
            head = (j + 128 * k) * heads // inner
            local[:, j + 128 * k : j + 128 * k + 128] = (
                inside_pair(turned, seen, scores, value[:, half], head, heads) + base[:, half]
            )


def earlier_kernel(normed_two, key_two, to_end_two, running_two, spread, w_xz, state, fall):
    me = lax.axis_index("curve")
    inner = state.shape[1]
    rows = normed_two.shape[1]
    state[...] = jnp.zeros_like(state)
    fall[...] = jnp.ones_like(fall)

    def chunk(c, _):
        normed = normed_two[c]
        lhs = by_rows(to_end_two[c], running_two[c]).astype(BF16)
        key_t = turn(key_two[c])
        for j in range(0, inner, 256):
            at = slice(j, j + 256)
            value = silu(dot(normed, w_xz[:, at])).astype(BF16).astype(F32)
            weighted = value * dot(lhs, spread[:, at])
            end_x = dot(lhs[rows - 16 :], spread[:, inner + j : inner + j + 256])[15:16]
            state[:, at] = state[:, at] * end_x + dot(key_t, weighted.astype(BF16))
            fall[:, at] = fall[:, at] * end_x
        return 0

    lax.fori_loop(0, me, chunk, 0)


def decay_rows(fall):
    high, low = split(fall)
    lines = iota((EXTRA, fall.shape[1]), 0)
    return jnp.where(lines == 0, high, jnp.where(lines == 1, low, 0.0)).astype(BF16)


def state_and_decay(ordered, u):
    states = ordered.shape[1] - EXTRA
    tail = ordered[u, states:].astype(F32)
    return ordered[u, :states].astype(F32), tail[0:1] + tail[1:2]


def join_kernel(radix, stride, last, *refs):
    deeper = stride > 1
    parts, before = refs[:radix], refs[radix] if deeper else None
    outs, ordered = refs[radix + 1 + deeper : -1], refs[-1]
    me = lax.rem(lax.div(lax.axis_index("tile"), stride), radix)
    states, width = parts[0].shape[0] - EXTRA, parts[0].shape[1]
    for k in range(radix):
        ordered[me ^ k] = parts[k][...]
    earlier = (jnp.zeros((states, width), F32), jnp.ones((1, width), F32))
    whole = None
    for u in range(radix if not last else radix - 1):
        one, fall = state_and_decay(ordered, u)
        if u < radix - 1:
            took = jnp.where(me > u, 1.0, 0.0)
            keep = jnp.where(me > u, fall, 1.0)
            earlier = (earlier[0] * keep + one * took, earlier[1] * keep)
        if not last:
            whole = (one, fall) if u == 0 else (whole[0] * fall + one, whole[1] * fall)
    state, fall = earlier
    if deeper:
        state = state * before[states : states + 1] + before[:states]
        fall = fall * before[states : states + 1]
    if last:
        outs[0][...] = state.astype(BF16)
        return
    outs[0][:states] = state
    outs[0][states:] = jnp.broadcast_to(fall, (8, width))
    outs[1][:states] = whole[0].astype(BF16)
    outs[1][states:] = decay_rows(whole[1])


def end_kernel(ks, first, final, *refs):
    pieces, refs = refs[: len(ks)], refs[len(ks) :]
    local, gate, query, decay, earlier, fall, gate_g, w_out = refs[:8]
    me = lax.axis_index("curve")
    rows, inner = local.shape
    part = pieces[0].shape[1]
    squares = jnp.zeros((rows, 1), F32)
    update = None
    for k, piece in zip(ks, pieces):
        at = pl.ds(pl.multiple_of((me ^ k) * part, 128), part)
        state = piece[...].astype(F32) * fall[0:1, at] + earlier[:, at]
        head_out = dot(query[...], state.astype(BF16)) * decay[:, at] + local[:, at]
        gated = head_out * gate[:, at]
        squares += jnp.sum(gated * gated, axis=-1, keepdims=True)
        of_part = dot((gated * gate_g[1:2, at]).astype(BF16), w_out[1, at, :])
        update = of_part if update is None else update + of_part
    refs = refs[8:]
    squares = jnp.broadcast_to(squares, (rows, 128))
    if not first:
        update, squares, refs = update + refs[0][...], squares + refs[1][...], refs[2:]
    if not final:
        refs[0][...] = update
        refs[1][...] = squares
        return
    x, live, out = refs
    factor = live[...] * lax.rsqrt(squares * (1.0 / inner) + EPS)
    for j in range(0, x.shape[1], 128):
        at = slice(j, j + 128)
        out[0, :, at] = (x[:, at].astype(F32) + factor * update[:, at]).astype(BF16)


def call(kernel, outs, scratch, *args, in_hbm=(), free=(), aliases={}, out_fixed=True):
    vmem = pl.BlockSpec(memory_space=pltpu.VMEM)
    spaces = [pltpu.HBM if i in in_hbm else pltpu.VMEM for i in range(len(args))]
    spaces = [pltpu.SMEM if i in free else space for i, space in enumerate(spaces)]
    args = [
        arg if space == pltpu.SMEM else pltpu.with_memory_space_constraint(arg, space)
        for arg, space in zip(args, spaces)
    ]
    return pl.pallas_call(
        kernel,
        out_shape=[(pltpu.VMEM if out_fixed else jax.ShapeDtypeStruct)(shape, kind) for shape, kind in outs],
        in_specs=[pl.BlockSpec(memory_space=space) for space in spaces],
        out_specs=[vmem] * len(outs),
        scratch_shapes=scratch,
        input_output_aliases=aliases,
        compiler_params=pltpu.CompilerParams(vmem_limit_bytes=VMEM_BYTES),
    )(*args)


def swap(value, axis, mask, size):
    return lax.ppermute(value, axis, [(i, i ^ mask) for i in range(size)])


def levels(size):
    steps, stride = [], 1
    while stride < size:
        radix = 4 if size // stride >= 4 else 2
        steps.append((radix, stride))
        stride *= radix
    return steps


def local(
    tiles,
    points,
    valid_rows,
    dest_shard,
    dest_slot,
    norm_gain,
    w_xz,
    w_bc,
    w_dt,
    dt_bias,
    decay_rate,
    skip_gain,
    gate_gain,
    w_out,
):
    n = lax.axis_size("curve")
    rows, width = points.shape[1:]
    heads, inner, key_width = w_dt.shape[2], w_out.shape[1], w_bc.shape[2] // 2
    part = inner // n
    params = (norm_gain, w_bc, jnp.swapaxes(w_dt, 1, 2), dt_bias, decay_rate, skip_gain, gate_gain)
    packed, norm_gain, w_bc, w_dt, dt_bias, decay_rate, skip_gain, gate_gain = call(
        functools.partial(pack_kernel, len(params)),
        [((rows + EXTRA, width), BF16)] + [(p.shape, p.dtype) for p in params],
        [pltpu.SemaphoreType.DMA((len(params) + 1,))],
        points,
        valid_rows,
        dest_shard,
        dest_slot,
        *params,
        in_hbm=(0, *range(4, 4 + len(params))),
        free=(1, 2, 3),
    )
    pieces = [packed] + [None] * (n - 1)
    for k in range(2, n, 2):
        pieces[k] = swap(packed, "curve", k, n)
    pieces[1] = swap(packed, "curve", 1, n)
    work = [
        ((n, rows, inner), F32),
        ((n, rows, inner), F32),
        ((n, rows, inner), F32),
        ((n, key_width, inner), F32),
        ((n, rows, key_width), BF16),
    ]
    w_held, spread, skip, *done = call(
        begin_kernel,
        [(w_xz.shape[1:], BF16), ((128, 2 * inner), BF16), ((8 * skip_gain.shape[0], inner), F32)] + work,
        [pltpu.SemaphoreType.DMA],
        packed,
        norm_gain,
        w_bc,
        w_dt,
        dt_bias,
        decay_rate,
        skip_gain,
        w_xz,
        in_hbm=(7,),
    )
    shared = (norm_gain, w_held, w_bc, w_dt, dt_bias, decay_rate, spread, skip)
    aliases = {10 + i: i for i in range(5)}
    *done, w_out = call(
        functools.partial(piece_kernel, 1, pl.ds(0, w_out.shape[0])),
        work + [(w_out.shape, BF16)],
        [pltpu.SemaphoreType.DMA],
        pieces[1],
        packed,
        *shared,
        *done,
        w_out,
        in_hbm=(15,),
        aliases=aliases,
    )
    for k in range(3, n, 2):
        (passed,) = call(relay_kernel, [(packed.shape, BF16)], [], pieces[k - 1], done[4])
        pieces[k] = swap(passed, "curve", 1, n)
    *done, w_two = call(
        functools.partial(piece_kernel, 2, 1),
        work + [(w_xz.shape[1:], BF16)],
        [pltpu.SemaphoreType.DMA],
        pieces[2],
        passed,
        *shared,
        *done,
        w_xz,
        in_hbm=(15,),
        aliases=aliases,
    )
    first = n + 11
    got = call(
        functools.partial(tile_kernel, n),
        work
        + [
            ((key_width + EXTRA, part), BF16),
            ((rows, width), BF16),
            ((rows, 128), F32),
            ((n, rows, width), BF16),
            ((n, rows, key_width), BF16),
            ((rows, key_width), BF16),
            ((n, heads, rows), F32),
            ((n, heads, rows), F32),
            ((n, heads, rows), F32),
        ],
        [
            pltpu.VMEM((n, rows, width), BF16),
            pltpu.VMEM((n, rows, width), BF16),
            pltpu.VMEM((n, 8, 128), F32),
            pltpu.VMEM((n, 8, 128), F32),
            pltpu.VMEM((key_width, inner), F32),
            pltpu.SMEM((n,), jnp.int32),
        ],
        *pieces,
        *shared,
        gate_gain,
        w_two,
        w_out,
        *done,
        aliases={first + i: i for i in range(5)},
    )
    send, own_x, own_live, normed_two, key_two, own_query, to_end_two, running_two, seen_two = got[5:]
    own, gate, decay = call(
        own_kernel,
        [((rows, inner), F32)] * 3,
        [],
        normed_two,
        key_two,
        own_query,
        to_end_two,
        running_two,
        seen_two,
        spread,
        skip,
        w_two,
    )
    earlier, fall = call(
        earlier_kernel,
        [((key_width, inner), F32), ((8, inner), F32)],
        [],
        normed_two,
        key_two,
        to_end_two,
        running_two,
        spread,
        w_two,
    )
    before = []
    steps = levels(tiles)
    for i, (radix, stride) in enumerate(steps):
        last = i == len(steps) - 1
        parts = [send] + [swap(send, "tile", k * stride, tiles) for k in range(1, radix)]
        outs = [((key_width, part), BF16)]
        if not last:
            outs = [((key_width + 8, part), F32), ((key_width + EXTRA, part), BF16)]
        got = call(
            functools.partial(join_kernel, radix, stride, last),
            outs,
            [pltpu.VMEM((radix, key_width + EXTRA, part), BF16)],
            *parts,
            *before,
            fall if last else decay,
        )
        if not last:
            before, send = [got[0]], got[1]
    incoming = got[0]
    states = [incoming] + [swap(incoming, "curve", k, n) for k in range(1, n)]
    common = (own, gate, own_query, decay, earlier, fall, gate_gain, w_out)
    partial = []
    for ks in ([0], list(range(3, n))):
        partial = call(
            functools.partial(end_kernel, ks, not partial, False),
            [((rows, width), F32), ((rows, 128), F32)],
            [],
            *[states[k] for k in ks],
            *common,
            *partial,
        )
    (out,) = call(
        functools.partial(end_kernel, [2, 1], False, True),
        [((1, rows, width), BF16)],
        [],
        states[2],
        states[1],
        *common,
        *partial,
        own_x,
        own_live,
        out_fixed=False,
    )
    return out


def solution(mesh):
    in_specs = (
        P("tile", "curve", None),
        P("tile", "curve"),
        P("tile", "curve", None),
        P("tile", "curve", None),
    ) + (P(),) * 9
    return jax.shard_map(
        functools.partial(local, mesh.shape["tile"]),
        mesh=mesh,
        in_specs=in_specs,
        out_specs=P("tile", "curve", None),
        check_vma=False,
    )
```

```python
import functools

import jax
import jax.numpy as jnp
from jax import lax
from jax.experimental import pallas as pl
from jax.experimental.pallas import tpu as pltpu
from jax.sharding import PartitionSpec as P

F32, BF16 = jnp.float32, jnp.bfloat16
EPS = 1e-5
LOG2E = 1.4426950408889634
EXTRA = 16
VMEM_BYTES = 20 * 1024 * 1024


def dot(a, b):
    return jnp.dot(a, b, preferred_element_type=F32)


def dot_nt(a, b):
    return lax.dot_general(a, b, (((1,), (1,)), ((), ())), preferred_element_type=F32)


def turn(x):
    return x.astype(F32).T.astype(x.dtype)


def silu(x):
    half = 0.5 * x
    return half + half * jnp.tanh(half)


def split(x):
    hi = x.astype(BF16).astype(F32)
    return hi, x - hi


def normalise(x, gain):
    wide = x.astype(F32)
    return (wide * lax.rsqrt(jnp.mean(wide * wide, axis=-1, keepdims=True) + EPS) * gain).astype(BF16)


def iota(shape, axis):
    return lax.broadcasted_iota(jnp.int32, shape, axis)


def column(row):
    heads = row.shape[1]
    same = iota((heads, heads), 0) == iota((heads, heads), 1)
    return jnp.sum(jnp.where(same, row, 0.0), axis=1, keepdims=True)


def head_steps(normed, valids, w_dt_t, bias, rate):
    heads = w_dt_t.shape[0]
    rows = normed.shape[0] // len(valids)
    raw = dot_nt(w_dt_t, normed) + column(bias)
    steps = jnp.maximum(raw, 0.0) + jnp.log1p(jnp.exp(-jnp.abs(raw)))
    lane = iota((heads, rows), 1).astype(F32)
    steps = jnp.concatenate(
        [
            jnp.where(lane < valid, steps[:, c * rows : (c + 1) * rows], 0.0)
            for c, valid in enumerate(valids)
        ],
        axis=0,
    )
    falls = -steps * jnp.concatenate([column(rate) * LOG2E] * len(valids), axis=0)
    upper = jnp.where(iota((rows, rows), 0) <= iota((rows, rows), 1), 1.0, 0.0).astype(BF16)
    high, rest = split(falls)
    middle, low = split(rest)
    running = (
        dot(high.astype(BF16), upper) + dot(middle.astype(BF16), upper) + dot(low.astype(BF16), upper)
    )
    to_end = jnp.exp2(running[:, rows - 1 : rows] - running) * steps
    return steps, to_end, running


def by_rows(to_end, running):
    parts = [*split(to_end), *split(jnp.exp2(running)), running]
    used = len(parts) * running.shape[0]
    stack = jnp.concatenate(parts + [jnp.zeros((128 - used, running.shape[1]), F32)], axis=0)
    return stack.T


def seen_from(steps, running):
    return running - jnp.where(steps > 0.0, jnp.log2(jnp.maximum(steps, 1e-37)), -1e30)


def inside_pair(turned, seen, scores, value, head, heads):
    rows = turned.shape[0]
    at = 4 * heads + head
    weights = [
        (jnp.exp2(jnp.minimum(turned[:, at + k : at + k + 1] - seen[head + k : head + k + 1], 120.0)) * scores).astype(BF16)
        for k in range(2)
    ]
    left = iota((rows, 128), 1) < 64
    zero = jnp.zeros_like(value)
    both = jnp.concatenate([jnp.where(left, value, zero), jnp.where(left, zero, value)], axis=0)
    return dot(jnp.concatenate(weights, axis=1), both)


def masked_scores(query, key):
    rows = query.shape[0]
    return jnp.where(iota((rows, rows), 0) >= iota((rows, rows), 1), dot_nt(query, key), 0.0)


def make_spread(spread, heads):
    inner = spread.shape[1] // 2
    head = lax.shift_right_logical(iota((128, inner), 1), (inner // heads).bit_length() - 1)
    row = iota((128, inner), 0)
    for g in range(2):
        hit = (row == head + 2 * heads * g) | (row == head + 2 * heads * g + heads)
        spread[:, g * inner : (g + 1) * inner] = jnp.where(hit, 1.0, 0.0).astype(BF16)


def make_skip(skip_g, spread, skip):
    layers, heads = skip_g.shape
    inner = skip.shape[1]
    for layer in range(layers):
        parts = [part for part in split(skip_g[layer : layer + 1, :])]
        row = jnp.concatenate(parts + [jnp.zeros((1, 128 - 2 * heads), F32)], axis=1)
        wide = jnp.broadcast_to(row, (16, 128)).astype(BF16)
        skip[8 * layer : 8 * layer + 8, :] = dot(wide, spread[:, :inner])[:8]


def pack_kernel(count, x, valid, shard, slot, *refs):
    sources, out, held, sems = refs[:count], refs[count], refs[count + 1 : -1], refs[-1]
    rows, width = x.shape[1:]
    copies = [pltpu.make_async_copy(x.at[0], out.at[pl.ds(0, rows)], sems.at[count])]
    copies += [pltpu.make_async_copy(a, b, sems.at[i]) for i, (a, b) in enumerate(zip(sources, held))]
    for copy in copies:
        copy.start()
    line, lane = iota((EXTRA, width), 0), iota((EXTRA, width), 1)
    live = valid[0, 0].astype(F32)
    place = (shard[0, 0, 0] + slot[0, 0, 0]).astype(F32)
    first = jnp.where(lane == 0, live, jnp.where(lane == 1, place, 0.0))
    out[rows:] = jnp.where(line == 0, first, 0.0).astype(BF16)
    for copy in copies:
        copy.wait()


def live_count(packed):
    at = packed.shape[0] - EXTRA
    return packed[at:, :128].astype(F32)[0:1, 0:1]


def place_of(packed):
    extra = packed[packed.shape[0] - EXTRA :, :128].astype(F32)
    hit = (iota((EXTRA, 128), 0) == 0) & (iota((EXTRA, 128), 1) == 1)
    return jnp.sum(jnp.where(hit, extra, 0.0)).astype(jnp.int32)


def block_of(packed):
    return packed[: packed.shape[0] - EXTRA]


def pieces_work(xs, valids, slots, params, work, ready=lambda: None):
    norm_g, w_xz, w_bc, w_dt, bias, rate, spread, skip = params
    gates, local, decay, grown, queries = work
    rows = xs[0].shape[0]
    heads, inner, key_width = w_dt.shape[1], w_xz.shape[1] // 2, w_bc.shape[2] // 2
    normed = normalise(jnp.concatenate(xs, axis=0), norm_g[0:1, :])
    bc = silu(dot(normed, w_bc[0])).astype(BF16)
    steps, to_end, running = head_steps(normed, valids, w_dt[0], bias[0:1, :], rate[0:1, :])
    seen = seen_from(steps, running)
    parts = []
    for i, slot in enumerate(slots):
        at, of = slice(i * rows, (i + 1) * rows), slice(i * heads, (i + 1) * heads)
        key, query = bc[at, :key_width], bc[at, key_width:]
        queries[slot] = query
        turned = by_rows(to_end[of], running[of])
        parts.append((slot, at, turned, turned.astype(BF16), seen[of], masked_scores(query, key), turn(key)))
    ready()
    for j in range(0, inner, 256):
        cols, ends = slice(j, j + 256), slice(inner + j, inner + j + 256)
        values = silu(dot(normed, w_xz[:, cols])).astype(BF16)
        gate = silu(dot(normed, w_xz[:, ends]))
        for slot, at, turned, lhs, seen_here, scores, key_t in parts:
            value = values[at]
            wide = value.astype(F32)
            gates[slot, :, cols] = gate[at]
            decay[slot, :, cols] = dot(lhs, spread[:, ends])
            grown[slot, :, cols] = dot(key_t, (wide * dot(lhs, spread[:, cols])).astype(BF16))
            base = skip[0:1, cols] * wide
            for k in range(2):
                half = slice(128 * k, 128 * k + 128)
                head = (j + 128 * k) * heads // inner
                local[slot, :, j + 128 * k : j + 128 * k + 128] = (
                    inside_pair(turned, seen_here, scores, value[:, half], head, heads) + base[:, half]
                )


def begin_kernel(packed, norm_g, w_dt, bias, rate, skip_g, w_bc_far, w_xz, w_bc, w_held, spread, skip, *refs):
    work, sems = refs[:-1], refs[-1]
    copies = [
        pltpu.make_async_copy(w_bc_far.at[0], w_bc.at[0], sems.at[0]),
        pltpu.make_async_copy(w_xz.at[0], w_held, sems.at[1]),
        pltpu.make_async_copy(w_bc_far.at[1], w_bc.at[1], sems.at[2]),
    ]
    for copy in copies:
        copy.start()
    make_spread(spread, w_dt.shape[1])
    make_skip(skip_g, spread, skip)
    params = (norm_g, w_held, w_bc, w_dt, bias, rate, spread, skip)
    copies[0].wait()
    pieces_work([block_of(packed)], [live_count(packed)], [0], params, work, copies[1].wait)
    copies[2].wait()


def piece_kernel(slot, layers, packed, late, *refs):
    held, sem = refs[-2:]
    copy = pltpu.make_async_copy(refs[13].at[layers], held, sem)
    copy.start()
    pieces_work([block_of(packed)], [live_count(packed)], [slot], refs[:8], refs[14:19])
    copy.wait()


def relay_kernel(x, *refs):
    refs[-1][...] = x[...]


def tile_kernel(n, *refs):
    pieces, refs = refs[:n], refs[n:]
    norm_g, w_held, w_bc, w_dt, bias, rate, spread, skip, gate_g, w_two, w_out = refs[:11]
    refs = refs[16:]
    work, refs = refs[:5], refs[5:]
    (
        send,
        own_x,
        own_live,
        normed_two,
        key_two,
        own_query,
        to_end_two,
        running_two,
        seen_two,
        x_one,
        x_two,
        valid_one,
        valid_two,
        state,
        dest,
    ) = refs
    gates, local, decay, grown, queries = work
    me = lax.axis_index("curve")
    rows, width = x_two.shape[1:]
    heads = w_dt.shape[1]
    inner = w_out.shape[1]
    key_width = w_bc.shape[2] // 2
    part = inner // n
    valid = [live_count(piece) for piece in pieces]
    xs = [block_of(piece) for piece in pieces]
    for k in range(n):
        x_one[k] = xs[k]
        dest[k] = place_of(pieces[k])
        valid_one[k] = jnp.broadcast_to(valid[k], (8, 128))
        valid_two[dest[k]] = jnp.broadcast_to(valid[k], (8, 128))
    params = (norm_g, w_held, w_bc, w_dt, bias, rate, spread, skip)
    pieces_work(xs[3:], valid[3:], list(range(3, n)), params, work)

    row = iota((rows, 128), 0).astype(F32)
    for c in range(n):
        k = me ^ c
        query = queries[k]
        squares = jnp.zeros((rows, 1), F32)
        update = None
        for j in range(0, inner, 256):
            at = slice(j, j + 256)
            out = local[k, :, at]
            if c:
                old = state[:, at]
                out += dot(query, old.astype(BF16)) * decay[k, :, at]
                if c < n - 1:
                    state[:, at] = old * decay[k, rows - 1 :, at] + grown[k, :, at]
            else:
                state[:, at] = grown[k, :, at]
            gated = out * gates[k, :, at]
            squares += jnp.sum(gated * gated, axis=-1, keepdims=True)
            of_part = dot((gated * gate_g[0:1, at]).astype(BF16), w_out[0, at, :])
            update = of_part if update is None else update + of_part
        scale = jnp.broadcast_to(lax.rsqrt(squares * (1.0 / inner) + EPS), (rows, 128))
        factor = jnp.where(row < valid_one[k][0:1], scale, 0.0)
        factor = jnp.concatenate([factor] * (width // 128), axis=1)
        new = (x_one[k].astype(F32) + update * factor).astype(BF16)
        x_two[dest[k]] = new
        normed_two[dest[k]] = normalise(new, norm_g[1:2, :])

    own_x[...] = x_two[me]
    own_live[...] = jnp.where(row < valid_two[me][0:1], 1.0, 0.0)
    normed = normed_two[...].reshape(n * rows, width)
    steps, to_end, running = head_steps(
        normed, [valid_two[c][0:1, 0:1] for c in range(n)], w_dt[1], bias[1:2, :], rate[1:2, :]
    )
    bc = silu(dot(normed, w_bc[1])).astype(BF16)
    at = pl.ds(pl.multiple_of(me * part, 128), part)
    value = silu(dot(normed, w_two[:, at])).astype(BF16).astype(F32)
    after = jnp.zeros((heads, 1), F32)
    suffixes = [None] * n
    for c in reversed(range(n)):
        suffixes[c] = after
        after = after + running[c * heads : (c + 1) * heads, rows - 1 :]
    whole = jnp.broadcast_to(after, (heads, rows))
    turned = [
        by_rows(to_end[c * heads : (c + 1) * heads] * jnp.exp2(suffixes[c]), whole).astype(BF16) for c in range(n)
    ]
    to_end_x = dot(jnp.concatenate(turned, axis=0), spread[:, at])
    fall = dot(turned[0][:16], spread[:, pl.ds(pl.multiple_of(inner + me * part, 128), part)])[0:1]
    send[:key_width] = dot(turn(bc[:, :key_width]), (value * to_end_x).astype(BF16)).astype(BF16)
    send[key_width:] = decay_rows(fall)
    seen = seen_from(steps, running)
    for c in range(n):
        chunk, of = slice(c * rows, (c + 1) * rows), slice(c * heads, (c + 1) * heads)
        key_two[c] = bc[chunk, :key_width]
        queries[c] = bc[chunk, key_width:]
        to_end_two[c] = to_end[of]
        running_two[c] = running[of]
        seen_two[c] = seen[of]
    own_query[...] = queries[me]


def own_kernel(
    normed_two, key_two, query, to_end_two, running_two, seen_two, spread, skip, w_xz, local, gate, decay
):
    me = lax.axis_index("curve")
    inner = local.shape[1]
    heads = seen_two.shape[1]
    normed = normed_two[me]
    turned = by_rows(to_end_two[me], running_two[me])
    lhs = turned.astype(BF16)
    seen = seen_two[me]
    scores = masked_scores(query[...], key_two[me])
    for j in range(0, inner, 256):
        at = slice(j, j + 256)
        value = silu(dot(normed, w_xz[:, at])).astype(BF16)
        gate[:, at] = silu(dot(normed, w_xz[:, inner + j : inner + j + 256]))
        decay[:, at] = dot(lhs, spread[:, inner + j : inner + j + 256])
        base = skip[8:9, at] * value.astype(F32)
        for k in range(2):
            half = slice(128 * k, 128 * k + 128)
            head = (j + 128 * k) * heads // inner
            local[:, j + 128 * k : j + 128 * k + 128] = (
                inside_pair(turned, seen, scores, value[:, half], head, heads) + base[:, half]
            )


def earlier_kernel(normed_two, key_two, to_end_two, running_two, spread, w_xz, state, fall):
    me = lax.axis_index("curve")
    inner = state.shape[1]
    rows = normed_two.shape[1]
    state[...] = jnp.zeros_like(state)
    fall[...] = jnp.ones_like(fall)

    def chunk(c, _):
        normed = normed_two[c]
        lhs = by_rows(to_end_two[c], running_two[c]).astype(BF16)
        key_t = turn(key_two[c])
        for j in range(0, inner, 256):
            at = slice(j, j + 256)
            value = silu(dot(normed, w_xz[:, at])).astype(BF16).astype(F32)
            weighted = value * dot(lhs, spread[:, at])
            end_x = dot(lhs[rows - 16 :], spread[:, inner + j : inner + j + 256])[15:16]
            state[:, at] = state[:, at] * end_x + dot(key_t, weighted.astype(BF16))
            fall[:, at] = fall[:, at] * end_x
        return 0

    lax.fori_loop(0, me, chunk, 0)


def decay_rows(fall):
    high, low = split(fall)
    lines = iota((EXTRA, fall.shape[1]), 0)
    return jnp.where(lines == 0, high, jnp.where(lines == 1, low, 0.0)).astype(BF16)


def state_and_decay(ordered, u):
    states = ordered.shape[1] - EXTRA
    tail = ordered[u, states:].astype(F32)
    return ordered[u, :states].astype(F32), tail[0:1] + tail[1:2]


def join_kernel(radix, stride, last, *refs):
    deeper = stride > 1
    parts, before = refs[:radix], refs[radix] if deeper else None
    outs, ordered = refs[radix + 1 + deeper : -1], refs[-1]
    me = lax.rem(lax.div(lax.axis_index("tile"), stride), radix)
    states, width = parts[0].shape[0] - EXTRA, parts[0].shape[1]
    for k in range(radix):
        ordered[me ^ k] = parts[k][...]
    earlier = (jnp.zeros((states, width), F32), jnp.ones((1, width), F32))
    whole = None
    for u in range(radix if not last else radix - 1):
        one, fall = state_and_decay(ordered, u)
        if u < radix - 1:
            took = jnp.where(me > u, 1.0, 0.0)
            keep = jnp.where(me > u, fall, 1.0)
            earlier = (earlier[0] * keep + one * took, earlier[1] * keep)
        if not last:
            whole = (one, fall) if u == 0 else (whole[0] * fall + one, whole[1] * fall)
    state, fall = earlier
    if deeper:
        state = state * before[states : states + 1] + before[:states]
        fall = fall * before[states : states + 1]
    if last:
        outs[0][...] = state.astype(BF16)
        return
    outs[0][:states] = state
    outs[0][states:] = jnp.broadcast_to(fall, (8, width))
    outs[1][:states] = whole[0].astype(BF16)
    outs[1][states:] = decay_rows(whole[1])


def end_kernel(ks, first, final, *refs):
    pieces, refs = refs[: len(ks)], refs[len(ks) :]
    local, gate, query, decay, earlier, fall, gate_g, w_out = refs[:8]
    me = lax.axis_index("curve")
    rows, inner = local.shape
    part = pieces[0].shape[1]
    squares = jnp.zeros((rows, 1), F32)
    update = None
    for k, piece in zip(ks, pieces):
        at = pl.ds(pl.multiple_of((me ^ k) * part, 128), part)
        state = piece[...].astype(F32) * fall[0:1, at] + earlier[:, at]
        head_out = dot(query[...], state.astype(BF16)) * decay[:, at] + local[:, at]
        gated = head_out * gate[:, at]
        squares += jnp.sum(gated * gated, axis=-1, keepdims=True)
        of_part = dot((gated * gate_g[1:2, at]).astype(BF16), w_out[1, at, :])
        update = of_part if update is None else update + of_part
    refs = refs[8:]
    squares = jnp.broadcast_to(squares, (rows, 128))
    if not first:
        update, squares, refs = update + refs[0][...], squares + refs[1][...], refs[2:]
    if not final:
        refs[0][...] = update
        refs[1][...] = squares
        return
    x, live, out = refs
    factor = live[...] * lax.rsqrt(squares * (1.0 / inner) + EPS)
    for j in range(0, x.shape[1], 128):
        at = slice(j, j + 128)
        out[0, :, at] = (x[:, at].astype(F32) + factor * update[:, at]).astype(BF16)


def call(kernel, outs, scratch, *args, in_hbm=(), free=(), aliases={}, out_fixed=True):
    vmem = pl.BlockSpec(memory_space=pltpu.VMEM)
    spaces = [pltpu.HBM if i in in_hbm else pltpu.VMEM for i in range(len(args))]
    spaces = [pltpu.SMEM if i in free else space for i, space in enumerate(spaces)]
    args = [
        arg if space == pltpu.SMEM else pltpu.with_memory_space_constraint(arg, space)
        for arg, space in zip(args, spaces)
    ]
    return pl.pallas_call(
        kernel,
        out_shape=[(pltpu.VMEM if out_fixed else jax.ShapeDtypeStruct)(shape, kind) for shape, kind in outs],
        in_specs=[pl.BlockSpec(memory_space=space) for space in spaces],
        out_specs=[vmem] * len(outs),
        scratch_shapes=scratch,
        input_output_aliases=aliases,
        compiler_params=pltpu.CompilerParams(vmem_limit_bytes=VMEM_BYTES),
    )(*args)


def swap(value, axis, mask, size):
    return lax.ppermute(value, axis, [(i, i ^ mask) for i in range(size)])


def levels(size):
    steps, stride = [], 1
    while stride < size:
        radix = 4 if size // stride >= 4 else 2
        steps.append((radix, stride))
        stride *= radix
    return steps


def local(
    tiles,
    points,
    valid_rows,
    dest_shard,
    dest_slot,
    norm_gain,
    w_xz,
    w_bc,
    w_dt,
    dt_bias,
    decay_rate,
    skip_gain,
    gate_gain,
    w_out,
):
    n = lax.axis_size("curve")
    rows, width = points.shape[1:]
    heads, inner, key_width = w_dt.shape[2], w_out.shape[1], w_bc.shape[2] // 2
    part = inner // n
    params = (norm_gain, jnp.swapaxes(w_dt, 1, 2), dt_bias, decay_rate, skip_gain, gate_gain)
    packed, norm_gain, w_dt, dt_bias, decay_rate, skip_gain, gate_gain = call(
        functools.partial(pack_kernel, len(params)),
        [((rows + EXTRA, width), BF16)] + [(p.shape, p.dtype) for p in params],
        [pltpu.SemaphoreType.DMA((len(params) + 1,))],
        points,
        valid_rows,
        dest_shard,
        dest_slot,
        *params,
        in_hbm=(0, *range(4, 4 + len(params))),
        free=(1, 2, 3),
    )
    pieces = [packed] + [None] * (n - 1)
    for k in range(2, n, 2):
        pieces[k] = swap(packed, "curve", k, n)
    pieces[1] = swap(packed, "curve", 1, n)
    work = [
        ((n, rows, inner), F32),
        ((n, rows, inner), F32),
        ((n, rows, inner), F32),
        ((n, key_width, inner), F32),
        ((n, rows, key_width), BF16),
    ]
    w_bc, w_held, spread, skip, *done = call(
        begin_kernel,
        [(w_bc.shape, BF16), (w_xz.shape[1:], BF16), ((128, 2 * inner), BF16), ((8 * skip_gain.shape[0], inner), F32)] + work,
        [pltpu.SemaphoreType.DMA((3,))],
        packed,
        norm_gain,
        w_dt,
        dt_bias,
        decay_rate,
        skip_gain,
        w_bc,
        w_xz,
        in_hbm=(6, 7),
    )
    shared = (norm_gain, w_held, w_bc, w_dt, dt_bias, decay_rate, spread, skip)
    aliases = {10 + i: i for i in range(5)}
    *done, w_out = call(
        functools.partial(piece_kernel, 1, pl.ds(0, w_out.shape[0])),
        work + [(w_out.shape, BF16)],
        [pltpu.SemaphoreType.DMA],
        pieces[1],
        packed,
        *shared,
        *done,
        w_out,
        in_hbm=(15,),
        aliases=aliases,
    )
    for k in range(3, n, 2):
        (passed,) = call(relay_kernel, [(packed.shape, BF16)], [], pieces[k - 1], done[4])
        pieces[k] = swap(passed, "curve", 1, n)
    *done, w_two = call(
        functools.partial(piece_kernel, 2, 1),
        work + [(w_xz.shape[1:], BF16)],
        [pltpu.SemaphoreType.DMA],
        pieces[2],
        passed,
        *shared,
        *done,
        w_xz,
        in_hbm=(15,),
        aliases=aliases,
    )
    first = n + 11
    got = call(
        functools.partial(tile_kernel, n),
        work
        + [
            ((key_width + EXTRA, part), BF16),
            ((rows, width), BF16),
            ((rows, 128), F32),
            ((n, rows, width), BF16),
            ((n, rows, key_width), BF16),
            ((rows, key_width), BF16),
            ((n, heads, rows), F32),
            ((n, heads, rows), F32),
            ((n, heads, rows), F32),
        ],
        [
            pltpu.VMEM((n, rows, width), BF16),
            pltpu.VMEM((n, rows, width), BF16),
            pltpu.VMEM((n, 8, 128), F32),
            pltpu.VMEM((n, 8, 128), F32),
            pltpu.VMEM((key_width, inner), F32),
            pltpu.SMEM((n,), jnp.int32),
        ],
        *pieces,
        *shared,
        gate_gain,
        w_two,
        w_out,
        *done,
        aliases={first + i: i for i in range(5)},
    )
    send, own_x, own_live, normed_two, key_two, own_query, to_end_two, running_two, seen_two = got[5:]
    own, gate, decay = call(
        own_kernel,
        [((rows, inner), F32)] * 3,
        [],
        normed_two,
        key_two,
        own_query,
        to_end_two,
        running_two,
        seen_two,
        spread,
        skip,
        w_two,
    )
    earlier, fall = call(
        earlier_kernel,
        [((key_width, inner), F32), ((8, inner), F32)],
        [],
        normed_two,
        key_two,
        to_end_two,
        running_two,
        spread,
        w_two,
    )
    before = []
    steps = levels(tiles)
    for i, (radix, stride) in enumerate(steps):
        last = i == len(steps) - 1
        parts = [send] + [swap(send, "tile", k * stride, tiles) for k in range(1, radix)]
        outs = [((key_width, part), BF16)]
        if not last:
            outs = [((key_width + 8, part), F32), ((key_width + EXTRA, part), BF16)]
        got = call(
            functools.partial(join_kernel, radix, stride, last),
            outs,
            [pltpu.VMEM((radix, key_width + EXTRA, part), BF16)],
            *parts,
            *before,
            fall if last else decay,
        )
        if not last:
            before, send = [got[0]], got[1]
    incoming = got[0]
    states = [incoming] + [swap(incoming, "curve", k, n) for k in range(1, n)]
    common = (own, gate, own_query, decay, earlier, fall, gate_gain, w_out)
    partial = []
    for ks in ([0], list(range(3, n))):
        partial = call(
            functools.partial(end_kernel, ks, not partial, False),
            [((rows, width), F32), ((rows, 128), F32)],
            [],
            *[states[k] for k in ks],
            *common,
            *partial,
        )
    (out,) = call(
        functools.partial(end_kernel, [2, 1], False, True),
        [((1, rows, width), BF16)],
        [],
        states[2],
        states[1],
        *common,
        *partial,
        own_x,
        own_live,
        out_fixed=False,
    )
    return out


def solution(mesh):
    in_specs = (
        P("tile", "curve", None),
        P("tile", "curve"),
        P("tile", "curve", None),
        P("tile", "curve", None),
    ) + (P(),) * 9
    return jax.shard_map(
        functools.partial(local, mesh.shape["tile"]),
        mesh=mesh,
        in_specs=in_specs,
        out_specs=P("tile", "curve", None),
        check_vma=False,
    )
```

```python
import functools

import jax
import jax.numpy as jnp
from jax import lax
from jax.experimental import pallas as pl
from jax.experimental.pallas import tpu as pltpu
from jax.sharding import PartitionSpec as P

F32, BF16 = jnp.float32, jnp.bfloat16
EPS = 1e-5
LOG2E = 1.4426950408889634
EXTRA = 16
VMEM_BYTES = 20 * 1024 * 1024


def dot(a, b):
    return jnp.dot(a, b, preferred_element_type=F32)


def dot_nt(a, b):
    return lax.dot_general(a, b, (((1,), (1,)), ((), ())), preferred_element_type=F32)


def turn(x):
    return x.astype(F32).T.astype(x.dtype)


def silu(x):
    half = 0.5 * x
    return half + half * jnp.tanh(half)


def split(x):
    hi = x.astype(BF16).astype(F32)
    return hi, x - hi


def normalise(x, gain):
    wide = x.astype(F32)
    return (wide * lax.rsqrt(jnp.mean(wide * wide, axis=-1, keepdims=True) + EPS) * gain).astype(BF16)


def iota(shape, axis):
    return lax.broadcasted_iota(jnp.int32, shape, axis)


def column(row):
    heads = row.shape[1]
    same = iota((heads, heads), 0) == iota((heads, heads), 1)
    return jnp.sum(jnp.where(same, row, 0.0), axis=1, keepdims=True)


def head_steps(normed, valids, w_dt_t, bias, rate):
    heads = w_dt_t.shape[0]
    rows = normed.shape[0] // len(valids)
    raw = dot_nt(w_dt_t, normed) + column(bias)
    steps = jnp.maximum(raw, 0.0) + jnp.log1p(jnp.exp(-jnp.abs(raw)))
    lane = iota((heads, rows), 1).astype(F32)
    steps = jnp.concatenate(
        [
            jnp.where(lane < valid, steps[:, c * rows : (c + 1) * rows], 0.0)
            for c, valid in enumerate(valids)
        ],
        axis=0,
    )
    falls = -steps * jnp.concatenate([column(rate) * LOG2E] * len(valids), axis=0)
    upper = jnp.where(iota((rows, rows), 0) <= iota((rows, rows), 1), 1.0, 0.0).astype(BF16)
    high, rest = split(falls)
    middle, low = split(rest)
    sums = dot(jnp.concatenate([high, middle, low], axis=0).astype(BF16), upper)
    count = falls.shape[0]
    running = sums[:count] + sums[count : 2 * count] + sums[2 * count :]
    to_end = jnp.exp2(running[:, rows - 1 : rows] - running) * steps
    return steps, to_end, running


def by_rows(to_end, running):
    parts = [*split(to_end), *split(jnp.exp2(running)), running]
    used = len(parts) * running.shape[0]
    stack = jnp.concatenate(parts + [jnp.zeros((128 - used, running.shape[1]), F32)], axis=0)
    return stack.T


def seen_from(steps, running):
    return running - jnp.where(steps > 0.0, jnp.log2(jnp.maximum(steps, 1e-37)), -1e30)


def inside_pair(turned, seen, scores, value, head, heads):
    rows = turned.shape[0]
    at = 4 * heads + head
    weights = [
        (jnp.exp2(jnp.minimum(turned[:, at + k : at + k + 1] - seen[head + k : head + k + 1], 120.0)) * scores).astype(BF16)
        for k in range(2)
    ]
    left = iota((rows, 128), 1) < 64
    zero = jnp.zeros_like(value)
    both = jnp.concatenate([jnp.where(left, value, zero), jnp.where(left, zero, value)], axis=0)
    return dot(jnp.concatenate(weights, axis=1), both)


def masked_scores(query, key):
    rows = query.shape[0]
    return jnp.where(iota((rows, rows), 0) >= iota((rows, rows), 1), dot_nt(query, key), 0.0)


def make_spread(spread, heads):
    inner = spread.shape[1] // 2
    head = lax.shift_right_logical(iota((128, inner), 1), (inner // heads).bit_length() - 1)
    row = iota((128, inner), 0)
    for g in range(2):
        hit = (row == head + 2 * heads * g) | (row == head + 2 * heads * g + heads)
        spread[:, g * inner : (g + 1) * inner] = jnp.where(hit, 1.0, 0.0).astype(BF16)


def make_skip(skip_g, spread, skip):
    layers, heads = skip_g.shape
    inner = skip.shape[1]
    for layer in range(layers):
        parts = [part for part in split(skip_g[layer : layer + 1, :])]
        row = jnp.concatenate(parts + [jnp.zeros((1, 128 - 2 * heads), F32)], axis=1)
        wide = jnp.broadcast_to(row, (16, 128)).astype(BF16)
        skip[8 * layer : 8 * layer + 8, :] = dot(wide, spread[:, :inner])[:8]


def pack_kernel(count, x, valid, shard, slot, *refs):
    sources, out, held, sems = refs[:count], refs[count], refs[count + 1 : -1], refs[-1]
    rows, width = x.shape[1:]
    copies = [pltpu.make_async_copy(x.at[0], out.at[pl.ds(0, rows)], sems.at[count])]
    copies += [pltpu.make_async_copy(a, b, sems.at[i]) for i, (a, b) in enumerate(zip(sources, held))]
    for copy in copies:
        copy.start()
    line, lane = iota((EXTRA, width), 0), iota((EXTRA, width), 1)
    live = valid[0, 0].astype(F32)
    place = (shard[0, 0, 0] + slot[0, 0, 0]).astype(F32)
    first = jnp.where(lane == 0, live, jnp.where(lane == 1, place, 0.0))
    out[rows:] = jnp.where(line == 0, first, 0.0).astype(BF16)
    for copy in copies:
        copy.wait()


def live_count(packed):
    at = packed.shape[0] - EXTRA
    return packed[at:, :128].astype(F32)[0:1, 0:1]


def place_of(packed):
    extra = packed[packed.shape[0] - EXTRA :, :128].astype(F32)
    hit = (iota((EXTRA, 128), 0) == 0) & (iota((EXTRA, 128), 1) == 1)
    return jnp.sum(jnp.where(hit, extra, 0.0)).astype(jnp.int32)


def block_of(packed):
    return packed[: packed.shape[0] - EXTRA]


def pieces_work(xs, valids, slots, params, work, ready=lambda: None):
    norm_g, w_xz, w_bc, w_dt, bias, rate, spread, skip = params
    gates, local, decay, grown, queries = work
    rows = xs[0].shape[0]
    heads, inner, key_width = w_dt.shape[1], w_xz.shape[1] // 2, w_bc.shape[2] // 2
    normed = normalise(jnp.concatenate(xs, axis=0), norm_g[0:1, :])
    bc = silu(dot(normed, w_bc[0])).astype(BF16)
    steps, to_end, running = head_steps(normed, valids, w_dt[0], bias[0:1, :], rate[0:1, :])
    seen = seen_from(steps, running)
    parts = []
    for i, slot in enumerate(slots):
        at, of = slice(i * rows, (i + 1) * rows), slice(i * heads, (i + 1) * heads)
        key, query = bc[at, :key_width], bc[at, key_width:]
        queries[slot] = query
        turned = by_rows(to_end[of], running[of])
        parts.append((slot, at, turned, turned.astype(BF16), seen[of], masked_scores(query, key), turn(key)))
    ready()
    for j in range(0, inner, 256):
        cols, ends = slice(j, j + 256), slice(inner + j, inner + j + 256)
        values = silu(dot(normed, w_xz[:, cols])).astype(BF16)
        gate = silu(dot(normed, w_xz[:, ends]))
        for slot, at, turned, lhs, seen_here, scores, key_t in parts:
            value = values[at]
            wide = value.astype(F32)
            gates[slot, :, cols] = gate[at]
            decay[slot, :, cols] = dot(lhs, spread[:, ends])
            grown[slot, :, cols] = dot(key_t, (wide * dot(lhs, spread[:, cols])).astype(BF16))
            base = skip[0:1, cols] * wide
            for k in range(2):
                half = slice(128 * k, 128 * k + 128)
                head = (j + 128 * k) * heads // inner
                local[slot, :, j + 128 * k : j + 128 * k + 128] = (
                    inside_pair(turned, seen_here, scores, value[:, half], head, heads) + base[:, half]
                )


def begin_kernel(packed, norm_g, w_dt, bias, rate, skip_g, w_bc_far, w_xz, w_bc, w_held, spread, skip, *refs):
    work, sems = refs[:-1], refs[-1]
    copies = [
        pltpu.make_async_copy(w_bc_far.at[0], w_bc.at[0], sems.at[0]),
        pltpu.make_async_copy(w_xz.at[0], w_held, sems.at[1]),
        pltpu.make_async_copy(w_bc_far.at[1], w_bc.at[1], sems.at[2]),
    ]
    for copy in copies:
        copy.start()
    make_spread(spread, w_dt.shape[1])
    make_skip(skip_g, spread, skip)
    params = (norm_g, w_held, w_bc, w_dt, bias, rate, spread, skip)
    copies[0].wait()
    pieces_work([block_of(packed)], [live_count(packed)], [0], params, work, copies[1].wait)
    copies[2].wait()


def piece_kernel(slot, layers, packed, late, *refs):
    held, sem = refs[-2:]
    copy = pltpu.make_async_copy(refs[13].at[layers], held, sem)
    copy.start()
    pieces_work([block_of(packed)], [live_count(packed)], [slot], refs[:8], refs[14:19])
    copy.wait()


def relay_kernel(x, *refs):
    refs[-1][...] = x[...]


def tile_kernel(n, *refs):
    pieces, refs = refs[:n], refs[n:]
    norm_g, w_held, w_bc, w_dt, bias, rate, spread, skip, gate_g, w_two, w_out = refs[:11]
    refs = refs[16:]
    work, refs = refs[:5], refs[5:]
    (
        send,
        own_x,
        own_live,
        normed_two,
        key_two,
        own_query,
        to_end_two,
        running_two,
        seen_two,
        x_one,
        x_two,
        valid_one,
        valid_two,
        state,
        dest,
    ) = refs
    gates, local, decay, grown, queries = work
    me = lax.axis_index("curve")
    rows, width = x_two.shape[1:]
    heads = w_dt.shape[1]
    inner = w_out.shape[1]
    key_width = w_bc.shape[2] // 2
    part = inner // n
    valid = [live_count(piece) for piece in pieces]
    xs = [block_of(piece) for piece in pieces]
    for k in range(n):
        x_one[k] = xs[k]
        dest[k] = place_of(pieces[k])
        valid_one[k] = jnp.broadcast_to(valid[k], (8, 128))
        valid_two[dest[k]] = jnp.broadcast_to(valid[k], (8, 128))
    params = (norm_g, w_held, w_bc, w_dt, bias, rate, spread, skip)
    pieces_work(xs[3:], valid[3:], list(range(3, n)), params, work)

    row = iota((rows, 128), 0).astype(F32)
    for c in range(n):
        k = me ^ c
        query = queries[k]
        squares = jnp.zeros((rows, 1), F32)
        update = None
        for j in range(0, inner, 256):
            at = slice(j, j + 256)
            out = local[k, :, at]
            if c:
                old = state[:, at]
                out += dot(query, old.astype(BF16)) * decay[k, :, at]
                if c < n - 1:
                    state[:, at] = old * decay[k, rows - 1 :, at] + grown[k, :, at]
            else:
                state[:, at] = grown[k, :, at]
            gated = out * gates[k, :, at]
            squares += jnp.sum(gated * gated, axis=-1, keepdims=True)
            of_part = dot((gated * gate_g[0:1, at]).astype(BF16), w_out[0, at, :])
            update = of_part if update is None else update + of_part
        scale = jnp.broadcast_to(lax.rsqrt(squares * (1.0 / inner) + EPS), (rows, 128))
        factor = jnp.where(row < valid_one[k][0:1], scale, 0.0)
        factor = jnp.concatenate([factor] * (width // 128), axis=1)
        new = (x_one[k].astype(F32) + update * factor).astype(BF16)
        x_two[dest[k]] = new
        normed_two[dest[k]] = normalise(new, norm_g[1:2, :])

    own_x[...] = x_two[me]
    own_live[...] = jnp.where(row < valid_two[me][0:1], 1.0, 0.0)
    normed = normed_two[...].reshape(n * rows, width)
    steps, to_end, running = head_steps(
        normed, [valid_two[c][0:1, 0:1] for c in range(n)], w_dt[1], bias[1:2, :], rate[1:2, :]
    )
    bc = silu(dot(normed, w_bc[1])).astype(BF16)
    at = pl.ds(pl.multiple_of(me * part, 128), part)
    value = silu(dot(normed, w_two[:, at])).astype(BF16).astype(F32)
    after = jnp.zeros((heads, 1), F32)
    suffixes = [None] * n
    for c in reversed(range(n)):
        suffixes[c] = after
        after = after + running[c * heads : (c + 1) * heads, rows - 1 :]
    whole = jnp.broadcast_to(after, (heads, rows))
    turned = [
        by_rows(to_end[c * heads : (c + 1) * heads] * jnp.exp2(suffixes[c]), whole).astype(BF16) for c in range(n)
    ]
    to_end_x = dot(jnp.concatenate(turned, axis=0), spread[:, at])
    fall = dot(turned[0][:16], spread[:, pl.ds(pl.multiple_of(inner + me * part, 128), part)])[0:1]
    send[:key_width] = dot(turn(bc[:, :key_width]), (value * to_end_x).astype(BF16)).astype(BF16)
    send[key_width:] = decay_rows(fall)
    seen = seen_from(steps, running)
    for c in range(n):
        chunk, of = slice(c * rows, (c + 1) * rows), slice(c * heads, (c + 1) * heads)
        key_two[c] = bc[chunk, :key_width]
        queries[c] = bc[chunk, key_width:]
        to_end_two[c] = to_end[of]
        running_two[c] = running[of]
        seen_two[c] = seen[of]
    own_query[...] = queries[me]


def own_kernel(
    normed_two, key_two, query, to_end_two, running_two, seen_two, spread, skip, w_xz, local, gate, decay
):
    me = lax.axis_index("curve")
    inner = local.shape[1]
    heads = seen_two.shape[1]
    normed = normed_two[me]
    turned = by_rows(to_end_two[me], running_two[me])
    lhs = turned.astype(BF16)
    seen = seen_two[me]
    scores = masked_scores(query[...], key_two[me])
    for j in range(0, inner, 256):
        at = slice(j, j + 256)
        value = silu(dot(normed, w_xz[:, at])).astype(BF16)
        gate[:, at] = silu(dot(normed, w_xz[:, inner + j : inner + j + 256]))
        decay[:, at] = dot(lhs, spread[:, inner + j : inner + j + 256])
        base = skip[8:9, at] * value.astype(F32)
        for k in range(2):
            half = slice(128 * k, 128 * k + 128)
            head = (j + 128 * k) * heads // inner
            local[:, j + 128 * k : j + 128 * k + 128] = (
                inside_pair(turned, seen, scores, value[:, half], head, heads) + base[:, half]
            )


def earlier_kernel(normed_two, key_two, to_end_two, running_two, spread, w_xz, state, fall):
    me = lax.axis_index("curve")
    inner = state.shape[1]
    rows = normed_two.shape[1]
    state[...] = jnp.zeros_like(state)
    fall[...] = jnp.ones_like(fall)

    def chunk(c, _):
        normed = normed_two[c]
        lhs = by_rows(to_end_two[c], running_two[c]).astype(BF16)
        key_t = turn(key_two[c])
        for j in range(0, inner, 256):
            at = slice(j, j + 256)
            value = silu(dot(normed, w_xz[:, at])).astype(BF16).astype(F32)
            weighted = value * dot(lhs, spread[:, at])
            end_x = dot(lhs[rows - 16 :], spread[:, inner + j : inner + j + 256])[15:16]
            state[:, at] = state[:, at] * end_x + dot(key_t, weighted.astype(BF16))
            fall[:, at] = fall[:, at] * end_x
        return 0

    lax.fori_loop(0, me, chunk, 0)


def decay_rows(fall):
    high, low = split(fall)
    lines = iota((EXTRA, fall.shape[1]), 0)
    return jnp.where(lines == 0, high, jnp.where(lines == 1, low, 0.0)).astype(BF16)


def state_and_decay(ordered, u):
    states = ordered.shape[1] - EXTRA
    tail = ordered[u, states:].astype(F32)
    return ordered[u, :states].astype(F32), tail[0:1] + tail[1:2]


def join_kernel(radix, stride, last, *refs):
    deeper = stride > 1
    parts, before = refs[:radix], refs[radix] if deeper else None
    outs, ordered = refs[radix + 1 + deeper : -1], refs[-1]
    me = lax.rem(lax.div(lax.axis_index("tile"), stride), radix)
    states, width = parts[0].shape[0] - EXTRA, parts[0].shape[1]
    for k in range(radix):
        ordered[me ^ k] = parts[k][...]
    earlier = (jnp.zeros((states, width), F32), jnp.ones((1, width), F32))
    whole = None
    for u in range(radix if not last else radix - 1):
        one, fall = state_and_decay(ordered, u)
        if u < radix - 1:
            took = jnp.where(me > u, 1.0, 0.0)
            keep = jnp.where(me > u, fall, 1.0)
            earlier = (earlier[0] * keep + one * took, earlier[1] * keep)
        if not last:
            whole = (one, fall) if u == 0 else (whole[0] * fall + one, whole[1] * fall)
    state, fall = earlier
    if deeper:
        state = state * before[states : states + 1] + before[:states]
        fall = fall * before[states : states + 1]
    if last:
        outs[0][...] = state.astype(BF16)
        return
    outs[0][:states] = state
    outs[0][states:] = jnp.broadcast_to(fall, (8, width))
    outs[1][:states] = whole[0].astype(BF16)
    outs[1][states:] = decay_rows(whole[1])


def end_kernel(ks, first, final, *refs):
    pieces, refs = refs[: len(ks)], refs[len(ks) :]
    local, gate, query, decay, earlier, fall, gate_g, w_out = refs[:8]
    me = lax.axis_index("curve")
    rows, inner = local.shape
    part = pieces[0].shape[1]
    squares = jnp.zeros((rows, 1), F32)
    update = None
    for k, piece in zip(ks, pieces):
        at = pl.ds(pl.multiple_of((me ^ k) * part, 128), part)
        state = piece[...].astype(F32) * fall[0:1, at] + earlier[:, at]
        head_out = dot(query[...], state.astype(BF16)) * decay[:, at] + local[:, at]
        gated = head_out * gate[:, at]
        squares += jnp.sum(gated * gated, axis=-1, keepdims=True)
        of_part = dot((gated * gate_g[1:2, at]).astype(BF16), w_out[1, at, :])
        update = of_part if update is None else update + of_part
    refs = refs[8:]
    squares = jnp.broadcast_to(squares, (rows, 128))
    if not first:
        update, squares, refs = update + refs[0][...], squares + refs[1][...], refs[2:]
    if not final:
        refs[0][...] = update
        refs[1][...] = squares
        return
    x, live, out = refs
    factor = live[...] * lax.rsqrt(squares * (1.0 / inner) + EPS)
    for j in range(0, x.shape[1], 128):
        at = slice(j, j + 128)
        out[0, :, at] = (x[:, at].astype(F32) + factor * update[:, at]).astype(BF16)


def call(kernel, outs, scratch, *args, in_hbm=(), free=(), aliases={}, out_fixed=True):
    vmem = pl.BlockSpec(memory_space=pltpu.VMEM)
    spaces = [pltpu.HBM if i in in_hbm else pltpu.VMEM for i in range(len(args))]
    spaces = [pltpu.SMEM if i in free else space for i, space in enumerate(spaces)]
    args = [
        arg if space == pltpu.SMEM else pltpu.with_memory_space_constraint(arg, space)
        for arg, space in zip(args, spaces)
    ]
    return pl.pallas_call(
        kernel,
        out_shape=[(pltpu.VMEM if out_fixed else jax.ShapeDtypeStruct)(shape, kind) for shape, kind in outs],
        in_specs=[pl.BlockSpec(memory_space=space) for space in spaces],
        out_specs=[vmem] * len(outs),
        scratch_shapes=scratch,
        input_output_aliases=aliases,
        compiler_params=pltpu.CompilerParams(vmem_limit_bytes=VMEM_BYTES),
    )(*args)


def swap(value, axis, mask, size):
    return lax.ppermute(value, axis, [(i, i ^ mask) for i in range(size)])


def levels(size):
    steps, stride = [], 1
    while stride < size:
        radix = 4 if size // stride >= 4 else 2
        steps.append((radix, stride))
        stride *= radix
    return steps


def local(
    tiles,
    points,
    valid_rows,
    dest_shard,
    dest_slot,
    norm_gain,
    w_xz,
    w_bc,
    w_dt,
    dt_bias,
    decay_rate,
    skip_gain,
    gate_gain,
    w_out,
):
    n = lax.axis_size("curve")
    rows, width = points.shape[1:]
    heads, inner, key_width = w_dt.shape[2], w_out.shape[1], w_bc.shape[2] // 2
    part = inner // n
    params = (norm_gain, jnp.swapaxes(w_dt, 1, 2), dt_bias, decay_rate, skip_gain, gate_gain)
    packed, norm_gain, w_dt, dt_bias, decay_rate, skip_gain, gate_gain = call(
        functools.partial(pack_kernel, len(params)),
        [((rows + EXTRA, width), BF16)] + [(p.shape, p.dtype) for p in params],
        [pltpu.SemaphoreType.DMA((len(params) + 1,))],
        points,
        valid_rows,
        dest_shard,
        dest_slot,
        *params,
        in_hbm=(0, *range(4, 4 + len(params))),
        free=(1, 2, 3),
    )
    pieces = [packed] + [None] * (n - 1)
    for k in range(2, n, 2):
        pieces[k] = swap(packed, "curve", k, n)
    pieces[1] = swap(packed, "curve", 1, n)
    work = [
        ((n, rows, inner), F32),
        ((n, rows, inner), F32),
        ((n, rows, inner), F32),
        ((n, key_width, inner), F32),
        ((n, rows, key_width), BF16),
    ]
    w_bc, w_held, spread, skip, *done = call(
        begin_kernel,
        [(w_bc.shape, BF16), (w_xz.shape[1:], BF16), ((128, 2 * inner), BF16), ((8 * skip_gain.shape[0], inner), F32)] + work,
        [pltpu.SemaphoreType.DMA((3,))],
        packed,
        norm_gain,
        w_dt,
        dt_bias,
        decay_rate,
        skip_gain,
        w_bc,
        w_xz,
        in_hbm=(6, 7),
    )
    shared = (norm_gain, w_held, w_bc, w_dt, dt_bias, decay_rate, spread, skip)
    aliases = {10 + i: i for i in range(5)}
    *done, w_out = call(
        functools.partial(piece_kernel, 1, pl.ds(0, w_out.shape[0])),
        work + [(w_out.shape, BF16)],
        [pltpu.SemaphoreType.DMA],
        pieces[1],
        packed,
        *shared,
        *done,
        w_out,
        in_hbm=(15,),
        aliases=aliases,
    )
    for k in range(3, n, 2):
        (passed,) = call(relay_kernel, [(packed.shape, BF16)], [], pieces[k - 1], done[4])
        pieces[k] = swap(passed, "curve", 1, n)
    *done, w_two = call(
        functools.partial(piece_kernel, 2, 1),
        work + [(w_xz.shape[1:], BF16)],
        [pltpu.SemaphoreType.DMA],
        pieces[2],
        passed,
        *shared,
        *done,
        w_xz,
        in_hbm=(15,),
        aliases=aliases,
    )
    first = n + 11
    got = call(
        functools.partial(tile_kernel, n),
        work
        + [
            ((key_width + EXTRA, part), BF16),
            ((rows, width), BF16),
            ((rows, 128), F32),
            ((n, rows, width), BF16),
            ((n, rows, key_width), BF16),
            ((rows, key_width), BF16),
            ((n, heads, rows), F32),
            ((n, heads, rows), F32),
            ((n, heads, rows), F32),
        ],
        [
            pltpu.VMEM((n, rows, width), BF16),
            pltpu.VMEM((n, rows, width), BF16),
            pltpu.VMEM((n, 8, 128), F32),
            pltpu.VMEM((n, 8, 128), F32),
            pltpu.VMEM((key_width, inner), F32),
            pltpu.SMEM((n,), jnp.int32),
        ],
        *pieces,
        *shared,
        gate_gain,
        w_two,
        w_out,
        *done,
        aliases={first + i: i for i in range(5)},
    )
    send, own_x, own_live, normed_two, key_two, own_query, to_end_two, running_two, seen_two = got[5:]
    own, gate, decay = call(
        own_kernel,
        [((rows, inner), F32)] * 3,
        [],
        normed_two,
        key_two,
        own_query,
        to_end_two,
        running_two,
        seen_two,
        spread,
        skip,
        w_two,
    )
    earlier, fall = call(
        earlier_kernel,
        [((key_width, inner), F32), ((8, inner), F32)],
        [],
        normed_two,
        key_two,
        to_end_two,
        running_two,
        spread,
        w_two,
    )
    before = []
    steps = levels(tiles)
    for i, (radix, stride) in enumerate(steps):
        last = i == len(steps) - 1
        parts = [send] + [swap(send, "tile", k * stride, tiles) for k in range(1, radix)]
        outs = [((key_width, part), BF16)]
        if not last:
            outs = [((key_width + 8, part), F32), ((key_width + EXTRA, part), BF16)]
        got = call(
            functools.partial(join_kernel, radix, stride, last),
            outs,
            [pltpu.VMEM((radix, key_width + EXTRA, part), BF16)],
            *parts,
            *before,
            fall if last else decay,
        )
        if not last:
            before, send = [got[0]], got[1]
    incoming = got[0]
    states = [incoming] + [swap(incoming, "curve", k, n) for k in range(1, n)]
    common = (own, gate, own_query, decay, earlier, fall, gate_gain, w_out)
    partial = []
    for ks in ([0], list(range(3, n))):
        partial = call(
            functools.partial(end_kernel, ks, not partial, False),
            [((rows, width), F32), ((rows, 128), F32)],
            [],
            *[states[k] for k in ks],
            *common,
            *partial,
        )
    (out,) = call(
        functools.partial(end_kernel, [2, 1], False, True),
        [((1, rows, width), BF16)],
        [],
        states[2],
        states[1],
        *common,
        *partial,
        own_x,
        own_live,
        out_fixed=False,
    )
    return out


def solution(mesh):
    in_specs = (
        P("tile", "curve", None),
        P("tile", "curve"),
        P("tile", "curve", None),
        P("tile", "curve", None),
    ) + (P(),) * 9
    return jax.shard_map(
        functools.partial(local, mesh.shape["tile"]),
        mesh=mesh,
        in_specs=in_specs,
        out_specs=P("tile", "curve", None),
        check_vma=False,
    )
```
